32 devices in a mesh: dp: 8 (over y, x, core), freq: 4 (over z).
Axes of the slice: x: 2, y: 2, z: 4, core: 2. Of those that a mesh axis runs over, the one named last changes fastest.
Arguments:
- inputs: float32 [512, 16, 768], P('freq', 'dp'), may hold values from -6 to 6
- cotangent: float32 [512, 16, 768], P('freq', 'dp'), may hold values from -6 to 6
- group: int32 [16], P('dp'), may hold values from 0 to 1, as said below
- lens: int32 [16, 4], P('dp'), may hold values from 64 to 128, as said below
- norm1_gain: float32 [768], replicated, may hold values from 0.25 to 1.75
- w_in: bfloat16 [768, 2304], P('freq'), may hold values from -0.21875 to 0.21875
- kernel_long: bfloat16 [512, 768], P('freq'), may hold values from -4 to 4
- kernel_short: bfloat16 [128, 768], P('freq'), may hold values from -4 to 4
- conv_weight: float32 [3, 768], replicated, may hold values from -2.5 to 2.5
- cond_gain: float32 [768], replicated, may hold values from 0.5 to 2
- w_out: bfloat16 [768, 768], P('freq'), may hold values from -0.21875 to 0.21875
- norm2_gain: float32 [768], replicated, may hold values from 0.25 to 1.75
- w_gate_up: bfloat16 [768, 6144], P('freq'), may hold values from -0.21875 to 0.21875
- w_down: bfloat16 [3072, 768], P('freq'), may hold values from -0.109375 to 0.109375
Outputs:
- layer_out: float32 [512, 16, 768], P('freq', 'dp')
- grad_inputs: float32 [512, 16, 768], P('freq', 'dp')
- grad_norm1_gain: float32 [768], replicated
- grad_w_in: float32 [768, 2304], P('freq')
- grad_kernel_long: float32 [512, 768], replicated
- grad_kernel_short: float32 [128, 768], replicated
- grad_conv_weight: float32 [3, 768], replicated
- grad_cond_gain: float32 [768], replicated
- grad_w_out: float32 [768, 768], P('freq')
- grad_norm2_gain: float32 [768], replicated
- grad_w_gate_up: float32 [768, 6144], P('freq')
- grad_w_down: float32 [3072, 768], P('freq')
The draws below stay inside these ranges and needn't reach their ends.
Inputs may be any that keep to these rules, and one draw needn't show every extreme that they name: Some slot has group 0 and some slot has group 1. `lens`: a group 0 slot holds one sequence whose length is the sum of its four counts; a group 1 slot holds four sequences with these lengths; some group 0 slot has all four counts equal to 128.
All inputs are finite; a program needn't handle non-finite values.
Results may differ from the reference program's by a relative error of at most 0.024.
Values may be sent and summed in bfloat16 or wider, within the bound.
No kernel may reach another device: no remote copies, remote signals or barrier semaphores. Data moves between devices by JAX's collectives and lax.ppermute only.
A program may use at most 192 MiB of HBM per device.

```python
import math
import jax
import jax.numpy as jnp
from jax import lax

MODEL_WIDTH = 768
FF = 3072
SLOT_LENGTH = 512
SHORT_LENGTH = 128
SLOT_COUNT = 16


def chosen_slots(key):
    complete_slot = jax.random.randint(key, (), 0, SLOT_COUNT)
    start_offset = jax.random.randint(jax.random.fold_in(key, 7), (), 1, SLOT_COUNT)
    packed_slot = (complete_slot + start_offset) % SLOT_COUNT
    return (complete_slot, packed_slot)


def draw_group(key, part):
    complete_slot, packed_slot = chosen_slots(key)
    key = jax.random.fold_in(key, 11)
    group = jax.random.randint(key, (SLOT_COUNT,), 0, 2)
    slot_places = jnp.arange(SLOT_COUNT)
    group = jnp.where(slot_places == complete_slot, 0, group)
    group = jnp.where(slot_places == packed_slot, 1, group)
    return group.astype(jnp.int32)


def draw_lens(key, part):
    complete_slot, packed_slot = chosen_slots(key)
    key = jax.random.fold_in(key, 12)
    slot_counts = jax.random.randint(key, (SLOT_COUNT, SLOT_LENGTH // SHORT_LENGTH), SHORT_LENGTH // 2, SHORT_LENGTH + 1)
    slot_counts = jnp.where(jnp.arange(SLOT_COUNT)[:, None] == complete_slot, SHORT_LENGTH, slot_counts)
    return slot_counts.astype(jnp.int32)


def levels(own_key, dims, split, low, top_value):
    level = 1.0
    for position, blocks in split:
        heights = jax.random.uniform(jax.random.fold_in(jax.random.fold_in(own_key, 6), position), (blocks,), jnp.float32, low / len(split), top_value / len(split))
        level = level * jnp.repeat(jnp.exp(heights), dims[position] // blocks).reshape((-1,) + (1,) * (len(dims) - 1 - position))
    return level


def bell_draw(own_key, shape, scale, most, pieces=(), held_as=jnp.bfloat16):
    loudness = levels(own_key, shape, pieces, -0.22, 0.18) if pieces else 1.0
    entries = jax.random.normal(own_key, shape, jnp.float32) * scale * loudness
    return jnp.minimum(jnp.maximum(entries, -most), most).astype(held_as)


def setup_inputs(seed: int = 0) -> dict:
    keys = jax.random.split(jax.random.key(seed), 15)
    inputs = bell_draw(keys[0], (SLOT_LENGTH, SLOT_COUNT, MODEL_WIDTH), 1.0, 6.0, ((0, 4), (1, 8)), jnp.float32)
    cotangent = bell_draw(keys[1], (SLOT_LENGTH, SLOT_COUNT, MODEL_WIDTH), 1.0, 6.0, ((0, 4), (1, 8)), jnp.float32)
    group = draw_group(jax.random.fold_in(keys[14], 71), 0)
    lens = draw_lens(jax.random.fold_in(keys[14], 71), 0)
    norm1_gain = jnp.clip(1.0 + 0.15 * jax.random.normal(keys[4], (MODEL_WIDTH,), jnp.float32), 0.25, 1.75)
    w_in = bell_draw(keys[5], (MODEL_WIDTH, 3 * MODEL_WIDTH), MODEL_WIDTH ** -0.5, 0.21875, ((0, 4),))
    kernel_long = bell_draw(keys[6], (SLOT_LENGTH, MODEL_WIDTH), 1.0, 4.0, ((0, 4),))
    kernel_short = bell_draw(keys[7], (SHORT_LENGTH, MODEL_WIDTH), 1.0, 4.0, ((0, 4),))
    conv_weight = bell_draw(keys[8], (3, MODEL_WIDTH), 0.6, 2.5, (), jnp.float32)
    cond_gain = jnp.clip(jnp.exp(jax.random.uniform(keys[9], (MODEL_WIDTH,), jnp.float32, math.log(0.5), math.log(2.0))), 0.5, 2.0)
    w_out = bell_draw(keys[10], (MODEL_WIDTH, MODEL_WIDTH), MODEL_WIDTH ** -0.5, 0.21875, ((0, 4),))
    norm2_gain = jnp.clip(1.0 + 0.15 * jax.random.normal(keys[11], (MODEL_WIDTH,), jnp.float32), 0.25, 1.75)
    w_gate_up = bell_draw(keys[12], (MODEL_WIDTH, 2 * FF), MODEL_WIDTH ** -0.5, 0.21875, ((0, 4),))
    w_down = bell_draw(keys[13], (FF, MODEL_WIDTH), FF ** -0.5, 0.109375, ((0, 4),))
    return dict(inputs=inputs, cotangent=cotangent, group=group, lens=lens, norm1_gain=norm1_gain, w_in=w_in, kernel_long=kernel_long, kernel_short=kernel_short, conv_weight=conv_weight, cond_gain=cond_gain, w_out=w_out, norm2_gain=norm2_gain, w_gate_up=w_gate_up, w_down=w_down)


@jax.custom_vjp
def low(v):
    return lax.optimization_barrier(v.astype(jnp.bfloat16)).astype(jnp.float32)

@jax.custom_vjp
def low_back(v):
    return v

def low_keep(v):
    return (low(v), None)

def low_pass(kept, grad):
    return (grad,)

def back_keep(v):
    return (v, None)

def back_low(kept, grad):
    return (low(grad),)
low.defvjp(low_keep, low_pass)
low_back.defvjp(back_keep, back_low)
EPSILON = 1e-05
HIGHEST = lax.Precision.HIGHEST

def layer_norm(values, gain):
    center = values - lax.optimization_barrier(jnp.mean(values, axis=-1, keepdims=True))
    spread = lax.optimization_barrier(jnp.mean(center * center, axis=-1, keepdims=True))
    return center * lax.rsqrt(spread + EPSILON) * gain

def cosine_table(length):
    freq = lax.broadcasted_iota(jnp.int32, (length, length), 0)
    posit = lax.broadcasted_iota(jnp.int32, (length, length), 1)
    phase = (2 * posit + 1) * freq % (4 * length)
    angle = phase.astype(jnp.float32) * (jnp.pi / (2 * length))
    weight = jnp.where(freq == 0, 1.0, 2.0) / length
    table = jnp.cos(angle) * jnp.sqrt(weight)
    return lax.optimization_barrier(table.astype(jnp.bfloat16)).astype(jnp.float32)

def slot_mask(group, lens, length):
    posit = jnp.arange(length, dtype=jnp.int32)
    total_len = lax.optimization_barrier(jnp.sum(lens, axis=1))
    long_mask = posit[:, None] < total_len[None, :]
    quarter_len = jnp.take(lens.T, posit // SHORT_LENGTH, axis=0)
    pack_mask = (posit % SHORT_LENGTH)[:, None] < quarter_len
    return jnp.where(group[None, :] == 1, pack_mask, long_mask).astype(jnp.float32)

def depthwise(values, conv_weight):
    border = jnp.zeros_like(values[:1])
    before = jnp.concatenate([border, values[:-1]], axis=0)
    after = jnp.concatenate([values[1:], border], axis=0)
    return conv_weight[0] * before + conv_weight[1] * values + conv_weight[2] * after

def conditioned(spectrum, cond_spec, base, cond_gain):
    return (base + cond_gain * (jnp.sqrt(cond_spec * cond_spec + 1.0) - 1.0)) * spectrum

def spectral(values, group, tab_long, tab_short, kernel_long, kernel_short, conv_weight, cond_gain):
    length, count, width = values.shape
    spec_long = low_back(jnp.einsum('ft,tbd->fbd', tab_long, values, precision=HIGHEST))
    cond_long = low_back(jnp.einsum('ft,tbd->fbd', tab_long, depthwise(values, conv_weight), precision=HIGHEST))
    filtered_long = low(conditioned(spec_long, cond_long, kernel_long[:, None, :], cond_gain))
    conv_long = jnp.einsum('ft,fbd->tbd', tab_long, filtered_long, precision=HIGHEST)
    blocks = values.reshape(length // SHORT_LENGTH, SHORT_LENGTH, count, width)
    cond_blocks = jax.vmap(depthwise, in_axes=(0, None))(blocks, conv_weight)
    spec_short = low_back(jnp.einsum('ft,qtbd->qfbd', tab_short, blocks, precision=HIGHEST))
    cond_short = low_back(jnp.einsum('ft,qtbd->qfbd', tab_short, cond_blocks, precision=HIGHEST))
    filtered_short = low(conditioned(spec_short, cond_short, kernel_short[None, :, None, :], cond_gain))
    conv_short = jnp.einsum('ft,qfbd->qtbd', tab_short, filtered_short, precision=HIGHEST)
    conv_short = conv_short.reshape(length, count, width)
    return jnp.where(group[None, :, None] == 1, conv_short, conv_long)

def forward(inputs, mask, group, tab_long, tab_short, norm1_gain, w_in, kernel_long, kernel_short, conv_weight, cond_gain, w_out, norm2_gain, w_gate_up, w_down):
    width = inputs.shape[-1]
    normed = low(layer_norm(inputs, norm1_gain))
    project = low_back(jnp.einsum('tbd,de->tbe', normed, w_in, precision=HIGHEST))
    outer = project[..., :width]
    left_part = project[..., width:2 * width]
    right_part = project[..., 2 * width:]
    values = low(left_part * right_part * mask[..., None])
    conv = low_back(spectral(values, group, tab_long, tab_short, kernel_long, kernel_short, conv_weight, cond_gain))
    mixed = low(outer * conv)
    residual = inputs + low_back(jnp.einsum('tbd,de->tbe', mixed, w_out, precision=HIGHEST))
    normed_two = low(layer_norm(residual, norm2_gain))
    gate_up = low_back(jnp.einsum('tbd,de->tbe', normed_two, w_gate_up, precision=HIGHEST))
    hidden = gate_up.shape[-1] // 2
    active = low(jax.nn.gelu(gate_up[..., :hidden]) * gate_up[..., hidden:])
    return residual + low_back(jnp.einsum('tbf,fd->tbd', active, w_down, precision=HIGHEST))

def reference(inputs, cotangent, group, lens, norm1_gain, w_in, kernel_long, kernel_short, conv_weight, cond_gain, w_out, norm2_gain, w_gate_up, w_down):
    length, slots, width = inputs.shape
    tab_long = cosine_table(length)
    tab_short = cosine_table(SHORT_LENGTH)
    weights = tuple((item.astype(jnp.float32) for item in (norm1_gain, w_in, kernel_long, kernel_short, conv_weight, cond_gain, w_out, norm2_gain, w_gate_up, w_down)))
    mask = slot_mask(group, lens, length)
    blocks = slots // 8

    def regroup(array):
        return jnp.moveaxis(array.reshape((length, blocks, 8) + array.shape[2:]), 1, 0)

    def advance(totals, item):
        block_in, block_cot, block_mask, block_group = item

        def apply(values, *params):
            return forward(values, block_mask, block_group, tab_long, tab_short, *params)
        result, pull = jax.vjp(apply, block_in, *weights)
        grads = pull(block_cot)
        totals = tuple((first + second for first, second in zip(totals, grads[1:])))
        return (totals, (result, grads[0]))
    zeros = tuple((jnp.zeros_like(item) for item in weights))
    totals, (results, grad_blocks) = lax.scan(advance, zeros, (regroup(inputs), regroup(cotangent), regroup(mask), group.reshape(blocks, 8)))

    def restore(array):
        return jnp.moveaxis(array, 0, 1).reshape(length, slots, width)
    return (restore(results), restore(grad_blocks), totals[0], totals[1], totals[2], totals[3], totals[4], totals[5], totals[6], totals[7], totals[8], totals[9])
```

```python
import math

import jax
import jax.numpy as jnp
import numpy as np
from jax import lax
from jax.sharding import PartitionSpec as P

SHORT_LENGTH = 128
EPSILON = 1e-05
BF = jnp.bfloat16
F32 = jnp.float32
GROUP = 8


def cosine_table(length):
    freq = np.arange(length)[:, None]
    posit = np.arange(length)[None, :]
    phase = (2 * posit + 1) * freq % (4 * length)
    weight = np.where(freq == 0, 1.0, 2.0) / length
    return (np.cos(phase * (math.pi / (2 * length))) * np.sqrt(weight)).astype(np.float32)


def dot(a, b):
    return lax.dot_general(a, b, (((1,), (0,)), ((), ())), preferred_element_type=F32)


def dot_nt(a, b):
    return lax.dot_general(a, b, (((1,), (1,)), ((), ())), preferred_element_type=F32)


def dot_tn(a, b):
    return lax.dot_general(a, b, (((0,), (0,)), ((), ())), preferred_element_type=F32)


def norm_parts(values):
    center = values - jnp.mean(values, axis=-1, keepdims=True)
    spread = jnp.mean(center * center, axis=-1, keepdims=True)
    inv = lax.rsqrt(spread + EPSILON)
    return center * inv, inv


def norm_pull(hat, inv, gain, grad):
    scaled = grad * gain
    mean_one = jnp.mean(scaled, axis=-1, keepdims=True)
    mean_two = jnp.mean(scaled * hat, axis=-1, keepdims=True)
    return inv * (scaled - mean_one - hat * mean_two), jnp.sum(grad * hat, axis=0)


def gated_unit(gate, upward):
    return jax.nn.gelu(gate) * upward


def pick(stacked, index):
    return lax.dynamic_index_in_dim(stacked, index, axis=0, keepdims=False)


def body(
    inputs,
    cotangent,
    group,
    lens,
    norm1_gain,
    w_in,
    kernel_long,
    kernel_short,
    conv_weight,
    cond_gain,
    w_out,
    norm2_gain,
    w_gate_up,
    w_down,
):
    nz = lax.axis_size("freq")
    ndp = lax.axis_size("dp")
    z = lax.axis_index("freq")
    d = lax.axis_index("dp")
    core = d % 2
    chip = (d // 2) % 4
    member = d % GROUP
    owned, slots, width = inputs.shape
    half = width // 2
    length = owned * nz
    tokens = owned * slots
    others = ndp // GROUP
    across = [[i + GROUP * g for g in range(others)] for i in range(GROUP)]
    blocks = [[g * GROUP + i for i in range(GROUP)] for g in range(others)]

    def core_swap(x):
        return lax.ppermute(x, "dp", [(i, i ^ 1) for i in range(ndp)])

    def chip_swap(x, m):
        return lax.ppermute(x, "dp", [(i, i ^ (2 * m)) for i in range(ndp)])

    def z_rot(x, k):
        return lax.ppermute(x, "freq", [(i, (i + k) % nz) for i in range(nz)])

    def mine(x, axis=-1):
        low, high = jnp.split(x, 2, axis=axis)
        return jnp.where(core == 0, low, high)

    def theirs(x, axis=-1):
        low, high = jnp.split(x, 2, axis=axis)
        return jnp.where(core == 0, high, low)

    def joined(own, other, axis=-1):
        return jnp.where(
            core == 0,
            jnp.concatenate([own, other], axis=axis),
            jnp.concatenate([other, own], axis=axis),
        )

    def from_z(rel):
        stacked = jnp.stack(rel)
        return jnp.stack([pick(stacked, (z - i) % nz) for i in range(nz)])

    def from_chips(rel):
        stacked = jnp.stack(rel)
        return jnp.stack([pick(stacked, chip ^ i) for i in range(4)])

    def z_swap(x):
        rel = [pick(x, z)] + [z_rot(pick(x, (z + k) % nz), k) for k in range(1, nz)]
        return from_z(rel)

    def over_groups(x):
        if others > 1:
            return lax.psum(x, "dp", axis_index_groups=across)
        return x

    x_own = jnp.swapaxes(inputs, 0, 1).reshape(tokens, width)
    cot_own = jnp.swapaxes(cotangent, 0, 1).reshape(tokens, width)

    local_in = jnp.concatenate(
        [mine(w_in.reshape(-1, 3, width)).reshape(-1, 3 * half), mine(w_out)], axis=1
    )
    rows = local_in.shape[0]
    quarter = rows // 4
    local_four = local_in.reshape(4, quarter, -1)
    near = pick(local_four, chip)
    by_z = [z_rot(near, k) for k in range(1, nz)]
    by_z_all = jnp.stack(by_z)
    by_chip = [chip_swap(by_z_all, m) for m in (1, 2, 3)]
    rel = [local_four]
    for k in range(nz - 1):
        rel.append(from_chips([by_z[k]] + [piece[k] for piece in by_chip]))
    both = from_z(rel).reshape(width, 4 * half)
    w_in_half = both[:, : 3 * half]
    out_cols = both[:, 3 * half :]
    w_out_rows = joined(mine(out_cols, 0), core_swap(theirs(out_cols, 0)))

    kernels = lax.all_gather(
        jnp.concatenate([mine(kernel_long), mine(kernel_short)], axis=0), "freq", axis=0
    )
    long_base = kernels[:, :owned].reshape(length, half)
    short_base = kernels[:, owned:].reshape(-1, half)

    hidden = w_down.shape[0] * nz
    per_z = w_down.shape[0]
    chunk = per_z // 6
    chunk_of = lambda zz, mm: jnp.where(mm < 2 * zz, mm, mm - 2)
    gu_local = w_gate_up
    pieces = []
    for side in range(2):
        for i in range(3):
            zz = i + (i >= chip).astype(jnp.int32)
            start = side * hidden + zz * per_z + chunk_of(zz, member) * chunk
            pieces.append(lax.dynamic_slice_in_dim(gu_local, start, chunk, axis=1))
    down_piece = lax.dynamic_slice_in_dim(
        w_down, jnp.clip(chunk_of(z, member), 0, 5) * chunk, chunk, axis=0
    )
    mlp_piece = jnp.concatenate([jnp.concatenate(pieces, axis=1), down_piece], axis=0)
    mlp_all = lax.all_gather(mlp_piece, "freq", axis=0)
    w_gu = mlp_all[:, :rows].reshape(width, width)
    down_four = mlp_all[:, rows:]
    w_dn = jnp.concatenate(
        [pick(down_four, i + (i >= chip).astype(jnp.int32)) for i in range(3)], axis=0
    )

    cot_low = cot_own.astype(BF)
    cot_near = jnp.stack([cot_low] + [chip_swap(cot_low, m) for m in (1, 2, 3)])
    cot_far = core_swap(cot_near)
    cot_all = jnp.concatenate([cot_near, cot_far], axis=1)

    marks = jnp.concatenate([group[:, None], lens], axis=1)
    marks = jnp.concatenate([marks, core_swap(marks)], axis=0)
    group_all = marks[:, 0]
    lens_all = marks[:, 1:]
    posit = z * owned + jnp.arange(owned, dtype=jnp.int32)
    hit = (posit // SHORT_LENGTH)[None, :, None] == jnp.arange(lens.shape[1], dtype=jnp.int32)
    quarter_len = jnp.sum(jnp.where(hit, lens_all[:, None, :], 0), axis=2)
    mask = jnp.where(
        group_all[:, None] == 1,
        (posit % SHORT_LENGTH)[None, :] < quarter_len,
        posit[None, :] < jnp.sum(lens_all, axis=1)[:, None],
    )
    mask = mask.astype(F32).reshape(2 * tokens, 1)

    hat_one, inv_one = norm_parts(x_own)
    normed = (hat_one * norm1_gain).astype(BF)
    normed_all = jnp.concatenate([normed, core_swap(normed)], axis=0)
    project = dot(normed_all, w_in_half)
    outer = project[:, :half]
    left_part = project[:, half : 2 * half]
    right_part = project[:, 2 * half :]
    values = (left_part * right_part * mask).astype(BF)
    vals = z_swap(values.reshape(2 * slots, owned, half)).reshape(length, half)

    slot_group = pick(group_all, z)
    table_long = jnp.asarray(cosine_table(length), BF)
    table_short = jnp.asarray(
        np.kron(np.eye(length // SHORT_LENGTH), cosine_table(SHORT_LENGTH)), BF
    )
    table = jnp.where(slot_group == 1, table_short, table_long)
    base = jnp.where(
        slot_group == 1, jnp.tile(short_base, (length // SHORT_LENGTH, 1)), long_base
    ).astype(F32)
    gain_half = mine(cond_gain)
    taps = mine(conv_weight)
    place = jnp.arange(length, dtype=jnp.int32)[:, None]
    starts = (place == 0) | ((slot_group == 1) & (place % SHORT_LENGTH == 0))
    ends = (place == length - 1) | (
        (slot_group == 1) & (place % SHORT_LENGTH == SHORT_LENGTH - 1)
    )
    border = jnp.zeros((1, half), F32)

    def earlier(x):
        return jnp.where(starts, 0.0, jnp.concatenate([border, x[:-1]], axis=0))

    def later(x):
        return jnp.where(ends, 0.0, jnp.concatenate([x[1:], border], axis=0))

    vals_wide = vals.astype(F32)
    before = earlier(vals_wide)
    after = later(vals_wide)
    cond = taps[0] * before + taps[1] * vals_wide + taps[2] * after
    cond_high = cond.astype(BF)
    cond_low = (cond - cond_high.astype(F32)).astype(BF)
    folded = dot(table, jnp.concatenate([vals, cond_high, cond_low], axis=1))
    spectrum = folded[:, :half]
    cond_spec = folded[:, half : 2 * half] + folded[:, 2 * half :]
    root = jnp.sqrt(cond_spec * cond_spec + 1.0)
    kern = base + gain_half * (root - 1.0)
    filtered = (kern * spectrum).astype(BF)
    conv_far = dot_tn(table, filtered).astype(BF)
    conv = z_swap(conv_far.reshape(nz, owned, half)).reshape(2 * tokens, half).astype(F32)

    mixed = (outer * conv).astype(BF)
    out_part = dot(mixed, w_out_rows)
    residual = (
        x_own + out_part[:tokens] + core_swap(out_part[tokens:].astype(BF)).astype(F32)
    )
    hat_two, inv_two = norm_parts(residual)
    normed_two = (hat_two * norm2_gain).astype(BF)

    arrived = [normed_two] + [chip_swap(normed_two, m) for m in (1, 2, 3)]
    seconds, acts, grads_gu, outs = [], [], [], []
    sums = []
    for m in range(4):
        second = jnp.concatenate([arrived[m], core_swap(arrived[m])], axis=0)
        gate_up = dot(second, w_gu)
        gate = gate_up[:, :half]
        upward = gate_up[:, half:]
        grad_active = dot_nt(cot_all[m], w_dn)
        active, pull = jax.vjp(gated_unit, gate, upward)
        grad_gate, grad_upward = pull(grad_active)
        grad_gu = jnp.concatenate([grad_gate, grad_upward], axis=1).astype(BF)
        part = dot_nt(grad_gu, w_gu)
        part = part[:tokens] + core_swap(part[tokens:].astype(BF)).astype(F32)
        sums.append(part)
        seconds.append(second)
        acts.append(active.astype(BF))
        grads_gu.append(grad_gu)
        outs.append(dot(acts[m], w_dn))
    grad_second = sums[0]
    for m in (1, 2, 3):
        grad_second = grad_second + chip_swap(sums[m].astype(BF), m).astype(F32)
    far = core_swap(jnp.stack([out[tokens:].astype(BF) for out in outs]))
    layer_out = residual + outs[0][:tokens] + far[0].astype(F32)
    for m in (1, 2, 3):
        part = (outs[m][:tokens] + far[m].astype(F32)).astype(BF)
        layer_out = layer_out + chip_swap(part, m).astype(F32)

    act_all = jnp.concatenate(acts, axis=0)
    grad_down = dot_tn(act_all, cot_all.reshape(-1, width)).astype(BF)
    grad_gu_w = dot_tn(
        jnp.concatenate(seconds, axis=0), jnp.concatenate(grads_gu, axis=0)
    ).astype(BF)
    down_three = grad_down.reshape(3, chunk, width)
    blocks_down = []
    for zz in range(4):
        at = jnp.clip(zz - (zz > chip).astype(jnp.int32), 0, 2)
        blocks_down.append(jnp.where(chip == zz, 0.0, pick(down_three, at)).astype(BF))
    mlp_grads = jnp.concatenate(
        [grad_gu_w.reshape(nz, rows, width), jnp.stack(blocks_down)], axis=1
    )
    mlp_share = lax.psum_scatter(mlp_grads, "freq", scatter_dimension=0, tiled=False)
    mlp_share = over_groups(mlp_share)
    mlp_sum = lax.all_gather(mlp_share, "dp", axis=0, axis_index_groups=blocks)
    cols = []
    for side in range(2):
        for zz in range(4):
            for c in range(6):
                mm = c if c < 2 * zz else c + 2
                i = zz - (zz > mm // 2)
                at = (side * 3 + i) * chunk
                cols.append(mlp_sum[mm, :rows, at : at + chunk])
    grad_w_gate_up = jnp.concatenate(cols, axis=1).astype(F32)
    grad_w_down = jnp.concatenate(
        [pick(mlp_sum, c + 2 * (c >= 2 * z).astype(jnp.int32))[rows:] for c in range(6)], axis=0
    ).astype(F32)

    pulled, gain_two = norm_pull(hat_two, inv_two, norm2_gain, grad_second)
    grad_residual = cot_own + pulled
    grad_mix = grad_residual.astype(BF)
    grad_mix_all = jnp.concatenate([grad_mix, core_swap(grad_mix)], axis=0)
    grad_mixed = dot_nt(grad_mix_all, w_out_rows)
    grad_outer = (grad_mixed * conv).astype(BF)
    grad_conv = (grad_mixed * outer).astype(BF)
    grad_conv_slot = z_swap(grad_conv.reshape(2 * slots, owned, half)).reshape(length, half)

    def shares(matrix, ride):
        four = matrix.astype(BF).reshape(nz, 4, quarter, -1)
        by_quarter = jnp.swapaxes(four, 0, 1)
        total = pick(by_quarter, chip).astype(F32)
        for m in (1, 2, 3):
            total = total + chip_swap(pick(by_quarter, chip ^ m), m).astype(F32)
        total = total.astype(BF)
        extra = jnp.zeros((16, total.shape[-1]), BF).at[0].set(ride.astype(BF))
        send = lambda i: jnp.concatenate([pick(total, i), extra], axis=0)
        piece = send(z).astype(F32)
        for k in range(1, nz):
            piece = piece + z_rot(send((z + k) % nz), k).astype(F32)
        piece = over_groups(piece.astype(BF))
        rel = [piece] + [chip_swap(piece, m) for m in (1, 2, 3)]
        whole = from_chips(rel)
        riding = jnp.sum(whole[:, quarter].astype(F32), axis=0)
        own = jnp.concatenate(
            [whole[:, :quarter].reshape(rows, -1), extra.at[0].set(riding.astype(BF))], axis=0
        )
        other = core_swap(own)
        return own[:rows], other[:rows], riding + other[rows].astype(F32)

    mixed_other = core_swap(mixed)
    mixed_other = jnp.concatenate([mixed_other[tokens:], mixed_other[:tokens]], axis=0)
    mixed_full = joined(mixed, mixed_other)
    grad_out_cols = dot_tn(mixed_full, mine(grad_mix_all))
    grad_in_outer = dot_tn(normed_all, grad_outer)
    early_own, early_other, grad_norm2_gain = shares(
        jnp.concatenate([grad_in_outer, grad_out_cols], axis=1), gain_two
    )

    grad_filtered = dot(table, grad_conv_slot)
    grad_spec = (grad_filtered * kern).astype(BF)
    grad_base = grad_filtered * spectrum
    grad_cond_spec = (grad_base * gain_half * cond_spec / root).astype(BF)
    unfolded = dot_tn(table, jnp.concatenate([grad_spec, grad_cond_spec], axis=1))
    grad_cond = unfolded[:, half:]
    grad_values = (
        unfolded[:, :half]
        + taps[0] * later(grad_cond)
        + taps[1] * grad_cond
        + taps[2] * earlier(grad_cond)
    ).astype(BF)
    grad_vals = z_swap(grad_values.reshape(nz, owned, half)).reshape(2 * tokens, half)
    grad_vals = grad_vals.astype(F32) * mask

    is_short = (slot_group == 1).astype(F32)
    small = jnp.stack(
        [
            jnp.sum(grad_base * (root - 1.0), axis=0),
            jnp.sum(grad_cond * before, axis=0),
            jnp.sum(grad_cond * vals_wide, axis=0),
            jnp.sum(grad_cond * after, axis=0),
        ]
    )
    fill = -(length + SHORT_LENGTH + 4) % (nz * 16)
    filters = jnp.concatenate(
        [
            grad_base * (1.0 - is_short),
            jnp.sum(grad_base.reshape(-1, SHORT_LENGTH, half), axis=0) * is_short,
            small,
            jnp.zeros((fill, half), F32),
        ],
        axis=0,
    ).astype(BF)
    filters = filters.reshape(nz, -1, half)
    piece = pick(filters, z).astype(F32)
    for k in range(1, nz):
        piece = piece + z_rot(pick(filters, (z + k) % nz), k).astype(F32)
    low = piece.astype(BF)
    total = low.astype(F32)
    for m in (1, 2, 3):
        total = total + chip_swap(low, m).astype(F32)
    low = over_groups(total.astype(BF))
    filt_own = from_z([low] + [z_rot(low, k) for k in range(1, nz)]).reshape(-1, half)
    filt = joined(filt_own, core_swap(filt_own)).astype(F32)
    grad_kernel_long = filt[:length]
    grad_kernel_short = filt[length : length + SHORT_LENGTH]
    tail = filt[length + SHORT_LENGTH :]

    grad_left = (grad_vals * right_part).astype(BF)
    grad_right = (grad_vals * left_part).astype(BF)
    grad_late = jnp.concatenate([grad_left, grad_right], axis=1)
    grad_project = jnp.concatenate([grad_outer, grad_late], axis=1)
    grad_late_w = dot_tn(normed_all, grad_late)
    grad_normed = dot_nt(grad_project, w_in_half)
    grad_normed = grad_normed[:tokens] + core_swap(grad_normed[tokens:].astype(BF)).astype(F32)
    pulled, gain_one = norm_pull(hat_one, inv_one, norm1_gain, grad_normed)
    grad_inputs = grad_residual + pulled
    late_own, late_other, grad_norm1_gain = shares(grad_late_w, gain_one)
    grad_w_in = jnp.concatenate(
        [
            joined(early_own[:, :half], early_other[:, :half]),
            joined(late_own[:, :half], late_other[:, :half]),
            joined(late_own[:, half:], late_other[:, half:]),
        ],
        axis=1,
    ).astype(F32)
    grad_w_out = joined(early_own[:, half:], early_other[:, half:]).astype(F32)

    def placed(x):
        return jnp.swapaxes(x.reshape(slots, owned, width), 0, 1)

    return (
        placed(layer_out),
        placed(grad_inputs),
        grad_norm1_gain,
        grad_w_in,
        grad_kernel_long,
        grad_kernel_short,
        tail[1:4],
        tail[0],
        grad_w_out,
        grad_norm2_gain,
        grad_w_gate_up,
        grad_w_down,
    )


def solution(mesh):
    return jax.shard_map(
        body,
        mesh=mesh,
        in_specs=(
            P("freq", "dp", None),
            P("freq", "dp", None),
            P("dp"),
            P("dp", None),
            P(),
            P("freq", None),
            P("freq", None),
            P("freq", None),
            P(),
            P(),
            P("freq", None),
            P(),
            P("freq", None),
            P("freq", None),
        ),
        out_specs=(
            P("freq", "dp", None),
            P("freq", "dp", None),
            P(),
            P("freq", None),
            P(),
            P(),
            P(),
            P(),
            P("freq", None),
            P(),
            P("freq", None),
            P("freq", None),
        ),
        check_vma=False,
    )
```

```python
import math

import jax
import jax.numpy as jnp
import numpy as np
from jax import lax
from jax.experimental import pallas as pl
from jax.experimental.pallas import tpu as pltpu
from jax.sharding import PartitionSpec as P

SHORT_LENGTH = 128
EPSILON = 1e-05
BF = jnp.bfloat16
F32 = jnp.float32
GROUP = 8
RIDE = 16
GELU_A = math.sqrt(2.0 / math.pi)
GELU_B = 0.044715


def cosine_table(length):
    freq = np.arange(length)[:, None]
    posit = np.arange(length)[None, :]
    phase = (2 * posit + 1) * freq % (4 * length)
    weight = np.where(freq == 0, 1.0, 2.0) / length
    return (np.cos(phase * (math.pi / (2 * length))) * np.sqrt(weight)).astype(np.float32)


def dot(a, b):
    return lax.dot_general(a, b, (((1,), (0,)), ((), ())), preferred_element_type=F32)


def dot_nt(a, b):
    return lax.dot_general(a, b, (((1,), (1,)), ((), ())), preferred_element_type=F32)


def dot_tn(a, b):
    return lax.dot_general(a, b, (((0,), (0,)), ((), ())), preferred_element_type=F32)


def norm_parts(values):
    center = values - jnp.mean(values, axis=-1, keepdims=True)
    spread = jnp.mean(center * center, axis=-1, keepdims=True)
    inv = lax.rsqrt(spread + EPSILON)
    return center * inv, inv


def norm_pull(hat, inv, gain, grad):
    scaled = grad * gain
    mean_one = jnp.mean(scaled, axis=-1, keepdims=True)
    mean_two = jnp.mean(scaled * hat, axis=-1, keepdims=True)
    return inv * (scaled - mean_one - hat * mean_two), jnp.sum(grad * hat, axis=0, keepdims=True)


def pick(stacked, index):
    return lax.dynamic_index_in_dim(stacked, index, axis=0, keepdims=False)


def run(kernel, name, outs, where, ins, scratch=(), after=(), flops=0):
    n_in, n_after = len(ins), len(after)

    def wrapped(*refs):
        kernel(*refs[: 1 + n_in], *refs[1 + n_in + n_after :])

    size = sum(x.size * x.dtype.itemsize for x in ins)
    size += sum(math.prod(s) * jnp.dtype(t).itemsize for s, t in outs)
    return pl.pallas_call(
        wrapped,
        out_shape=[jax.ShapeDtypeStruct(s, t) for s, t in outs],
        in_specs=[pl.BlockSpec(memory_space=pltpu.SMEM)]
        + [pl.BlockSpec(memory_space=pltpu.VMEM)] * n_in
        + [pl.BlockSpec(memory_space=pl.ANY)] * n_after,
        out_specs=[pl.BlockSpec(memory_space=pltpu.VMEM)] * len(outs),
        scratch_shapes=list(scratch),
        compiler_params=pltpu.CompilerParams(vmem_limit_bytes=50 * 2**20),
        cost_estimate=pl.CostEstimate(flops=int(flops), bytes_accessed=int(size), transcendentals=0),
        name=name,
    )(where, *ins, *after)


def rows_at(index, size):
    return pl.ds(pl.multiple_of(index * size, 16), size)


def project_kernel(where, na, nb, local, n1, n2, n3, c1, c2, c3, mask, w, outer, left, right, v0, v1, v2, v3, vals):
    z, chip = where[0], where[1]
    rows = local.shape[0]
    quarter = rows // 4
    half = outer.shape[1]
    w[rows_at(z, rows), :] = local[...]
    for k, near in ((1, n1), (2, n2), (3, n3)):
        base = ((z - k) & 3) * 4
        w[rows_at(base + chip, quarter), :] = near[...]
        for m, far in ((1, c1), (2, c2), (3, c3)):
            w[rows_at(base + (chip ^ m), quarter), :] = far[k - 1]
    count = na.shape[0]
    for i, tokens in enumerate((na, nb)):
        at = pl.ds(i * count, count)
        full = dot(tokens[...], w[...])
        a, b, c = full[:, :half], full[:, half : 2 * half], full[:, 2 * half :]
        outer[at, :] = a
        left[at, :] = b
        right[at, :] = c
        vals[at, :] = (b * c * mask[at, :]).astype(BF)
    owned = v0.shape[0]
    for k, out in enumerate((v0, v1, v2, v3)):
        out[...] = vals[rows_at((z + k) & 3, owned), :]


def neighbours(x, short, length):
    place = lax.broadcasted_iota(jnp.int32, x.shape, 0)
    starts = (place == 0) | (short & (place % SHORT_LENGTH == 0))
    ends = (place == length - 1) | (short & (place % SHORT_LENGTH == SHORT_LENGTH - 1))
    earlier = jnp.where(starts, 0.0, pltpu.roll(x, 1, 0))
    later = jnp.where(ends, 0.0, pltpu.roll(x, length - 1, 0))
    return earlier, later


def fold_kernel(where, v0, r1, r2, r3, table, flipped, base, gain, taps, vals, spectrum, cond_spec, o0, o1, o2, o3, triple, filtered, conv):
    z, short = where[0], where[3] == 1
    owned, half = v0.shape
    length = vals.shape[0]
    for k, piece in enumerate((v0, r1, r2, r3)):
        vals[rows_at((z - k) & 3, owned), :] = piece[...]
    wide = vals[...].astype(F32)
    before, after = neighbours(wide, short, length)
    cond = taps[0:1, :] * before + taps[1:2, :] * wide + taps[2:3, :] * after
    high = cond.astype(BF)
    triple[:, :half] = vals[...]
    triple[:, half : 2 * half] = high
    triple[:, 2 * half :] = (cond - high.astype(F32)).astype(BF)
    step = length // 2
    for i in range(2):
        at = pl.ds(i * step, step)
        folded = dot(table[at, :], triple[...])
        spec = folded[:, :half]
        cspec = folded[:, half : 2 * half] + folded[:, 2 * half :]
        spectrum[at, :] = spec
        cond_spec[at, :] = cspec
        kern = base[at, :] + gain[...] * (jnp.sqrt(cspec * cspec + 1.0) - 1.0)
        filtered[at, :] = (kern * spec).astype(BF)
    conv[...] = dot(flipped[...], filtered[...]).astype(BF)
    for k, out in enumerate((o0, o1, o2, o3)):
        out[...] = conv[rows_at((z + k) & 3, owned), :]


def mix_kernel(where, outer, c0, r1, r2, r3, w_rows, conv, mixed, own, other):
    z = where[0]
    owned = c0.shape[0]
    for k, piece in enumerate((c0, r1, r2, r3)):
        conv[rows_at((z - k) & 3, owned), :] = piece[...]
    mixed[...] = (outer[...] * conv[...].astype(F32)).astype(BF)
    count = own.shape[0]
    own[...] = dot(mixed[pl.ds(0, count), :], w_rows[...])
    other[...] = dot(mixed[pl.ds(count, count), :], w_rows[...]).astype(BF)


def second_kernel(where, x, own, came, gain, residual, normed):
    total = x[...] + own[...] + came[...].astype(F32)
    residual[...] = total
    hat, _ = norm_parts(total)
    normed[...] = (hat * gain[...]).astype(BF)


def feed_kernel(where, sa, sb, ca, cb, w_gu, w_dn, act, grads, own, other):
    half = act.shape[1]
    count = sa.shape[0]
    for i, (second, cot, out) in enumerate(((sa, ca, own), (sb, cb, other))):
        at = pl.ds(i * count, count)
        gate_up = dot(second[...], w_gu[...])
        gate, upward = gate_up[:, :half], gate_up[:, half:]
        grad_act = dot_nt(cot[...], w_dn[...])
        square = gate * gate
        tanh = jnp.tanh(GELU_A * gate * (1.0 + GELU_B * square))
        cdf = 0.5 * (1.0 + tanh)
        unit = gate * cdf
        slope = cdf + 0.5 * gate * (1.0 - tanh * tanh) * (GELU_A * (1.0 + 3.0 * GELU_B * square))
        act[at, :] = (unit * upward).astype(BF)
        grads[at, :half] = (grad_act * upward * slope).astype(BF)
        grads[at, half:] = (grad_act * unit).astype(BF)
        out[...] = dot_nt(grads[at, :], w_gu[...]).astype(out.dtype)


def down_kernel(where, a0, a1, a2, a3, w_dn, p0, p1, p2, p3, others):
    count = p0.shape[0]
    for m, (act, out) in enumerate(((a0, p0), (a1, p1), (a2, p2), (a3, p3))):
        out[...] = dot(act[pl.ds(0, count), :], w_dn[...]).astype(out.dtype)
        others[m] = dot(act[pl.ds(count, count), :], w_dn[...]).astype(BF)


def feed_weight_kernel(where, a0, a1, a2, a3, g0, g1, g2, g3, sa0, sa1, sa2, sa3, sb0, sb1, sb2, sb3, ca, cb, out, acts, grads, seconds, cots):
    chip = where[1]
    count, width = sa0.shape
    for m, (a, g, sa, sb) in enumerate(
        ((a0, g0, sa0, sb0), (a1, g1, sa1, sb1), (a2, g2, sa2, sb2), (a3, g3, sa3, sb3))
    ):
        at = pl.ds(m * 2 * count, 2 * count)
        acts[at, :] = a[...]
        grads[at, :] = g[...]
        seconds[pl.ds(m * 2 * count, count), :] = sa[...]
        seconds[pl.ds(m * 2 * count + count, count), :] = sb[...]
        cots[pl.ds(m * 2 * count, count), :] = ca[m]
        cots[pl.ds(m * 2 * count + count, count), :] = cb[m]
    nz, piece, _ = out.shape
    chunk = acts.shape[1] // 3
    rows = piece - chunk
    total = dot_tn(seconds[...], grads[...])
    for i in range(nz):
        out[i, pl.ds(0, rows), :] = total[i * rows : (i + 1) * rows].astype(BF)
    down = dot_tn(acts[...], cots[...])
    out[chip, pl.ds(rows, chunk), :] = jnp.zeros((chunk, width), BF)
    for i in range(3):
        to = i + (i >= chip).astype(jnp.int32)
        out[to, pl.ds(rows, chunk), :] = down[i * chunk : (i + 1) * chunk].astype(BF)


def second_back_kernel(where, residual, gain, cot, own, r1, r2, r3, grad_residual, low, grad_gain):
    grad = own[...] + r1[...].astype(F32) + r2[...].astype(F32) + r3[...].astype(F32)
    hat, inv = norm_parts(residual[...])
    pulled, grad_gain[...] = norm_pull(hat, inv, gain[...], grad)
    total = cot[...] + pulled
    grad_residual[...] = total
    low[...] = total.astype(BF)


def mix_back_kernel(where, ga, gb, w_rows, outer, conv, grad_outer, o0, o1, o2, o3, grad_conv):
    z = where[0]
    count = ga.shape[0]
    for i, grad in enumerate((ga, gb)):
        at = pl.ds(i * count, count)
        mixed = dot_nt(grad[...], w_rows[...])
        grad_outer[at, :] = (mixed * conv[at, :].astype(F32)).astype(BF)
        grad_conv[at, :] = (mixed * outer[at, :]).astype(BF)
    owned = o0.shape[0]
    for k, out in enumerate((o0, o1, o2, o3)):
        out[...] = grad_conv[rows_at((z + k) & 3, owned), :]


def fold_back_kernel(where, g0, r1, r2, r3, table, flipped, spectrum, cond_spec, base, gain, taps, vals, o0, o1, o2, o3, f0, f1, f2, f3, grads, double, filters):
    z, short = where[0], where[3] == 1
    owned, half = g0.shape
    length = vals.shape[0]
    for k, piece in enumerate((g0, r1, r2, r3)):
        grads[rows_at((z - k) & 3, owned), :] = piece[...]
    gf = dot(table[...], grads[...])
    cspec = cond_spec[...]
    root = jnp.sqrt(cspec * cspec + 1.0)
    above = root - 1.0
    grad_base = gf * spectrum[...]
    double[:, :half] = (gf * (base[...] + gain[...] * above)).astype(BF)
    double[:, half:] = (grad_base * gain[...] * (cspec / root)).astype(BF)
    unfolded = dot(flipped[...], double[...])
    grad_cond = unfolded[:, half:]
    wide = vals[...].astype(F32)
    before, after = neighbours(wide, short, length)
    grad_before, grad_after = neighbours(grad_cond, short, length)
    grads[...] = (
        unfolded[:, :half]
        + taps[0:1, :] * grad_after
        + taps[1:2, :] * grad_cond
        + taps[2:3, :] * grad_before
    ).astype(BF)
    for k, out in enumerate((o0, o1, o2, o3)):
        out[...] = grads[rows_at((z + k) & 3, owned), :]
    is_short = jnp.where(short, 1.0, 0.0)
    filters[pl.ds(0, length), :] = (grad_base * (1.0 - is_short)).astype(BF)
    folded = grad_base[:SHORT_LENGTH]
    for i in range(1, length // SHORT_LENGTH):
        folded = folded + grad_base[i * SHORT_LENGTH : (i + 1) * SHORT_LENGTH]
    filters[pl.ds(length, SHORT_LENGTH), :] = (folded * is_short).astype(BF)
    rest = filters.shape[0] - length - SHORT_LENGTH
    small = [
        jnp.sum(grad_base * above, axis=0, keepdims=True),
        jnp.sum(grad_cond * before, axis=0, keepdims=True),
        jnp.sum(grad_cond * wide, axis=0, keepdims=True),
        jnp.sum(grad_cond * after, axis=0, keepdims=True),
        jnp.zeros((rest - 4, half), F32),
    ]
    filters[pl.ds(length + SHORT_LENGTH, rest), :] = jnp.concatenate(small, axis=0).astype(BF)
    size = f0.shape[0]
    for k, out in enumerate((f0, f1, f2, f3)):
        out[...] = filters[rows_at((z + k) & 3, size), :]


def write_pieces(whole, outs, chip):
    rows = whole.shape[0] // 4
    quarter = rows // 4
    for m, out in enumerate(outs):
        for i in range(4):
            out[pl.ds(i * quarter, quarter), :] = whole[rows_at(i * 4 + (chip ^ m), quarter), :]


def late_kernel(where, g0, r1, r2, r3, left, right, mask, na, nb, late, p0, p1, p2, p3, grads, whole):
    z, chip = where[0], where[1]
    owned, half = g0.shape
    for k, piece in enumerate((g0, r1, r2, r3)):
        grads[rows_at((z - k) & 3, owned), :] = piece[...].astype(F32)
    count = na.shape[0]
    for i in range(2):
        at = pl.ds(i * count, count)
        grad = grads[at, :] * mask[at, :]
        late[at, :half] = (grad * right[at, :]).astype(BF)
        late[at, half:] = (grad * left[at, :]).astype(BF)
    total = dot_tn(na[...], late[pl.ds(0, count), :]) + dot_tn(nb[...], late[pl.ds(count, count), :])
    whole[...] = total.astype(BF)
    write_pieces(whole, (p0, p1, p2, p3), chip)


def early_kernel(where, na, nb, grad_outer, mixed, other_mixed, ga, gb, p0, p1, p2, p3, whole):
    chip, core = where[1], where[2]
    count = na.shape[0]
    half = mixed.shape[1]
    total = dot_tn(na[...], grad_outer[pl.ds(0, count), :])
    total = total + dot_tn(nb[...], grad_outer[pl.ds(count, count), :])
    whole[:, :half] = total.astype(BF)
    first = jnp.where(core == 0, ga[:, :half], ga[:, half:])
    second = jnp.where(core == 0, gb[:, :half], gb[:, half:])
    mine = dot_tn(mixed[pl.ds(0, count), :], first) + dot_tn(mixed[pl.ds(count, count), :], second)
    theirs = dot_tn(other_mixed[pl.ds(count, count), :], first)
    theirs = theirs + dot_tn(other_mixed[pl.ds(0, count), :], second)
    whole[rows_at(core, half), half:] = mine.astype(BF)
    whole[rows_at(1 - core, half), half:] = theirs.astype(BF)
    write_pieces(whole, (p0, p1, p2, p3), chip)


def first_grad_kernel(where, grad_outer, late, w, own, other):
    half = grad_outer.shape[1]
    count = own.shape[0]
    for i, out in enumerate((own, other)):
        at = pl.ds(i * count, count)
        total = dot_nt(grad_outer[at, :], w[:, :half]) + dot_nt(late[at, :], w[:, half:])
        out[...] = total.astype(out.dtype)


def first_back_kernel(where, x, gain, grad_residual, own, came, grad_inputs, grad_gain):
    grad = own[...] + came[...].astype(F32)
    hat, inv = norm_parts(x[...])
    pulled, grad_gain[...] = norm_pull(hat, inv, gain[...], grad)
    grad_inputs[...] = grad_residual[...] + pulled


def share_kernel(where, own, r1, r2, r3, ride, o0, o1, o2, o3, total):
    z = where[0]
    total[...] = (
        own[...].astype(F32) + r1[...].astype(F32) + r2[...].astype(F32) + r3[...].astype(F32)
    ).astype(BF)
    quarter = own.shape[0] // 4
    width = own.shape[1]
    first = lax.broadcasted_iota(jnp.int32, (RIDE, width), 0) == 0
    extra = jnp.where(first, jnp.broadcast_to(ride[...], (RIDE, width)), 0.0).astype(BF)
    for k, out in enumerate((o0, o1, o2, o3)):
        out[pl.ds(0, quarter), :] = total[rows_at((z + k) & 3, quarter), :]
        out[pl.ds(quarter, RIDE), :] = extra


def sum_kernel(where, own, r1, r2, r3, out):
    total = own[...].astype(F32) + r1[...].astype(F32) + r2[...].astype(F32) + r3[...].astype(F32)
    out[...] = total.astype(out.dtype)


def order_kernel(where, own, r1, r2, r3, out):
    chip = where[1]
    quarter = own.shape[0] - RIDE
    riding = jnp.zeros((1, own.shape[1]), F32)
    for m, piece in enumerate((own, r1, r2, r3)):
        out[rows_at(chip ^ m, quarter), :] = piece[pl.ds(0, quarter), :]
        riding = riding + piece[pl.ds(quarter, RIDE), :].astype(F32)[0:1]
    first = lax.broadcasted_iota(jnp.int32, (RIDE, own.shape[1]), 0) == 0
    extra = jnp.where(first, jnp.broadcast_to(riding, (RIDE, own.shape[1])), 0.0)
    out[pl.ds(4 * quarter, RIDE), :] = extra.astype(BF)


def feed_order_kernel(where, shares, gate_up, down):
    z = where[0]
    rows = gate_up.shape[0]
    chunk = shares.shape[1] - rows
    per_z = 6 * chunk
    for side in range(2):
        for zz in range(4):
            for c in range(6):
                mm = c if c < 2 * zz else c + 2
                at = (side * 3 + zz - (zz > mm // 2)) * chunk
                to = side * 4 * per_z + zz * per_z + c * chunk
                gate_up[:, to : to + chunk] = shares[mm, :rows, at : at + chunk].astype(F32)
    for c in range(6):
        mm = c + 2 * (c >= 2 * z).astype(jnp.int32)
        down[pl.ds(c * chunk, chunk), :] = shares[mm, pl.ds(rows, chunk), :].astype(F32)


def last_kernel(where, early, early_other, late, late_other, w_in, w_out):
    core = where[2]
    rows = w_in.shape[0]
    width = w_out.shape[1]
    half = width // 2
    for own, other, at, to, out in (
        (early, early_other, 0, 0, w_in),
        (late, late_other, 0, width, w_in),
        (late, late_other, half, 2 * width, w_in),
        (early, early_other, half, 0, w_out),
    ):
        a = own[:rows, at : at + half].astype(F32)
        b = other[:rows, at : at + half].astype(F32)
        out[:, to : to + half] = jnp.where(core == 0, a, b)
        out[:, to + half : to + width] = jnp.where(core == 0, b, a)


def body(
    inputs,
    cotangent,
    group,
    lens,
    norm1_gain,
    w_in,
    kernel_long,
    kernel_short,
    conv_weight,
    cond_gain,
    w_out,
    norm2_gain,
    w_gate_up,
    w_down,
):
    nz = lax.axis_size("freq")
    ndp = lax.axis_size("dp")
    z = lax.axis_index("freq")
    d = lax.axis_index("dp")
    core = d % 2
    chip = (d // 2) % 4
    member = d % GROUP
    owned, slots, width = inputs.shape
    half = width // 2
    length = owned * nz
    tokens = owned * slots
    rows = w_in.shape[0]
    quarter = rows // 4
    others = ndp // GROUP
    across = [[i + GROUP * g for g in range(others)] for i in range(GROUP)]
    blocks = [[g * GROUP + i for i in range(GROUP)] for g in range(others)]

    def core_swap(x):
        return lax.ppermute(x, "dp", [(i, i ^ 1) for i in range(ndp)])

    def chip_swap(x, m):
        return lax.ppermute(x, "dp", [(i, i ^ (2 * m)) for i in range(ndp)])

    def z_rot(x, k):
        return lax.ppermute(x, "freq", [(i, (i + k) % nz) for i in range(nz)])

    def mine(x, axis=-1):
        low, high = jnp.split(x, 2, axis=axis)
        return jnp.where(core == 0, low, high)

    def theirs(x, axis=-1):
        low, high = jnp.split(x, 2, axis=axis)
        return jnp.where(core == 0, high, low)

    def joined(own, other, axis=-1):
        return jnp.where(
            core == 0,
            jnp.concatenate([own, other], axis=axis),
            jnp.concatenate([other, own], axis=axis),
        )

    def from_z(rel):
        stacked = jnp.stack(rel)
        return jnp.concatenate([pick(stacked, (z - i) % nz) for i in range(nz)], axis=0)

    def z_swap(pieces):
        return [pieces[0]] + [z_rot(pieces[k], k) for k in range(1, nz)]

    def over_groups(x):
        if others > 1:
            return lax.psum(x, "dp", axis_index_groups=across)
        return x

    def in_cols(x):
        return jnp.concatenate([mine(x[:, i * width : (i + 1) * width]) for i in range(3)], axis=1)

    near = in_cols(lax.dynamic_slice_in_dim(w_in, chip * quarter, quarter, axis=0))
    in_near = [z_rot(near, k) for k in range(1, nz)]
    in_stack = jnp.stack(in_near)
    in_far = [chip_swap(in_stack, m) for m in (1, 2, 3)]

    out_local = mine(w_out)
    out_piece = lax.dynamic_slice_in_dim(out_local, chip * quarter, quarter, axis=0)
    out_near = [z_rot(out_piece, k) for k in range(1, nz)]
    out_stack = jnp.stack(out_near)
    out_far = [chip_swap(out_stack, m) for m in (1, 2, 3)]
    rel = [out_local]
    for k in range(nz - 1):
        by_chip = jnp.stack([out_near[k]] + [piece[k] for piece in out_far])
        rel.append(jnp.concatenate([pick(by_chip, chip ^ i) for i in range(4)], axis=0))
    out_cols = from_z(rel)
    w_out_rows = joined(mine(out_cols, 0), core_swap(theirs(out_cols, 0)))

    filt_piece = jnp.concatenate([mine(kernel_long), mine(kernel_short)], axis=0)
    filt_rel = z_swap([filt_piece] * nz)
    long_base = from_z([x[:owned] for x in filt_rel])
    short_base = from_z([x[owned:] for x in filt_rel])

    hidden = w_down.shape[0] * nz
    per_z = w_down.shape[0]
    chunk = per_z // 6

    def chunk_of(zz):
        return jnp.where(member < 2 * zz, member, member - 2)

    pieces = []
    for side in range(2):
        for i in range(3):
            zz = i + (i >= chip).astype(jnp.int32)
            start = side * hidden + zz * per_z + chunk_of(zz) * chunk
            pieces.append(lax.dynamic_slice_in_dim(w_gate_up, start, chunk, axis=1))
    down_piece = lax.dynamic_slice_in_dim(
        w_down, jnp.clip(chunk_of(z), 0, 5) * chunk, chunk, axis=0
    )
    mlp_piece = jnp.concatenate([jnp.concatenate(pieces, axis=1), down_piece], axis=0)
    mlp_all = lax.all_gather(mlp_piece, "freq", axis=0)
    w_gu = mlp_all[:, :rows].reshape(width, width)
    down_four = mlp_all[:, rows:]
    w_dn = jnp.concatenate(
        [pick(down_four, i + (i >= chip).astype(jnp.int32)) for i in range(3)], axis=0
    )

    x_own = jnp.swapaxes(inputs, 0, 1).reshape(tokens, width)
    cot_own = jnp.swapaxes(cotangent, 0, 1).reshape(tokens, width)
    cot_low = cot_own.astype(BF)
    cot_near = jnp.stack([cot_low] + [chip_swap(cot_low, m) for m in (1, 2, 3)])
    cot_far = core_swap(cot_near)

    marks = jnp.concatenate([group[:, None], lens], axis=1)
    marks = jnp.concatenate([marks, core_swap(marks)], axis=0)
    group_all = marks[:, 0]
    lens_all = marks[:, 1:]
    posit = z * owned + jnp.arange(owned, dtype=jnp.int32)
    hit = (posit // SHORT_LENGTH)[None, :, None] == jnp.arange(lens.shape[1], dtype=jnp.int32)
    quarter_len = jnp.sum(jnp.where(hit, lens_all[:, None, :], 0), axis=2)
    mask = jnp.where(
        group_all[:, None] == 1,
        (posit % SHORT_LENGTH)[None, :] < quarter_len,
        posit[None, :] < jnp.sum(lens_all, axis=1)[:, None],
    )
    mask = mask.astype(F32).reshape(2 * tokens, 1)
    slot_group = pick(group_all, z)
    where = jnp.stack([z, chip, core, slot_group, z, z, z, z]).astype(jnp.int32)

    repeat = length // SHORT_LENGTH
    long_table = cosine_table(length)
    short_table = np.kron(np.eye(repeat), cosine_table(SHORT_LENGTH)).astype(np.float32)
    is_short = slot_group == 1
    table = jnp.where(is_short, jnp.asarray(short_table, BF), jnp.asarray(long_table, BF))
    flipped = jnp.where(is_short, jnp.asarray(short_table.T, BF), jnp.asarray(long_table.T, BF))
    base = jnp.where(is_short, jnp.tile(short_base, (repeat, 1)), long_base).astype(F32)
    gain_half = mine(cond_gain)[None]
    taps = mine(conv_weight)
    gain_one = norm1_gain[None]
    gain_two = norm2_gain[None]

    hat_one, _ = norm_parts(x_own)
    normed = (hat_one * gain_one).astype(BF)
    normed_other = core_swap(normed)
    piece = ((owned, half), BF)
    many = 2 * tokens
    w_in_half, outer, left, right, *sends = run(
        project_kernel,
        "project",
        [((width, 3 * half), BF)] + [((many, half), F32)] * 3 + [piece] * 4,
        where,
        [normed, normed_other, in_cols(w_in), *in_near, *in_far, mask],
        [pltpu.VMEM((many, half), BF)],
        flops=2 * many * width * 3 * half,
    )
    came = z_swap(sends)
    vals, spectrum, cond_spec, *sends = run(
        fold_kernel,
        "fold",
        [((length, half), BF)] + [((length, half), F32)] * 2 + [piece] * 4,
        where,
        [*came, table, flipped, base, gain_half, taps],
        [
            pltpu.VMEM((length, 3 * half), BF),
            pltpu.VMEM((length, half), BF),
            pltpu.VMEM((length, half), BF),
        ],
        flops=2 * length * length * 4 * half,
    )
    came = z_swap(sends)
    conv, mixed, part_own, part_other = run(
        mix_kernel,
        "mix",
        [((many, half), BF)] * 2 + [((tokens, width), F32), ((tokens, width), BF)],
        where,
        [outer, *came, w_out_rows],
        flops=2 * many * half * width,
    )
    residual, normed_two = run(
        second_kernel,
        "second_norm",
        [((tokens, width), F32), ((tokens, width), BF)],
        where,
        [x_own, part_own, core_swap(part_other), gain_two],
        flops=tokens * width * 12,
    )

    arrived = [normed_two] + [chip_swap(normed_two, m) for m in (1, 2, 3)]
    seconds, acts, grads_gu, sums = [], [], [], []
    order = ()
    for m in range(4):
        second = core_swap(arrived[m])
        act, grad_gu, own, other = run(
            feed_kernel,
            "feed",
            [((many, half), BF), ((many, width), BF), ((tokens, width), F32), ((tokens, width), BF)],
            where,
            [arrived[m], second, cot_near[m], cot_far[m], w_gu, w_dn],
            after=order,
            flops=2 * many * width * (2 * width + half),
        )
        order = (act,)
        seconds.append(second)
        acts.append(act)
        grads_gu.append(grad_gu)
        sums.append(own + core_swap(other).astype(F32))
    backs = [chip_swap(sums[m].astype(BF), m) for m in (1, 2, 3)]
    grad_residual, grad_mix, grad_gain_two = run(
        second_back_kernel,
        "second_norm_back",
        [((tokens, width), F32), ((tokens, width), BF), ((1, width), F32)],
        where,
        [residual, gain_two, cot_own, sums[0], *backs],
        flops=tokens * width * 30,
    )
    grad_mix_other = core_swap(grad_mix)
    grad_outer, *sends = run(
        mix_back_kernel,
        "mix_back",
        [((many, half), BF)] + [piece] * 4,
        where,
        [grad_mix, grad_mix_other, w_out_rows, outer, conv],
        [pltpu.VMEM((many, half), BF)],
        flops=2 * many * half * width,
    )
    came = z_swap(sends)

    mlp_grads = run(
        feed_weight_kernel,
        "feed_weights",
        [((nz, rows + chunk, width), BF)],
        where,
        [*acts, *grads_gu, *arrived, *seconds, cot_near, cot_far],
        [
            pltpu.VMEM((4 * many, half), BF),
            pltpu.VMEM((4 * many, width), BF),
            pltpu.VMEM((4 * many, width), BF),
            pltpu.VMEM((4 * many, width), BF),
        ],
        after=(grad_outer,),
        flops=2 * 4 * many * width * (width + half),
    )[0]
    mlp_share = lax.psum_scatter(mlp_grads, "freq", scatter_dimension=0, tiled=False)
    mlp_share = over_groups(mlp_share)
    mlp_sum = lax.all_gather(mlp_share, "dp", axis=0, axis_index_groups=blocks)
    grad_w_gate_up, grad_w_down = run(
        feed_order_kernel,
        "feed_order",
        [((rows, 2 * hidden), F32), ((per_z, width), F32)],
        where,
        [mlp_sum],
    )

    def shares(parts, ride):
        total = [parts[0]] + [chip_swap(parts[m], m) for m in (1, 2, 3)]
        sends = run(
            share_kernel,
            "share",
            [((quarter + RIDE, width), BF)] * 4,
            where,
            [*total, ride],
            [pltpu.VMEM((rows, width), BF)],
        )
        piece = run(sum_kernel, "sum", [((quarter + RIDE, width), BF)], where, z_swap(sends))[0]
        piece = over_groups(piece)
        rel = [piece] + [chip_swap(piece, m) for m in (1, 2, 3)]
        own = run(order_kernel, "order", [((rows + RIDE, width), BF)], where, rel)[0]
        return own, core_swap(own)

    parts = run(
        early_kernel,
        "early_weights",
        [((rows, width), BF)] * 4,
        where,
        [normed, normed_other, grad_outer, mixed, core_swap(mixed), grad_mix, grad_mix_other],
        [pltpu.VMEM((width, width), BF)],
        after=(mlp_grads,),
        flops=2 * many * width * width,
    )
    early, early_other = shares(parts, grad_gain_two)

    fill = -(length + SHORT_LENGTH + 4) % (nz * 16)
    size = (length + SHORT_LENGTH + 4 + fill) // nz
    *sends, f0, f1, f2, f3 = run(
        fold_back_kernel,
        "fold_back",
        [piece] * 4 + [((size, half), BF)] * 4,
        where,
        [*came, table, flipped, spectrum, cond_spec, base, gain_half, taps, vals],
        [
            pltpu.VMEM((length, half), BF),
            pltpu.VMEM((length, 2 * half), BF),
            pltpu.VMEM((size * nz, half), BF),
        ],
        flops=2 * length * length * 3 * half,
    )
    came = z_swap(sends)
    late, *parts = run(
        late_kernel,
        "late_weights",
        [((many, width), BF)] + [((rows, width), BF)] * 4,
        where,
        [*came, left, right, mask, normed, normed_other],
        [pltpu.VMEM((many, half), F32), pltpu.VMEM((width, width), BF)],
        flops=2 * many * width * width,
    )
    own, other = run(
        first_grad_kernel,
        "first_grad",
        [((tokens, width), F32), ((tokens, width), BF)],
        where,
        [grad_outer, late, w_in_half],
        flops=2 * many * width * 3 * half,
    )
    grad_inputs, grad_gain_one = run(
        first_back_kernel,
        "first_norm_back",
        [((tokens, width), F32), ((1, width), F32)],
        where,
        [x_own, gain_one, grad_residual, own, core_swap(other)],
        flops=tokens * width * 30,
    )
    late_own, late_other = shares(parts, grad_gain_one)

    low = run(sum_kernel, "sum", [((size, half), BF)], where, z_swap([f0, f1, f2, f3]))[0]
    near = [low] + [chip_swap(low, m) for m in (1, 2, 3)]
    low = run(sum_kernel, "sum", [((size, half), BF)], where, near)[0]
    low = over_groups(low)
    filt_own = from_z(z_swap([low] * nz))
    filt = joined(filt_own, core_swap(filt_own)).astype(F32)
    tail = filt[length + SHORT_LENGTH :]

    p0, p1, p2, p3, far = run(
        down_kernel,
        "down",
        [((tokens, width), F32)] * 4 + [((4, tokens, width), BF)],
        where,
        [*acts, w_dn],
        after=(parts[0],),
        flops=2 * 4 * many * width * half,
    )
    far = core_swap(far)
    layer_out = residual + p0 + far[0].astype(F32)
    for m, part in ((1, p1), (2, p2), (3, p3)):
        part = (part + far[m].astype(F32)).astype(BF)
        layer_out = layer_out + chip_swap(part, m).astype(F32)

    grad_w_in, grad_w_out = run(
        last_kernel,
        "last",
        [((rows, 3 * width), F32), ((rows, width), F32)],
        where,
        [early, early_other, late_own, late_other],
    )

    def riding(own, other):
        return own[rows].astype(F32) + other[rows].astype(F32)

    def placed(x):
        return jnp.swapaxes(x.reshape(slots, owned, width), 0, 1)

    return (
        placed(layer_out),
        placed(grad_inputs),
        riding(late_own, late_other),
        grad_w_in,
        filt[:length],
        filt[length : length + SHORT_LENGTH],
        tail[1:4],
        tail[0],
        grad_w_out,
        riding(early, early_other),
        grad_w_gate_up,
        grad_w_down,
    )


def solution(mesh):
    return jax.shard_map(
        body,
        mesh=mesh,
        in_specs=(
            P("freq", "dp", None),
            P("freq", "dp", None),
            P("dp"),
            P("dp", None),
            P(),
            P("freq", None),
            P("freq", None),
            P("freq", None),
            P(),
            P(),
            P("freq", None),
            P(),
            P("freq", None),
            P("freq", None),
        ),
        out_specs=(
            P("freq", "dp", None),
            P("freq", "dp", None),
            P(),
            P("freq", None),
            P(),
            P(),
            P(),
            P(),
            P("freq", None),
            P(),
            P("freq", None),
            P("freq", None),
        ),
        check_vma=False,
    )
```

```python
import functools
import math

import jax
import jax.numpy as jnp
import numpy as np
from jax import lax
from jax.experimental import pallas as pl
from jax.experimental.pallas import tpu as pltpu
from jax.sharding import PartitionSpec as P

SHORT_LENGTH = 128
EPSILON = 1e-05
BF = jnp.bfloat16
F32 = jnp.float32
GROUP = 8
RIDE = 16
COSTS = {
    "project": 20,
    "fold": 20,
    "mix": 15,
    "second_norm": 4,
    "feed": 5,
    "feed_place": 3,
    "down": 4,
    "feed_weights": 5,
    "second_norm_back": 12,
    "mix_back": 5,
    "fold_back": 20,
    "late_weights": 15,
    "first_grad": 4,
    "first_norm_back": 3,
    "late_share": 22,
    "late_sum": 20,
    "gather": 15,
    "last": 6,
    "feed_order": 4,
}
GELU_A = math.sqrt(2.0 / math.pi)
GELU_B = 0.044715


def cosine_table(length):
    freq = np.arange(length)[:, None]
    posit = np.arange(length)[None, :]
    phase = (2 * posit + 1) * freq % (4 * length)
    weight = np.where(freq == 0, 1.0, 2.0) / length
    return (np.cos(phase * (math.pi / (2 * length))) * np.sqrt(weight)).astype(np.float32)


def dot(a, b):
    return lax.dot_general(a, b, (((1,), (0,)), ((), ())), preferred_element_type=F32)


def dot_nt(a, b):
    return lax.dot_general(a, b, (((1,), (1,)), ((), ())), preferred_element_type=F32)


def dot_tn(a, b):
    return lax.dot_general(a, b, (((0,), (0,)), ((), ())), preferred_element_type=F32)


def norm_parts(values):
    center = values - jnp.mean(values, axis=-1, keepdims=True)
    spread = jnp.mean(center * center, axis=-1, keepdims=True)
    inv = lax.rsqrt(spread + EPSILON)
    return center * inv, inv


def norm_pull(hat, inv, gain, grad):
    scaled = grad * gain
    mean_one = jnp.mean(scaled, axis=-1, keepdims=True)
    mean_two = jnp.mean(scaled * hat, axis=-1, keepdims=True)
    return inv * (scaled - mean_one - hat * mean_two), jnp.sum(grad * hat, axis=0, keepdims=True)


def pick(stacked, index):
    return lax.dynamic_index_in_dim(stacked, index, axis=0, keepdims=False)


def run(kernel, name, outs, where, ins, scratch=(), after=()):
    after = [x for x in after if x is not None]
    n_in, n_after = len(ins), len(after)

    def wrapped(*refs):
        kernel(*refs[: 1 + n_in], *refs[1 + n_in + n_after :])

    size = sum(x.size * x.dtype.itemsize for x in ins)
    size += sum(math.prod(s) * jnp.dtype(t).itemsize for s, t in outs)
    return pl.pallas_call(
        wrapped,
        out_shape=[jax.ShapeDtypeStruct(s, t) for s, t in outs],
        in_specs=[pl.BlockSpec(memory_space=pltpu.SMEM)]
        + [
            pl.BlockSpec(memory_space=pltpu.SMEM if x.dtype == jnp.int32 else pltpu.VMEM)
            for x in ins
        ]
        + [pl.BlockSpec(memory_space=pl.ANY)] * n_after,
        out_specs=[pl.BlockSpec(memory_space=pltpu.VMEM)] * len(outs),
        scratch_shapes=list(scratch),
        compiler_params=pltpu.CompilerParams(vmem_limit_bytes=50 * 2**20),
        cost_estimate=pl.CostEstimate(
            flops=int(COSTS.get(name, 1) * 1.15e9), bytes_accessed=int(size), transcendentals=0
        ),
        name=name,
    )(where, *ins, *after)


def rows_at(index, size):
    return pl.ds(pl.multiple_of(index * size, 16), size)


def feed_pick_kernel(where, w_gate_up, w_down, out):
    z, chip, core = where[0], where[1], where[2]
    rows, columns = w_gate_up.shape
    hidden = columns // 2
    per_z = w_down.shape[0]
    chunk = per_z // 6
    member = 2 * chip + core
    for side in range(2):
        for i in range(3):
            zz = i + (i >= chip).astype(jnp.int32)
            c = jnp.where(member < 2 * zz, member, member - 2)
            start = pl.multiple_of(side * hidden + zz * per_z + c * chunk, 128)
            to = (side * 3 + i) * chunk
            out[pl.ds(0, rows), to : to + chunk] = w_gate_up[:, pl.ds(start, chunk)]
    c = jnp.clip(jnp.where(member < 2 * z, member, member - 2), 0, 5)
    out[pl.ds(rows, chunk), :] = w_down[rows_at(c, chunk), :]


def hand_on_kernel(where, n1, n2, n3, in_stack, out_stack):
    wide = in_stack.shape[2]
    for k, near in enumerate((n1, n2, n3)):
        in_stack[k] = near[:, :wide]
        out_stack[k] = near[:, wide:]


def project_kernel(where, marks_own, marks_other, na, nb, local, n1, n2, n3, c1, c2, c3, out_near, cot_in, long_in, short_in, w, outer, left, right, v0, v1, v2, v3, out_stack, cot_low, long, short, vals):
    z, chip = where[0], where[1]
    out_stack[...] = out_near[...]
    cot_low[...] = cot_in[...].astype(BF)
    rows = local.shape[0]
    quarter = rows // 4
    half = outer.shape[1]
    wide = 3 * half
    owned, part = long_in.shape[0], short_in.shape[0]

    def place_filters(at, piece):
        a, b = owned // 4, part // 4
        long[pl.ds(pl.multiple_of(at * a, 8), a), :] = piece[:a]
        short[pl.ds(pl.multiple_of(at * b, 8), b), :] = piece[a : a + b]

    w[rows_at(z, rows), :] = local[...]
    long[rows_at(z, owned), :] = long_in[...].astype(F32)
    short[rows_at(z, part), :] = short_in[...].astype(F32)
    for k, near in ((1, n1), (2, n2), (3, n3)):
        base = ((z - k) & 3) * 4
        w[rows_at(base + chip, quarter), :] = near[:, :wide]
        place_filters(base + chip, near[:, wide : wide + half].astype(F32))
        for m, far in ((1, c1), (2, c2), (3, c3)):
            w[rows_at(base + (chip ^ m), quarter), :] = far[k - 1, :, :wide]
            place_filters(base + (chip ^ m), far[k - 1, :, wide:].astype(F32))
    count = na.shape[0]
    place = lax.broadcasted_iota(jnp.int32, (owned, half), 0)
    for i, (tokens, marks) in enumerate(((na, marks_own), (nb, marks_other))):
        at = pl.ds(i * count, count)
        full = dot(tokens[...], w[...])
        a, b, c = full[:, :half], full[:, half : 2 * half], full[:, 2 * half :]
        outer[at, :] = a
        left[at, :] = b
        right[at, :] = c
        for s in range(count // owned):
            valid = valid_rows(marks, s, z, owned)
            low = slice(s * owned, (s + 1) * owned)
            vals[pl.ds(i * count + s * owned, owned), :] = jnp.where(
                place < valid, b[low] * c[low], 0.0
            ).astype(BF)
    for k, out in enumerate((v0, v1, v2, v3)):
        out[...] = vals[rows_at((z + k) & 3, owned), :]


def valid_rows(marks, s, z, owned):
    total = marks[s, 1] + marks[s, 2] + marks[s, 3] + marks[s, 4]
    return jnp.where(marks[s, 0] == 1, marks[s, 1 + z], total - owned * z)


def neighbours(x, short, length):
    place = lax.broadcasted_iota(jnp.int32, x.shape, 0)
    starts = (place == 0) | (short & (place % SHORT_LENGTH == 0))
    ends = (place == length - 1) | (short & (place % SHORT_LENGTH == SHORT_LENGTH - 1))
    earlier = jnp.where(starts, 0.0, pltpu.roll(x, 1, 0))
    later = jnp.where(ends, 0.0, pltpu.roll(x, length - 1, 0))
    return earlier, later


def fold_kernel(where, v0, r1, r2, r3, long, short_base, table, flipped, gain, taps, vals, spectrum, cond_spec, base, o0, o1, o2, o3, triple, filtered, conv):
    z, short = where[0], where[3] == 1
    owned, half = v0.shape
    length = vals.shape[0]
    for i in range(length // SHORT_LENGTH):
        at = pl.ds(i * SHORT_LENGTH, SHORT_LENGTH)
        base[at, :] = jnp.where(short, short_base[...], long[at, :])
    for k, piece in enumerate((v0, r1, r2, r3)):
        vals[rows_at((z - k) & 3, owned), :] = piece[...]
    wide = vals[...].astype(F32)
    before, after = neighbours(wide, short, length)
    cond = taps[0:1, :] * before + taps[1:2, :] * wide + taps[2:3, :] * after
    high = cond.astype(BF)
    triple[:, :half] = vals[...]
    triple[:, half : 2 * half] = high
    triple[:, 2 * half :] = (cond - high.astype(F32)).astype(BF)
    step = length // 2
    for i in range(2):
        at = pl.ds(i * step, step)
        folded = dot(table[at, :], triple[...])
        spec = folded[:, :half]
        cspec = folded[:, half : 2 * half] + folded[:, 2 * half :]
        spectrum[at, :] = spec
        cond_spec[at, :] = cspec
        kern = base[at, :] + gain[...] * (jnp.sqrt(cspec * cspec + 1.0) - 1.0)
        filtered[at, :] = (kern * spec).astype(BF)
    conv[...] = dot(flipped[...], filtered[...]).astype(BF)
    for k, out in enumerate((o0, o1, o2, o3)):
        out[...] = conv[rows_at((z + k) & 3, owned), :]


def out_rows_kernel(where, mlp_in, local, near_all, c1, c2, c3, keep, send, mlp_all, whole):
    z, chip, core = where[0], where[1], where[2]
    rows, half = local.shape
    mlp_all[...] = mlp_in[...]
    quarter = rows // 4
    whole[rows_at(z, rows), :] = local[...]
    for k in (1, 2, 3):
        base = ((z - k) & 3) * 4
        whole[rows_at(base + chip, quarter), :] = near_all[k - 1]
        for m, far in ((1, c1), (2, c2), (3, c3)):
            whole[rows_at(base + (chip ^ m), quarter), :] = far[k - 1]
    keep[...] = whole[rows_at(core, half), :]
    send[...] = whole[rows_at(1 - core, half), :]


def mix_kernel(where, outer, c0, r1, r2, r3, w_keep, w_came, conv, mixed, own, other, w_rows):
    z, core = where[0], where[2]
    half = outer.shape[1]
    w_rows[:, :half] = jnp.where(core == 0, w_keep[...], w_came[...])
    w_rows[:, half:] = jnp.where(core == 0, w_came[...], w_keep[...])
    owned = c0.shape[0]
    for k, piece in enumerate((c0, r1, r2, r3)):
        conv[rows_at((z - k) & 3, owned), :] = piece[...]
    mixed[...] = (outer[...] * conv[...].astype(F32)).astype(BF)
    count = own.shape[0]
    own[...] = dot(mixed[pl.ds(0, count), :], w_rows[...])
    other[...] = dot(mixed[pl.ds(count, count), :], w_rows[...]).astype(BF)


def second_kernel(where, x, own, came, gain, residual, normed):
    total = x[...] + own[...] + came[...].astype(F32)
    residual[...] = total
    hat, _ = norm_parts(total)
    normed[...] = (hat * gain[...]).astype(BF)


def feed_place_kernel(where, own, other, w_gu, w_dn):
    chip = where[1]
    rows = w_gu.shape[1] // 4
    chunk = own.shape[1] - rows
    for p, part in enumerate((own, other)):
        for i in range(4):
            w_gu[p, pl.ds(i * rows, rows), :] = part[i, pl.ds(0, rows), :]
        for i in range(3):
            at = i + (i >= chip).astype(jnp.int32)
            w_dn[p, pl.ds(i * chunk, chunk), :] = part[at, pl.ds(rows, chunk), :]


def feed_kernel(where, second, cot, w_gu, w_dn, act, grads, out):
    half = w_dn.shape[1]
    width = second.shape[1]
    total = None
    for p in range(2):
        gate_up = dot(second[...], w_gu[p])
        gate, upward = gate_up[:, :half], gate_up[:, half:]
        grad_act = dot_nt(cot[...], w_dn[p])
        square = gate * gate
        tanh = jnp.tanh(GELU_A * gate * (1.0 + GELU_B * square))
        cdf = 0.5 * (1.0 + tanh)
        unit = gate * cdf
        slope = cdf + 0.5 * gate * (1.0 - tanh * tanh) * (GELU_A * (1.0 + 3.0 * GELU_B * square))
        act[:, p * half : (p + 1) * half] = (unit * upward).astype(BF)
        grads[:, p * width : p * width + half] = (grad_act * upward * slope).astype(BF)
        grads[:, p * width + half : (p + 1) * width] = (grad_act * unit).astype(BF)
        part = dot_nt(grads[:, p * width : (p + 1) * width], w_gu[p])
        total = part if total is None else total + part
    out[...] = total.astype(out.dtype)


def down_kernel(where, a0, a1, a2, a3, w_dn, out):
    chip = where[1]
    half = w_dn.shape[1]
    for m, act in enumerate((a0, a1, a2, a3)):
        total = dot(act[:, :half], w_dn[0]) + dot(act[:, half:], w_dn[1])
        out[chip ^ m] = total.astype(BF)


def feed_weight_kernel(p, where, a0, a1, a2, a3, g0, g1, g2, g3, s0, s1, s2, s3, c0, c1, c2, c3, *rest):
    came, (out, acts, grads, seconds, cots) = rest[:-5], rest[-5:]
    chip = where[1]
    count, width = s0.shape
    half = width // 2
    for m, (a, g, s, c) in enumerate(
        ((a0, g0, s0, c0), (a1, g1, s1, c1), (a2, g2, s2, c2), (a3, g3, s3, c3))
    ):
        at = pl.ds(m * count, count)
        acts[at, :] = a[:, p * half : (p + 1) * half]
        grads[at, :] = g[:, p * width : (p + 1) * width]
        seconds[at, :] = s[...]
        cots[at, :] = c[...]
    nz, piece, _ = out.shape
    chunk = half // 3
    rows = piece - chunk

    def put(i, start, value):
        place = pl.ds(start, value.shape[0])
        if came:
            value = value + came[0][i, place, :].astype(F32)
        out[i, place, :] = value.astype(BF)

    total = dot_tn(seconds[...], grads[...])
    for i in range(nz):
        put(i, 0, total[i * rows : (i + 1) * rows])
    down = dot_tn(acts[...], cots[...])
    out[chip, pl.ds(rows, chunk), :] = jnp.zeros((chunk, width), BF)
    for i in range(3):
        to = i + (i >= chip).astype(jnp.int32)
        put(to, rows, down[i * chunk : (i + 1) * chunk])


def copy_kernel(where, a, out):
    out[...] = a[...]


def layer_out_kernel(where, residual, rest, out):
    total = residual[...] + rest[...].astype(F32)
    owned = out.shape[0]
    for i in range(out.shape[1]):
        out[:, i, :] = total[i * owned : (i + 1) * owned]


def second_back_kernel(where, residual, gain, cot, own, r1, r2, r3, grad_residual, low, grad_gain):
    grad = own[...] + r1[...].astype(F32) + r2[...].astype(F32) + r3[...].astype(F32)
    hat, inv = norm_parts(residual[...])
    pulled, grad_gain[...] = norm_pull(hat, inv, gain[...], grad)
    total = cot[...] + pulled
    grad_residual[...] = total
    low[...] = total.astype(BF)


def mix_back_kernel(where, ga, gb, w_rows, outer, conv, na, nb, mixed, other_mixed, grad_outer, o0, o1, o2, o3, p0, p1, p2, p3, grad_conv, whole):
    z, chip, core = where[0], where[1], where[2]
    count = ga.shape[0]
    half = outer.shape[1]
    for i, grad in enumerate((ga, gb)):
        at = pl.ds(i * count, count)
        grad_mixed = dot_nt(grad[...], w_rows[...])
        grad_outer[at, :] = (grad_mixed * conv[at, :].astype(F32)).astype(BF)
        grad_conv[at, :] = (grad_mixed * outer[at, :]).astype(BF)
    owned = o0.shape[0]
    for k, out in enumerate((o0, o1, o2, o3)):
        out[...] = grad_conv[rows_at((z + k) & 3, owned), :]
    total = dot_tn(na[...], grad_outer[pl.ds(0, count), :])
    total = total + dot_tn(nb[...], grad_outer[pl.ds(count, count), :])
    whole[:, :half] = total.astype(BF)
    first = jnp.where(core == 0, ga[:, :half], ga[:, half:])
    second = jnp.where(core == 0, gb[:, :half], gb[:, half:])
    mine = dot_tn(mixed[pl.ds(0, count), :], first) + dot_tn(mixed[pl.ds(count, count), :], second)
    theirs = dot_tn(other_mixed[pl.ds(count, count), :], first)
    theirs = theirs + dot_tn(other_mixed[pl.ds(0, count), :], second)
    whole[rows_at(core, half), half:] = mine.astype(BF)
    whole[rows_at(1 - core, half), half:] = theirs.astype(BF)
    write_pieces(whole, (p0, p1, p2, p3), chip)


def fold_back_kernel(where, g0, r1, r2, r3, table, flipped, spectrum, cond_spec, base, gain, taps, vals, o0, o1, o2, o3, f0, f1, f2, f3, grads, double, filters):
    z, short = where[0], where[3] == 1
    owned, half = g0.shape
    length = vals.shape[0]
    for k, piece in enumerate((g0, r1, r2, r3)):
        grads[rows_at((z - k) & 3, owned), :] = piece[...]
    gf = dot(table[...], grads[...])
    cspec = cond_spec[...]
    root = jnp.sqrt(cspec * cspec + 1.0)
    above = root - 1.0
    grad_base = gf * spectrum[...]
    double[:, :half] = (gf * (base[...] + gain[...] * above)).astype(BF)
    double[:, half:] = (grad_base * gain[...] * (cspec / root)).astype(BF)
    unfolded = dot(flipped[...], double[...])
    grad_cond = unfolded[:, half:]
    wide = vals[...].astype(F32)
    before, after = neighbours(wide, short, length)
    grad_before, grad_after = neighbours(grad_cond, short, length)
    grads[...] = (
        unfolded[:, :half]
        + taps[0:1, :] * grad_after
        + taps[1:2, :] * grad_cond
        + taps[2:3, :] * grad_before
    ).astype(BF)
    for k, out in enumerate((o0, o1, o2, o3)):
        out[...] = grads[rows_at((z + k) & 3, owned), :]
    is_short = jnp.where(short, 1.0, 0.0)
    filters[pl.ds(0, length), :] = (grad_base * (1.0 - is_short)).astype(BF)
    folded = grad_base[:SHORT_LENGTH]
    for i in range(1, length // SHORT_LENGTH):
        folded = folded + grad_base[i * SHORT_LENGTH : (i + 1) * SHORT_LENGTH]
    filters[pl.ds(length, SHORT_LENGTH), :] = (folded * is_short).astype(BF)
    rest = filters.shape[0] - length - SHORT_LENGTH
    small = [
        jnp.sum(grad_base * above, axis=0, keepdims=True),
        jnp.sum(grad_cond * before, axis=0, keepdims=True),
        jnp.sum(grad_cond * wide, axis=0, keepdims=True),
        jnp.sum(grad_cond * after, axis=0, keepdims=True),
        jnp.zeros((rest - 4, half), F32),
    ]
    filters[pl.ds(length + SHORT_LENGTH, rest), :] = jnp.concatenate(small, axis=0).astype(BF)
    size = f0.shape[0]
    for k, out in enumerate((f0, f1, f2, f3)):
        start = ((z + k) & 3) * 2
        out[:, :half] = filters[rows_at(start, size), :]
        out[:, half:] = filters[rows_at(start + 1, size), :]


def write_pieces(whole, outs, chip):
    rows = whole.shape[0] // 4
    quarter = rows // 4
    for m, out in enumerate(outs):
        for i in range(4):
            out[pl.ds(i * quarter, quarter), :] = whole[rows_at(i * 4 + (chip ^ m), quarter), :]


def late_kernel(where, marks_own, marks_other, g0, r1, r2, r3, left, right, na, nb, late, p0, p1, p2, p3, grads, whole):
    z, chip = where[0], where[1]
    owned, half = g0.shape
    for k, piece in enumerate((g0, r1, r2, r3)):
        grads[rows_at((z - k) & 3, owned), :] = piece[...].astype(F32)
    count = na.shape[0]
    place = lax.broadcasted_iota(jnp.int32, (owned, half), 0)
    for i, marks in enumerate((marks_own, marks_other)):
        for s in range(count // owned):
            at = pl.ds(i * count + s * owned, owned)
            grad = jnp.where(place < valid_rows(marks, s, z, owned), grads[at, :], 0.0)
            late[at, :half] = (grad * right[at, :]).astype(BF)
            late[at, half:] = (grad * left[at, :]).astype(BF)
    total = dot_tn(na[...], late[pl.ds(0, count), :]) + dot_tn(nb[...], late[pl.ds(count, count), :])
    whole[...] = total.astype(BF)
    write_pieces(whole, (p0, p1, p2, p3), chip)


def first_grad_kernel(where, grad_outer, late, w, own, other):
    half = grad_outer.shape[1]
    count = own.shape[0]
    for i, out in enumerate((own, other)):
        at = pl.ds(i * count, count)
        total = dot_nt(grad_outer[at, :], w[:, :half]) + dot_nt(late[at, :], w[:, half:])
        out[...] = total.astype(out.dtype)


def first_back_kernel(where, x, gain, grad_residual, own, came, grad_inputs, grad_gain):
    grad = own[...] + came[...].astype(F32)
    hat, inv = norm_parts(x[...])
    pulled, grad_gain[...] = norm_pull(hat, inv, gain[...], grad)
    total = grad_residual[...] + pulled
    owned = grad_inputs.shape[0]
    for i in range(grad_inputs.shape[1]):
        grad_inputs[:, i, :] = total[i * owned : (i + 1) * owned]


def added(pieces):
    total = pieces[0][...].astype(F32)
    for piece in pieces[1:]:
        total = total + piece[...].astype(F32)
    return total


def ridden(row, width):
    first = lax.broadcasted_iota(jnp.int32, (RIDE, width), 0) == 0
    return jnp.where(first, jnp.broadcast_to(row, (RIDE, width)), 0.0).astype(BF)


def early_share_kernel(where, p0, r1, r2, r3, ride, f0, f1, f2, f3, o0, o1, o2, o3, total):
    z = where[0]
    total[...] = added((p0, r1, r2, r3)).astype(BF)
    quarter = p0.shape[0] // 4
    extra = ridden(ride[...], p0.shape[1])
    for k, (filt, out) in enumerate(((f0, o0), (f1, o1), (f2, o2), (f3, o3))):
        out[pl.ds(0, quarter), :] = total[rows_at((z + k) & 3, quarter), :]
        out[pl.ds(quarter, RIDE), :] = extra
        out[pl.ds(quarter + RIDE, filt.shape[0]), :] = filt[...]


def late_share_kernel(where, p0, r1, r2, r3, ride, e0, e1, e2, e3, o0, o1, o2, o3, early, total):
    z = where[0]
    total[...] = added((p0, r1, r2, r3)).astype(BF)
    quarter = p0.shape[0] // 4
    extra = ridden(ride[...], p0.shape[1])
    for k, out in enumerate((o0, o1, o2, o3)):
        out[pl.ds(0, quarter), :] = total[rows_at((z + k) & 3, quarter), :]
        out[pl.ds(quarter, RIDE), :] = extra
    early[...] = added((e0, e1, e2, e3)).astype(BF)


def in_order(where, pieces, out, start):
    chip = where[1]
    quarter = pieces[0].shape[0] - RIDE
    width = pieces[0].shape[1]
    riding = jnp.zeros((1, width), F32)
    for m, piece in enumerate(pieces):
        out[rows_at(start // quarter + (chip ^ m), quarter), :] = piece[pl.ds(0, quarter), :]
        riding = riding + piece[pl.ds(quarter, RIDE), :].astype(F32)[0:1]
    out[pl.ds(start + 4 * quarter, RIDE), :] = ridden(riding, width)


def late_sum_kernel(where, s0, r1, r2, r3, e0, e1, e2, e3, piece, filt, early):
    piece[...] = added((s0, r1, r2, r3)).astype(BF)
    size = s0.shape[0]
    filt[...] = added([e.at[pl.ds(size, filt.shape[0])] for e in (e0, e1, e2, e3)]).astype(BF)
    in_order(where, [e.at[pl.ds(0, size)] for e in (e0, e1, e2, e3)], early, 0)


def gather_kernel(where, s0, r1, r2, r3, f0, f1, f2, f3, early, out):
    z = where[0]
    in_order(where, (s0, r1, r2, r3), out, 0)
    size = early.shape[0]
    out[pl.ds(size, size), :] = early[...]
    step = f0.shape[0]
    for k, piece in enumerate((f0, f1, f2, f3)):
        out[pl.ds(pl.multiple_of(2 * size + ((z - k) & 3) * step, 16), step), :] = piece[...]


def feed_order_kernel(where, shares, gate_up, down):
    z = where[0]
    rows = gate_up.shape[0]
    chunk = shares.shape[1] - rows
    per_z = 6 * chunk
    for side in range(2):
        for zz in range(4):
            for c in range(6):
                mm = c if c < 2 * zz else c + 2
                at = (side * 3 + zz - (zz > mm // 2)) * chunk
                to = side * 4 * per_z + zz * per_z + c * chunk
                gate_up[:, to : to + chunk] = shares[mm, :rows, at : at + chunk].astype(F32)
    for c in range(6):
        mm = c + 2 * (c >= 2 * z).astype(jnp.int32)
        down[pl.ds(c * chunk, chunk), :] = shares[mm, pl.ds(rows, chunk), :].astype(F32)


def last_kernel(where, own, other, w_in, w_out, long, short, gain, taps, norm_one, norm_two):
    core = where[2]
    rows = w_in.shape[0]
    width = w_out.shape[1]
    half = width // 2
    size = rows + RIDE

    def write(out, to, a, b):
        a, b = a.astype(F32), b.astype(F32)
        out[:, to : to + half] = jnp.where(core == 0, a, b)
        out[:, to + half : to + width] = jnp.where(core == 0, b, a)

    for start, at, to, out in (
        (size, 0, 0, w_in),
        (0, 0, width, w_in),
        (0, half, 2 * width, w_in),
        (size, half, 0, w_out),
    ):
        place = (pl.ds(start, rows), slice(at, at + half))
        write(out, to, own[place], other[place])
    for start, out in ((0, norm_one), (size, norm_two)):
        place = pl.ds(start + rows, RIDE)
        out[...] = (own[place, :].astype(F32) + other[place, :].astype(F32))[0:1]
    fold = (own.shape[0] - 2 * size) // 4
    length, part = long.shape[0], short.shape[0]

    def filter_rows(ref, start, count):
        got = []
        while count:
            block, inside = start // fold, start % fold
            step = min(count, fold - inside)
            place = pl.ds(2 * size + block // 2 * fold + inside, step)
            got.append(ref[place, half:] if block % 2 else ref[place, :half])
            start, count = start + step, count - step
        return jnp.concatenate(got, axis=0) if len(got) > 1 else got[0]

    for i in range(0, length, SHORT_LENGTH):
        a, b = filter_rows(own, i, SHORT_LENGTH), filter_rows(other, i, SHORT_LENGTH)
        write(long.at[pl.ds(i, SHORT_LENGTH)], 0, a, b)
    write(short, 0, filter_rows(own, length, part), filter_rows(other, length, part))
    a, b = filter_rows(own, length + part, 16), filter_rows(other, length + part, 16)
    write(gain, 0, a[0:1], b[0:1])
    write(taps, 0, a[1:4], b[1:4])


def body(
    inputs,
    cotangent,
    group,
    lens,
    norm1_gain,
    w_in,
    kernel_long,
    kernel_short,
    conv_weight,
    cond_gain,
    w_out,
    norm2_gain,
    w_gate_up,
    w_down,
):
    nz = lax.axis_size("freq")
    ndp = lax.axis_size("dp")
    z = lax.axis_index("freq")
    d = lax.axis_index("dp")
    core = d % 2
    chip = (d // 2) % 4
    member = d % GROUP
    owned, slots, width = inputs.shape
    half = width // 2
    length = owned * nz
    tokens = owned * slots
    rows = w_in.shape[0]
    quarter = rows // 4
    others = ndp // GROUP
    blocks = [[g * GROUP + i for i in range(GROUP)] for g in range(others)]
    same_core = [[g * GROUP + 2 * i + c for i in range(4)] for g in range(others) for c in range(2)]
    across = [[i + GROUP * g for g in range(others)] for i in range(GROUP)]

    def core_swap(x):
        return lax.ppermute(x, "dp", [(i, i ^ 1) for i in range(ndp)])

    def chip_swap(x, m):
        return lax.ppermute(x, "dp", [(i, i ^ (2 * m)) for i in range(ndp)])

    def z_rot(x, k):
        return lax.ppermute(x, "freq", [(i, (i + k) % nz) for i in range(nz)])

    def mine(x, axis=-1):
        low, high = jnp.split(x, 2, axis=axis)
        return jnp.where(core == 0, low, high)

    def theirs(x, axis=-1):
        low, high = jnp.split(x, 2, axis=axis)
        return jnp.where(core == 0, high, low)

    def joined(own, other, axis=-1):
        return jnp.where(
            core == 0,
            jnp.concatenate([own, other], axis=axis),
            jnp.concatenate([other, own], axis=axis),
        )

    def from_z(rel):
        stacked = jnp.stack(rel)
        return jnp.concatenate([pick(stacked, (z - i) % nz) for i in range(nz)], axis=0)

    def z_swap(pieces):
        return [pieces[0]] + [z_rot(pieces[k], k) for k in range(1, nz)]

    def over_groups(x):
        if others > 1:
            return lax.psum(x, "dp", axis_index_groups=across)
        return x

    def in_cols(x):
        return jnp.concatenate([mine(x[:, i * width : (i + 1) * width]) for i in range(3)], axis=1)

    where = jnp.stack([z, chip, core, z]).astype(jnp.int32)
    start = chip * quarter
    part = kernel_short.shape[0]
    long_half, short_half = mine(kernel_long), mine(kernel_short)
    filt_near = jnp.concatenate(
        [
            lax.dynamic_slice_in_dim(long_half, chip * (owned // 4), owned // 4, axis=0),
            lax.dynamic_slice_in_dim(short_half, chip * (part // 4), part // 4, axis=0),
            jnp.zeros((quarter - (owned + part) // 4, half), BF),
        ],
        axis=0,
    )
    near = jnp.concatenate(
        [
            in_cols(lax.dynamic_slice_in_dim(w_in, start, quarter, axis=0)),
            filt_near,
            mine(lax.dynamic_slice_in_dim(w_out, start, quarter, axis=0)),
        ],
        axis=1,
    )
    both_near = [z_rot(near, k) for k in range(1, nz)]

    hidden = w_down.shape[0] * nz
    per_z = w_down.shape[0]
    chunk = per_z // 6
    taken = rows + chunk

    x_own = jnp.swapaxes(inputs, 0, 1).reshape(tokens, width)
    cot_own = jnp.swapaxes(cotangent, 0, 1).reshape(tokens, width)

    marks = jnp.concatenate([group[:, None], lens], axis=1).astype(jnp.int32)
    marks_other = core_swap(marks)
    group_all = jnp.concatenate([marks[:, 0], marks_other[:, 0]])
    slot_group = pick(group_all, z)
    spot = jnp.stack([z, chip, core, slot_group]).astype(jnp.int32)

    repeat = length // SHORT_LENGTH
    long_table = cosine_table(length)
    short_table = np.kron(np.eye(repeat), cosine_table(SHORT_LENGTH)).astype(np.float32)
    is_short = slot_group == 1
    table = jnp.where(is_short, jnp.asarray(short_table, BF), jnp.asarray(long_table, BF))
    flipped = jnp.where(is_short, jnp.asarray(short_table.T, BF), jnp.asarray(long_table.T, BF))
    gain_half = mine(cond_gain)[None]
    taps = mine(conv_weight)
    gain_one = norm1_gain[None]
    gain_two = norm2_gain[None]

    hat_one, _ = norm_parts(x_own)
    normed = (hat_one * gain_one).astype(BF)
    normed_other = core_swap(normed)
    piece = ((owned, half), BF)
    many = 2 * tokens
    out_local = mine(w_out)
    in_stack, out_near = run(
        hand_on_kernel,
        "hand_on",
        [((3, quarter, 4 * half), BF), ((3, quarter, half), BF)],
        where,
        both_near,
    )
    mlp_piece = run(
        feed_pick_kernel,
        "feed_pick",
        [((taken, width), BF)],
        where,
        [w_gate_up, w_down],
        after=(in_stack,),
    )[0]
    mlp_got = lax.all_gather(mlp_piece, "freq", axis=0)
    in_far = [chip_swap(in_stack, m) for m in (1, 2, 3)]
    w_in_half, outer, left, right, s0, s1, s2, s3, out_stack, cot_low, long, short = run(
        project_kernel,
        "project",
        [((width, 3 * half), BF)]
        + [((many, half), F32)] * 3
        + [piece] * 4
        + [((3, quarter, half), BF), ((tokens, width), BF)]
        + [((length, half), F32), ((part * nz, half), F32)],
        where,
        [
            marks,
            marks_other,
            normed,
            normed_other,
            in_cols(w_in),
            *both_near,
            *in_far,
            out_near,
            cot_own,
            long_half,
            short_half,
        ],
        [pltpu.VMEM((many, half), BF)],
    )
    came = z_swap([s0, s1, s2, s3])
    out_far = [chip_swap(out_stack, m) for m in (1, 2, 3)]
    cots = [cot_low] + [chip_swap(cot_low, m) for m in (1, 2)]
    vals, spectrum, cond_spec, base, *sends = run(
        fold_kernel,
        "fold",
        [((length, half), BF)] + [((length, half), F32)] * 3 + [piece] * 4,
        spot,
        [*came, long, short, table, flipped, gain_half, taps],
        [
            pltpu.VMEM((length, 3 * half), BF),
            pltpu.VMEM((length, half), BF),
            pltpu.VMEM((length, half), BF),
        ],
        after=(*cots[1:], *out_far),
    )
    came = z_swap(sends)
    cot_far = run(copy_kernel, "cot_far", [(cot_low.shape, BF)], where, [cot_low], after=(vals,))[0]
    cots.append(chip_swap(cot_far, 3))
    w_keep, w_send, mlp_all = run(
        out_rows_kernel,
        "out_rows",
        [((half, half), BF)] * 2 + [((nz, taken, width), BF)],
        where,
        [mlp_got, out_local, out_near, *out_far],
        [pltpu.VMEM((width, half), BF)],
        after=(vals,),
    )
    w_gu, w_dn = run(
        feed_place_kernel,
        "feed_place",
        [((2, width, width), BF), ((2, half, width), BF)],
        where,
        [mlp_all, core_swap(mlp_all)],
    )
    conv, mixed, part_own, part_other, w_out_rows = run(
        mix_kernel,
        "mix",
        [((many, half), BF)] * 2
        + [((tokens, width), F32), ((tokens, width), BF), ((half, width), BF)],
        where,
        [outer, *came, w_keep, core_swap(w_send)],
        after=(w_gu, cots[3]),
    )
    residual, normed_two = run(
        second_kernel,
        "second_norm",
        [((tokens, width), F32), ((tokens, width), BF)],
        where,
        [x_own, part_own, core_swap(part_other), gain_two],
    )

    arrived = [normed_two] + [chip_swap(normed_two, m) for m in (1, 2, 3)]
    acts, grads_gu, sums = [], [], []
    order = ()
    for m in range(4):
        act, grad_gu, part = run(
            feed_kernel,
            "feed",
            [((tokens, width), BF), ((tokens, 2 * width), BF), ((tokens, width), BF if m else F32)],
            where,
            [arrived[m], cots[m], w_gu, w_dn],
            after=order,
        )
        order = (act,)
        acts.append(act)
        grads_gu.append(grad_gu)
        sums.append(part)
    backs = [chip_swap(sums[m], m) for m in (1, 2, 3)]
    partial_out = run(
        down_kernel,
        "down",
        [((4, tokens, width), BF)],
        where,
        [*acts, w_dn],
    )[0]
    down_sum = lax.psum_scatter(
        partial_out, "dp", scatter_dimension=0, axis_index_groups=same_core, tiled=False
    )
    grad_residual, grad_mix, grad_gain_two = run(
        second_back_kernel,
        "second_norm_back",
        [((tokens, width), F32), ((tokens, width), BF), ((1, width), F32)],
        where,
        [residual, gain_two, cot_own, sums[0], *backs],
    )
    grad_mix_other = core_swap(grad_mix)
    grad_outer, s0, s1, s2, s3, *early_parts = run(
        mix_back_kernel,
        "mix_back",
        [((many, half), BF)] + [piece] * 4 + [((rows, width), BF)] * 4,
        where,
        [
            grad_mix,
            grad_mix_other,
            w_out_rows,
            outer,
            conv,
            normed,
            normed_other,
            mixed,
            core_swap(mixed),
        ],
        [pltpu.VMEM((many, half), BF), pltpu.VMEM((width, width), BF)],
    )
    came = z_swap([s0, s1, s2, s3])

    def near_by(piece):
        return [piece] + [chip_swap(piece, m) for m in (1, 2, 3)]

    def exchanged(parts):
        return [parts[0]] + [chip_swap(parts[m], m) for m in (1, 2, 3)]

    early_all = exchanged(early_parts)

    def feed_weights(p, came, after):
        return run(
            functools.partial(feed_weight_kernel, p),
            "feed_weights",
            [((nz, taken, width), BF)],
            where,
            [*acts, *grads_gu, *arrived, *cots, *came],
            [
                pltpu.VMEM((4 * tokens, half), BF),
                pltpu.VMEM((4 * tokens, width), BF),
                pltpu.VMEM((4 * tokens, width), BF),
                pltpu.VMEM((4 * tokens, width), BF),
            ],
            after=after,
        )[0]

    mlp_send = feed_weights(1, [], (grad_outer,))
    mlp_grads = feed_weights(0, [core_swap(mlp_send)], ())
    mlp_share = lax.psum_scatter(mlp_grads, "freq", scatter_dimension=0, tiled=False)

    fill = -(length + SHORT_LENGTH + 4) % (nz * 32)
    size = (length + SHORT_LENGTH + 4 + fill) // nz // 2
    *sends, f0, f1, f2, f3 = run(
        fold_back_kernel,
        "fold_back",
        [piece] * 4 + [((size, width), BF)] * 4,
        spot,
        [*came, table, flipped, spectrum, cond_spec, base, gain_half, taps, vals],
        [
            pltpu.VMEM((length, half), BF),
            pltpu.VMEM((length, 2 * half), BF),
            pltpu.VMEM((2 * size * nz, half), BF),
        ],
        after=early_all[1:],
    )
    came = z_swap(sends)
    pack = quarter + RIDE + size
    early_sends = run(
        early_share_kernel,
        "early_share",
        [((pack, width), BF)] * 4,
        where,
        [*early_all, grad_gain_two, f0, f1, f2, f3],
        [pltpu.VMEM((rows, width), BF)],
    )
    late, *late_parts = run(
        late_kernel,
        "late_weights",
        [((many, width), BF)] + [((rows, width), BF)] * 4,
        where,
        [marks, marks_other, *came, left, right, normed, normed_other],
        [pltpu.VMEM((many, half), F32), pltpu.VMEM((width, width), BF)],
        after=(early_sends[0],),
    )
    late_all = exchanged(late_parts)
    own, other = run(
        first_grad_kernel,
        "first_grad",
        [((tokens, width), F32), ((tokens, width), BF)],
        where,
        [grad_outer, late, w_in_half],
    )
    layer_out = run(
        layer_out_kernel,
        "layer_out",
        [((owned, slots, width), F32)],
        where,
        [residual, down_sum],
        after=(own,),
    )[0]
    grad_inputs, grad_gain_one = run(
        first_back_kernel,
        "first_norm_back",
        [((owned, slots, width), F32), ((1, width), F32)],
        where,
        [x_own, gain_one, grad_residual, own, core_swap(other)],
        after=(layer_out,),
    )
    mlp_sum = lax.all_gather(over_groups(mlp_share), "dp", axis=0, axis_index_groups=blocks)
    *late_sends, early = run(
        late_share_kernel,
        "late_share",
        [((quarter + RIDE, width), BF)] * 4 + [((pack, width), BF)],
        where,
        [*late_all, grad_gain_one, *z_swap(early_sends)],
        [pltpu.VMEM((rows, width), BF)],
    )
    late_piece, filt, early = run(
        late_sum_kernel,
        "late_sum",
        [((quarter + RIDE, width), BF), ((size, width), BF), ((rows + RIDE, width), BF)],
        where,
        [*z_swap(late_sends), *near_by(over_groups(early))],
    )
    gathered = run(
        gather_kernel,
        "gather",
        [((2 * (rows + RIDE) + nz * size, width), BF)],
        where,
        [*near_by(over_groups(late_piece)), *z_swap([filt] * nz), early],
    )[0]
    grad_w_gate_up, grad_w_down = run(
        feed_order_kernel,
        "feed_order",
        [((rows, 2 * hidden), F32), ((per_z, width), F32)],
        where,
        [mlp_sum],
    )
    grad_w_in, grad_w_out, grad_long, grad_short, grad_cond, grad_taps, grad_one, grad_two = run(
        last_kernel,
        "last",
        [
            ((rows, 3 * width), F32),
            ((rows, width), F32),
            ((length, width), F32),
            ((SHORT_LENGTH, width), F32),
            ((1, width), F32),
            ((3, width), F32),
            ((1, width), F32),
            ((1, width), F32),
        ],
        where,
        [gathered, core_swap(gathered)],
    )

    return (
        layer_out,
        grad_inputs,
        grad_one.reshape(width),
        grad_w_in,
        grad_long,
        grad_short,
        grad_taps,
        grad_cond.reshape(width),
        grad_w_out,
        grad_two.reshape(width),
        grad_w_gate_up,
        grad_w_down,
    )


def solution(mesh):
    return jax.shard_map(
        body,
        mesh=mesh,
        in_specs=(
            P("freq", "dp", None),
            P("freq", "dp", None),
            P("dp"),
            P("dp", None),
            P(),
            P("freq", None),
            P("freq", None),
            P("freq", None),
            P(),
            P(),
            P("freq", None),
            P(),
            P("freq", None),
            P("freq", None),
        ),
        out_specs=(
            P("freq", "dp", None),
            P("freq", "dp", None),
            P(),
            P("freq", None),
            P(),
            P(),
            P(),
            P(),
            P("freq", None),
            P(),
            P("freq", None),
            P("freq", None),
        ),
        check_vma=False,
    )
```

```python
import math

import jax
import jax.numpy as jnp
import numpy as np
from jax import lax
from jax.experimental import pallas as pl
from jax.experimental.pallas import tpu as pltpu
from jax.sharding import PartitionSpec as P

SHORT_LENGTH = 128
EPSILON = 1e-05
BF = jnp.bfloat16
F32 = jnp.float32
GROUP = 8
RIDE = 16
COSTS = {
    "near": 3,
    "first_norm": 3,
    "hand_on": 15,
    "project": 25,
    "fold": 20,
    "out_rows": 2,
    "mix": 15,
    "second_norm": 4,
    "feed": 5,
    "feed_place": 3,
    "down": 4,
    "feed_weights": 8,
    "second_norm_back": 3,
    "mix_back": 3,
    "fold_back": 50,
    "early_share": 1,
    "late_weights": 45,
    "first_grad": 3,
    "first_norm_back": 3,
    "late_share": 55,
    "late_sum": 50,
    "gather": 45,
    "last": 6,
    "feed_order": 4,
}
VMEM, HBM = pltpu.VMEM, pltpu.HBM
GELU_A = math.sqrt(2.0 / math.pi)
GELU_B = 0.044715


def cosine_table(length):
    freq = np.arange(length)[:, None]
    posit = np.arange(length)[None, :]
    phase = (2 * posit + 1) * freq % (4 * length)
    weight = np.where(freq == 0, 1.0, 2.0) / length
    return (np.cos(phase * (math.pi / (2 * length))) * np.sqrt(weight)).astype(np.float32)


def dot(a, b):
    return lax.dot_general(a, b, (((1,), (0,)), ((), ())), preferred_element_type=F32)


def dot_nt(a, b):
    return lax.dot_general(a, b, (((1,), (1,)), ((), ())), preferred_element_type=F32)


def dot_tn(a, b):
    return lax.dot_general(a, b, (((0,), (0,)), ((), ())), preferred_element_type=F32)


def norm_parts(values):
    center = values - jnp.mean(values, axis=-1, keepdims=True)
    spread = jnp.mean(center * center, axis=-1, keepdims=True)
    inv = lax.rsqrt(spread + EPSILON)
    return center * inv, inv


def norm_pull(hat, inv, gain, grad):
    scaled = grad * gain
    mean_one = jnp.mean(scaled, axis=-1, keepdims=True)
    mean_two = jnp.mean(scaled * hat, axis=-1, keepdims=True)
    return inv * (scaled - mean_one - hat * mean_two), jnp.sum(grad * hat, axis=0, keepdims=True)


def pick(stacked, index):
    return lax.dynamic_index_in_dim(stacked, index, axis=0, keepdims=False)


class Far:
    def __init__(self, array, start=None, size=None):
        self.array = pltpu.with_memory_space_constraint(array, pltpu.HBM)
        self.start = start
        self.shape = array.shape if start is None else (size, *array.shape[1:])

    def source(self, ref, where):
        return ref if self.start is None else ref.at[rows_at(self.start(where), self.shape[0])]


class Held:
    def __init__(self, array):
        self.array = pltpu.with_memory_space_constraint(array, pltpu.VMEM)


class Fetched:
    def __init__(self, ref, copy):
        self.ref, self.copy, self.shape = ref, copy, ref.shape

    def ready(self):
        if self.copy is not None:
            self.copy.wait()
            self.copy = None
        return self.ref

    def __getitem__(self, place):
        return self.ready()[place]

    @property
    def at(self):
        return self.ready().at


class Kept:
    def __init__(self, ref, copy):
        self.ref, self.copy, self.shape, self.dtype = ref, copy, ref.shape, ref.dtype
        self.started = False

    def __getitem__(self, place):
        return self.ref[place]

    def __setitem__(self, place, value):
        self.ref[place] = value

    def flush(self):
        if not self.started:
            self.copy.start()
            self.started = True


def run(kernel, name, outs, where, ins, scratch=(), after=()):
    arrays = [x.array if isinstance(x, (Far, Held)) else x for x in ins]
    far_in = [isinstance(x, Far) for x in ins]
    far_out = [o[2:] == (HBM,) for o in outs]
    shapes = [o[2](*o[:2]) if len(o) > 2 else jax.ShapeDtypeStruct(*o) for o in outs]
    outs = [o[:2] for o in outs]
    n_in, n_after, n_out, n_scratch = len(ins), len(after), len(outs), len(scratch)
    buffers = [pltpu.VMEM(x.shape, x.array.dtype) for x in ins if isinstance(x, Far)]
    buffers += [pltpu.VMEM(s, t) for (s, t), far in zip(outs, far_out) if far]

    def wrapped(*refs):
        where_ref, in_refs = refs[0], list(refs[1 : 1 + n_in])
        rest = list(refs[1 + n_in + n_after :])
        out_refs, rest = rest[:n_out], rest[n_out:]
        own, held = rest[:n_scratch], rest[n_scratch:]
        if not buffers:
            kernel(where_ref, *in_refs, *out_refs, *own)
            return
        held, sems = held[:-1], held[-1]
        number = 0
        for i in range(n_in):
            if far_in[i]:
                source = ins[i].source(in_refs[i], where_ref)
                copy = pltpu.make_async_copy(source, held[number], sems.at[number])
                copy.start()
                in_refs[i] = Fetched(held[number], copy)
                number += 1
        kept = []
        for i in range(n_out):
            if far_out[i]:
                copy = pltpu.make_async_copy(held[number], out_refs[i], sems.at[number])
                out_refs[i] = Kept(held[number], copy)
                kept.append(out_refs[i])
                number += 1
        kernel(where_ref, *in_refs, *out_refs, *own)
        for ref in kept:
            ref.flush()
        for ref in kept:
            ref.copy.wait()
        for ref in in_refs:
            if isinstance(ref, Fetched):
                ref.ready()

    size = sum(x.size * x.dtype.itemsize for x in arrays)
    size += sum(math.prod(s) * jnp.dtype(t).itemsize for s, t in outs)
    far = pl.BlockSpec(memory_space=pltpu.HBM)
    near = pl.BlockSpec(memory_space=pltpu.VMEM)
    small = pl.BlockSpec(memory_space=pltpu.SMEM)
    return pl.pallas_call(
        wrapped,
        out_shape=shapes,
        in_specs=[small]
        + [far if f else small if x.dtype == jnp.int32 else near for x, f in zip(arrays, far_in)]
        + [pl.BlockSpec(memory_space=pl.ANY)] * n_after,
        out_specs=[far if f else near for f in far_out],
        scratch_shapes=list(scratch)
        + buffers
        + ([pltpu.SemaphoreType.DMA((len(buffers),))] if buffers else []),
        compiler_params=pltpu.CompilerParams(vmem_limit_bytes=24 * 2**20),
        cost_estimate=pl.CostEstimate(
            flops=int(COSTS.get(name, 1) * 1.15e9), bytes_accessed=int(size), transcendentals=0
        ),
        name=name,
    )(where, *arrays, *after)


def rows_at(index, size):
    return pl.ds(pl.multiple_of(index * size, 16), size)


def first_norm_kernel(where, x, gain, normed):
    owned = x.shape[0]
    for s in range(x.shape[1]):
        hat, _ = norm_parts(x[:, s, :])
        normed[pl.ds(s * owned, owned), :] = (hat * gain[...]).astype(BF)


def low_kernel(where, x, out):
    owned = x.shape[0]
    for s in range(x.shape[1]):
        out[pl.ds(s * owned, owned), :] = x[:, s, :].astype(BF)


def near_kernel(where, w_in, w_out, near):
    core = where[2]
    half = w_out.shape[1] // 2
    for i, ref in enumerate((w_in, w_in, w_in, w_out)):
        at = i % 3 * 2 * half
        near[:, i * half : (i + 1) * half] = jnp.where(
            core == 0, ref[:, at : at + half], ref[:, at + half : at + 2 * half]
        )


def local_kernel(where, w_in, w_out, long, short, local, out_local, long_half, short_half):
    core = where[2]
    width = w_out.shape[1]
    half = width // 2

    def mine(x, start):
        return jnp.where(core == 0, x[:, start : start + half], x[:, start + half : start + width])

    for i in range(3):
        local[:, i * half : (i + 1) * half] = mine(w_in, i * width)
    out_local[...] = mine(w_out, 0)
    long_half[...] = mine(long, 0)
    short_half[...] = mine(short, 0)


def hand_on_kernel(where, n1, n2, n3, in_stack, out_stack):
    wide = in_stack.shape[2]
    for k, near in enumerate((n1, n2, n3)):
        in_stack[k] = near[:, :wide]
        out_stack[k] = near[:, wide:]


def feed_pick_kernel(where, w_gate_up, w_down, mlp):
    z, chip, core = where[0], where[1], where[2]
    rows = w_gate_up.shape[0]
    hidden = w_gate_up.shape[1] // 2
    per_z = w_down.shape[0]
    chunk = per_z // 6
    member = 2 * chip + core
    for side in range(2):
        for i in range(3):
            zz = i + (i >= chip).astype(jnp.int32)
            c = jnp.where(member < 2 * zz, member, member - 2)
            start = pl.multiple_of(side * hidden + zz * per_z + c * chunk, 128)
            to = (side * 3 + i) * chunk
            mlp[pl.ds(0, rows), to : to + chunk] = w_gate_up[:, pl.ds(start, chunk)]
    c = jnp.clip(jnp.where(member < 2 * z, member, member - 2), 0, 5)
    mlp[pl.ds(rows, chunk), :] = w_down[rows_at(c, chunk), :]


def valid_rows(marks, s, z, owned):
    total = marks[s, 1] + marks[s, 2] + marks[s, 3] + marks[s, 4]
    return jnp.where(marks[s, 0] == 1, marks[s, 1 + z], total - owned * z)


def split_channels(whole, packs):
    count, owned, lanes = packs.shape
    part = lanes // count
    for there in range(count):
        for s in range(count):
            packs[there, :, s * part : (s + 1) * part] = whole[
                s * owned : (s + 1) * owned, there * part : (there + 1) * part
            ]


def join_channels(z, pieces, packs, whole):
    count, owned, lanes = packs.shape
    part = lanes // count
    for k, piece in enumerate(pieces):
        packs[(z - k) & 3] = piece[...]
    for there in range(count):
        for s in range(count):
            whole[s * owned : (s + 1) * owned, there * part : (there + 1) * part] = packs[
                there, :, s * part : (s + 1) * part
            ]


def project_kernel(where, marks_own, marks_other, na, nb, local, n1, n2, n3, c1, c2, c3, long_in, short_in, v0, v1, v2, v3, w, outer, left, right, vals, packs, folds):
    z, chip = where[0], where[1]
    rows = local.shape[0]
    quarter = rows // 4
    half = outer.shape[1]
    wide = 3 * half
    w[rows_at(z, rows), :] = local[...]
    for k, near in ((1, n1), (2, n2), (3, n3)):
        base = ((z - k) & 3) * 4
        w[rows_at(base + chip, quarter), :] = near[:, :wide]
        for m, far in ((1, c1), (2, c2), (3, c3)):
            w[rows_at(base + (chip ^ m), quarter), :] = far[k - 1]
    w.flush()
    owned = packs.shape[1]
    count = na.shape[0]
    place = lax.broadcasted_iota(jnp.int32, (owned, half), 0)
    for i, (tokens, marks) in enumerate(((na, marks_own), (nb, marks_other))):
        at = pl.ds(i * count, count)
        full = dot(tokens[...], w[...])
        a, b, c = full[:, :half], full[:, half : 2 * half], full[:, 2 * half :]
        outer[at, :] = a
        left[at, :] = b.astype(BF)
        right[at, :] = c.astype(BF)
        for s in range(count // owned):
            valid = valid_rows(marks, s, z, owned)
            low = slice(s * owned, (s + 1) * owned)
            vals[pl.ds(i * count + s * owned, owned), :] = jnp.where(
                place < valid, b[low] * c[low], 0.0
            ).astype(BF)
    for ref in (outer, left, right):
        ref.flush()
    split_channels(vals, packs)
    part = half // 4
    block = (long_in.shape[0] + short_in.shape[0]) // 4
    folds[...] = jnp.zeros(folds.shape, F32)
    for there in range(4):
        lanes = slice(there * part, (there + 1) * part)
        both = jnp.concatenate([long_in[:, lanes], short_in[:, lanes]], axis=0).astype(F32)
        for g in range(4):
            folds[there, pl.ds(0, block), g * part : (g + 1) * part] = both[g * block : (g + 1) * block]
    for k, out in enumerate((v0, v1, v2, v3)):
        out[pl.ds(0, owned), :] = packs[(z + k) & 3]
        rest = out.shape[0] - owned
        out[pl.ds(owned, rest), :] = folds[(z + k) & 3].astype(BF)


def short_lanes(marks_own, marks_other, shape):
    part = shape[1] // 4
    slot = lax.broadcasted_iota(jnp.int32, shape, 1) // part
    groups = [marks_own[0, 0], marks_own[1, 0], marks_other[0, 0], marks_other[1, 0]]
    return sum(jnp.where(slot == s, group, 0) for s, group in enumerate(groups)) == 1


def neighbours(x, short):
    length = x.shape[0]
    place = lax.broadcasted_iota(jnp.int32, x.shape, 0)
    starts = (place == 0) | (short & (place % SHORT_LENGTH == 0))
    ends = (place == length - 1) | (short & (place % SHORT_LENGTH == SHORT_LENGTH - 1))
    earlier = jnp.where(starts, 0.0, pltpu.roll(x, 1, 0))
    later = jnp.where(ends, 0.0, pltpu.roll(x, length - 1, 0))
    return earlier, later


def both_tables(long, short, x, mask):
    whole = dot(long[...], x)
    parts = [
        dot(short[...], x[i * SHORT_LENGTH : (i + 1) * SHORT_LENGTH])
        for i in range(x.shape[0] // SHORT_LENGTH)
    ]
    return jnp.where(mask, jnp.concatenate(parts, axis=0), whole)


def fold_kernel(where, marks_own, marks_other, v0, r1, r2, r3, long, long_t, short, short_t, gain, taps, o0, o1, o2, o3, vals, spectrum, cond_spec, base, low_base, low_short, conv):
    z = where[0]
    length, half = vals.shape
    owned = length // 4
    part = half // 4
    block = (owned + SHORT_LENGTH // 4) // 4
    for k, piece in enumerate((v0, r1, r2, r3)):
        there = (z - k) & 3
        vals[rows_at(there, owned), :] = piece[pl.ds(0, owned), :]
        got = piece[pl.ds(owned, block), :].astype(F32)
        got = jnp.concatenate([got[:, g * part : (g + 1) * part] for g in range(4)], axis=0)
        low_base[rows_at(there, owned), :] = got[:owned]
        low_short[rows_at(there, SHORT_LENGTH // 4), :] = got[owned:]
    vals.flush()
    mask = short_lanes(marks_own, marks_other, (length, half))
    tall = jnp.concatenate([low_short[...]] * (length // SHORT_LENGTH), axis=0)
    base[...] = jnp.where(
        mask, jnp.concatenate([tall] * 4, axis=1), jnp.concatenate([low_base[...]] * 4, axis=1)
    ).astype(BF)
    base.flush()
    wide = vals[...].astype(F32)
    before, after = neighbours(wide, mask)
    cond = taps[0:1, :] * before + taps[1:2, :] * wide + taps[2:3, :] * after
    high = cond.astype(BF)
    low = (cond - high.astype(F32)).astype(BF)
    spec = both_tables(long, short, vals[...], mask)
    spectrum[...] = spec
    spectrum.flush()
    cspec = both_tables(long, short, high, mask) + both_tables(long, short, low, mask)
    cond_spec[...] = cspec
    cond_spec.flush()
    kern = base[...].astype(F32) + gain[...] * (jnp.sqrt(cspec * cspec + 1.0) - 1.0)
    filtered = (kern * spec).astype(BF)
    conv[...] = both_tables(long_t, short_t, filtered, mask).astype(BF)
    for k, out in enumerate((o0, o1, o2, o3)):
        out[...] = conv[rows_at((z + k) & 3, owned), :]


def out_rows_kernel(where, local, near_all, c1, c2, c3, keep, send, whole):
    z, chip, core = where[0], where[1], where[2]
    rows, half = local.shape
    quarter = rows // 4
    whole[rows_at(z, rows), :] = local[...]
    for k in (1, 2, 3):
        base = ((z - k) & 3) * 4
        whole[rows_at(base + chip, quarter), :] = near_all[k - 1]
        for m, far in ((1, c1), (2, c2), (3, c3)):
            whole[rows_at(base + (chip ^ m), quarter), :] = far[k - 1]
    keep[...] = whole[rows_at(core, half), :]
    send[...] = whole[rows_at(1 - core, half), :]


def mix_kernel(where, outer, c0, r1, r2, r3, w_keep, w_came, own, other, conv, mixed, w_rows, packs):
    z, core = where[0], where[2]
    half = outer.shape[1]
    w_rows[:, :half] = jnp.where(core == 0, w_keep[...], w_came[...])
    w_rows[:, half:] = jnp.where(core == 0, w_came[...], w_keep[...])
    w_rows.flush()
    join_channels(z, (c0, r1, r2, r3), packs, conv)
    conv.flush()
    mixed[...] = (outer[...] * conv[...].astype(F32)).astype(BF)
    count = own.shape[0]
    other[...] = dot(mixed[pl.ds(count, count), :], w_rows[...]).astype(BF)
    own[...] = dot(mixed[pl.ds(0, count), :], w_rows[...])


def second_kernel(where, x, own, came, gain, normed, residual):
    owned = x.shape[0]
    for s in range(x.shape[1]):
        at = pl.ds(s * owned, owned)
        total = x[:, s, :] + own[at, :] + came[at, :].astype(F32)
        residual[at, :] = total
        hat, _ = norm_parts(total)
        normed[at, :] = (hat * gain[...]).astype(BF)


def feed_place_kernel(where, own, other, w_gu, w_dn):
    chip = where[1]
    rows = w_gu.shape[1] // 4
    chunk = own.shape[1] - rows
    for p, part in enumerate((own, other)):
        for i in range(4):
            w_gu[p, pl.ds(i * rows, rows), :] = part[i, pl.ds(0, rows), :]
        for i in range(3):
            at = i + (i >= chip).astype(jnp.int32)
            w_dn[p, pl.ds(i * chunk, chunk), :] = part[at, pl.ds(rows, chunk), :]


def feed_kernel(where, second, cot, w_gu, w_dn, out, layer, act, grads):
    half = w_dn.shape[1]
    width = second.shape[1]
    for p in range(2):
        gate_up = dot(second[...], w_gu[p])
        gate, upward = gate_up[:, :half], gate_up[:, half:]
        grad_act = dot_nt(cot[...], w_dn[p])
        square = gate * gate
        tanh = jnp.tanh(GELU_A * gate * (1.0 + GELU_B * square))
        cdf = 0.5 * (1.0 + tanh)
        unit = gate * cdf
        slope = cdf + 0.5 * gate * (1.0 - tanh * tanh) * (GELU_A * (1.0 + 3.0 * GELU_B * square))
        act[:, p * half : (p + 1) * half] = (unit * upward).astype(BF)
        grads[:, p * width : p * width + half] = (grad_act * upward * slope).astype(BF)
        grads[:, p * width + half : (p + 1) * width] = (grad_act * unit).astype(BF)
    total = dot_nt(grads[:, :width], w_gu[0]) + dot_nt(grads[:, width:], w_gu[1])
    out[...] = total.astype(out.dtype)
    total = dot(act[:, :half], w_dn[0]) + dot(act[:, half:], w_dn[1])
    layer[...] = total.astype(layer.dtype)


def feed_weight_kernel(where, a0, a1, a2, a3, g0, g1, g2, g3, s0, s1, s2, s3, c0, c1, c2, c3, send, keep):
    chip = where[1]
    width = s0.shape[1]
    half = width // 2
    nz, piece, _ = keep.shape
    chunk = half // 3
    rows = piece - chunk
    for p, out in ((1, send), (0, keep)):
        total = None
        for s, g in ((s0, g0), (s1, g1), (s2, g2), (s3, g3)):
            part = dot_tn(s[...], g[:, p * width : (p + 1) * width])
            total = part if total is None else total + part
        for i in range(nz):
            out[i, pl.ds(0, rows), :] = total[i * rows : (i + 1) * rows].astype(BF)
        down = None
        for a, c in ((a0, c0), (a1, c1), (a2, c2), (a3, c3)):
            part = dot_tn(a[:, p * half : (p + 1) * half], c[...])
            down = part if down is None else down + part
        out[chip, pl.ds(rows, chunk), :] = jnp.zeros((chunk, width), BF)
        for i in range(3):
            to = i + (i >= chip).astype(jnp.int32)
            out[to, pl.ds(rows, chunk), :] = down[i * chunk : (i + 1) * chunk].astype(BF)


def copy_kernel(where, a, out):
    out[...] = a[...]


def add_kernel(where, a, b, out):
    out[...] = (a[...].astype(F32) + b[...].astype(F32)).astype(BF)


def layer_out_kernel(where, residual, own, r1, r2, r3, out):
    owned = out.shape[0]
    for s in range(out.shape[1]):
        at = pl.ds(s * owned, owned)
        out[:, s, :] = residual[at, :] + added([x.at[at] for x in (own, r1, r2, r3)])


def second_back_kernel(where, residual, gain, cot, own, r1, r2, r3, low, grad_gain, grad_residual):
    owned = cot.shape[0]
    grad = own[...] + r1[...].astype(F32) + r2[...].astype(F32) + r3[...].astype(F32)
    hat, inv = norm_parts(residual[...])
    pulled, grad_gain[...] = norm_pull(hat, inv, gain[...], grad)
    for s in range(cot.shape[1]):
        at = pl.ds(s * owned, owned)
        total = cot[:, s, :] + pulled[s * owned : (s + 1) * owned]
        grad_residual[at, :] = total
        low[at, :] = total.astype(BF)


def write_pieces(whole, outs, chip):
    rows = whole.shape[0] // 4
    quarter = rows // 4
    for m, out in enumerate(outs):
        for i in range(4):
            out[pl.ds(i * quarter, quarter), :] = whole[rows_at(i * 4 + (chip ^ m), quarter), :]


def mix_back_kernel(where, ga, gb, w_rows, outer, conv, na, nb, mixed, other_mixed, o0, o1, o2, o3, p0, p1, p2, p3, grad_outer, grad_conv, packs, whole):
    z, chip, core = where[0], where[1], where[2]
    count = ga.shape[0]
    half = outer.shape[1]
    for i, grad in enumerate((ga, gb)):
        at = pl.ds(i * count, count)
        grad_mixed = dot_nt(grad[...], w_rows[...])
        grad_outer[at, :] = (grad_mixed * conv[at, :].astype(F32)).astype(BF)
        grad_conv[at, :] = (grad_mixed * outer[at, :]).astype(BF)
    grad_outer.flush()
    split_channels(grad_conv, packs)
    for k, out in enumerate((o0, o1, o2, o3)):
        out[...] = packs[(z + k) & 3]
    total = dot_tn(na[...], grad_outer[pl.ds(0, count), :])
    total = total + dot_tn(nb[...], grad_outer[pl.ds(count, count), :])
    whole[:, :half] = total.astype(BF)
    first = jnp.where(core == 0, ga[:, :half], ga[:, half:])
    second = jnp.where(core == 0, gb[:, :half], gb[:, half:])
    mine = dot_tn(mixed[pl.ds(0, count), :], first) + dot_tn(mixed[pl.ds(count, count), :], second)
    theirs = dot_tn(other_mixed[pl.ds(count, count), :], first)
    theirs = theirs + dot_tn(other_mixed[pl.ds(0, count), :], second)
    whole[rows_at(core, half), half:] = mine.astype(BF)
    whole[rows_at(1 - core, half), half:] = theirs.astype(BF)
    write_pieces(whole, (p0, p1, p2, p3), chip)


def fold_back_kernel(where, marks_own, marks_other, g0, r1, r2, r3, long, short, spectrum, cond_spec, base, gain, taps, vals, long_t, short_t, o0, o1, o2, o3, filt, grads):
    z = where[0]
    length, half = grads.shape
    owned = length // 4
    part = half // 4
    for k, piece in enumerate((g0, r1, r2, r3)):
        grads[rows_at((z - k) & 3, owned), :] = piece[...]
    mask = short_lanes(marks_own, marks_other, (length, half))
    gf = both_tables(long, short, grads[...], mask)
    cspec = cond_spec[...]
    root = jnp.sqrt(cspec * cspec + 1.0)
    above = root - 1.0
    grad_base = gf * spectrum[...]
    grad_spec = (gf * (base[...].astype(F32) + gain[...] * above)).astype(BF)
    grad_cspec = (grad_base * gain[...] * (cspec / root)).astype(BF)
    grad_cond = both_tables(long_t, short_t, grad_cspec, mask)
    direct = both_tables(long_t, short_t, grad_spec, mask)
    wide = vals[...].astype(F32)
    before, after = neighbours(wide, mask)
    grad_before, grad_after = neighbours(grad_cond, mask)
    grads[...] = (
        direct + taps[0:1, :] * grad_after + taps[1:2, :] * grad_cond + taps[2:3, :] * grad_before
    ).astype(BF)
    for k, out in enumerate((o0, o1, o2, o3)):
        out[...] = grads[rows_at((z + k) & 3, owned), :]

    def over_slots(x):
        return sum(x[:, s * part : (s + 1) * part] for s in range(4))

    shorts = jnp.where(mask, grad_base, 0.0)
    small = [
        jnp.sum(x, axis=0, keepdims=True)
        for x in (grad_base * above, grad_cond * before, grad_cond * wide, grad_cond * after)
    ]
    folded = sum(
        shorts[i * SHORT_LENGTH : (i + 1) * SHORT_LENGTH] for i in range(length // SHORT_LENGTH)
    )
    fill = filt.shape[0] * (filt.shape[1] // part) - length - SHORT_LENGTH - 4
    found = jnp.concatenate(
        [
            over_slots(grad_base - shorts),
            over_slots(folded),
            over_slots(jnp.concatenate(small, axis=0)),
            jnp.zeros((fill, part), F32),
        ],
        axis=0,
    )
    size = filt.shape[0]
    blocks = [found[g * size : (g + 1) * size] for g in range(filt.shape[1] // part)]
    filt[...] = jnp.concatenate(blocks, axis=1).astype(BF)


def late_kernel(where, marks_own, marks_other, g0, r1, r2, r3, left, right, na, nb, e0, e1, e2, e3, ride, p0, p1, p2, p3, o0, o1, o2, o3, late, grads, packs, whole, total):
    z, chip = where[0], where[1]
    early_share_kernel(where, e0, e1, e2, e3, ride, o0, o1, o2, o3, total)
    half = left.shape[1]
    owned = packs.shape[1]
    join_channels(z, (g0, r1, r2, r3), packs, grads)
    count = na.shape[0]
    place = lax.broadcasted_iota(jnp.int32, (owned, half), 0)
    for i, marks in enumerate((marks_own, marks_other)):
        for s in range(count // owned):
            at = pl.ds(i * count + s * owned, owned)
            valid = valid_rows(marks, s, z, owned)
            grad = jnp.where(place < valid, grads[at, :].astype(F32), 0.0)
            late[at, :half] = (grad * right[at, :].astype(F32)).astype(BF)
            late[at, half:] = (grad * left[at, :].astype(F32)).astype(BF)
    total = dot_tn(na[...], late[pl.ds(0, count), :]) + dot_tn(nb[...], late[pl.ds(count, count), :])
    whole[...] = total.astype(BF)
    write_pieces(whole, (p0, p1, p2, p3), chip)


def first_grad_kernel(where, grad_outer, late, w, own, other):
    half = grad_outer.shape[1]
    count = own.shape[0]
    for i, out in ((1, other), (0, own)):
        at = pl.ds(i * count, count)
        total = dot_nt(grad_outer[at, :], w[:, :half]) + dot_nt(late[at, :], w[:, half:])
        out[...] = total.astype(out.dtype)


def first_back_kernel(where, x, gain, grad_residual, own, came, grad_gain, grad_inputs):
    owned = x.shape[0]
    riding = None
    for s in range(x.shape[1]):
        at = pl.ds(s * owned, owned)
        hat, inv = norm_parts(x[:, s, :])
        pulled, part = norm_pull(hat, inv, gain[...], own[at, :] + came[at, :].astype(F32))
        grad_inputs[:, s, :] = grad_residual[at, :] + pulled
        riding = part if riding is None else riding + part
    grad_gain[...] = riding


def added(pieces):
    total = pieces[0][...].astype(F32)
    for piece in pieces[1:]:
        total = total + piece[...].astype(F32)
    return total


def ridden(row, width):
    first = lax.broadcasted_iota(jnp.int32, (RIDE, width), 0) == 0
    return jnp.where(first, jnp.broadcast_to(row, (RIDE, width)), 0.0).astype(BF)


def early_share_kernel(where, p0, r1, r2, r3, ride, o0, o1, o2, o3, total):
    z = where[0]
    total[...] = added((p0, r1, r2, r3)).astype(BF)
    quarter = p0.shape[0] // 4
    extra = ridden(ride[...], p0.shape[1])
    for k, out in enumerate((o0, o1, o2, o3)):
        out[pl.ds(0, quarter), :] = total[rows_at((z + k) & 3, quarter), :]
        out[pl.ds(quarter, RIDE), :] = extra


def late_share_kernel(where, p0, r1, r2, r3, ride, filt, e0, e1, e2, e3, o0, o1, o2, o3, early, total):
    early_share_kernel(where, p0, r1, r2, r3, ride, o0, o1, o2, o3, total)
    size = e0.shape[0]
    early[pl.ds(0, size), :] = added((e0, e1, e2, e3)).astype(BF)
    early[pl.ds(size, filt.shape[0]), :] = filt[...]


def in_order(where, pieces, out, start):
    chip = where[1]
    quarter = pieces[0].shape[0] - RIDE
    for m, piece in enumerate(pieces):
        out[rows_at(start // quarter + (chip ^ m), quarter), :] = piece[pl.ds(0, quarter), :]
    riding = added([piece[pl.ds(quarter, RIDE), :] for piece in pieces])
    out[pl.ds(start + 4 * quarter, RIDE), :] = riding.astype(BF)


def late_sum_kernel(where, s0, r1, r2, r3, e0, e1, e2, e3, piece, early, filt):
    piece[...] = added((s0, r1, r2, r3)).astype(BF)
    size = s0.shape[0]
    parts = (e0, e1, e2, e3)
    in_order(where, [e.at[pl.ds(0, size)] for e in parts], early, 0)
    filt[...] = added([e.at[pl.ds(size, filt.shape[0])] for e in parts]).astype(BF)


def gather_kernel(where, s0, r1, r2, r3, f0, f1, f2, f3, early, out):
    z = where[0]
    in_order(where, (s0, r1, r2, r3), out, 0)
    size = early.shape[0]
    out[pl.ds(size, size), :] = early[...]
    step = f0.shape[0]
    for k, piece in enumerate((f0, f1, f2, f3)):
        at = 2 * size + ((z - k) & 3) * step
        out[pl.ds(pl.multiple_of(at, 16), step), :] = piece[...]


def feed_order_kernel(where, shares, gate_up, down):
    z = where[0]
    rows = gate_up.shape[0]
    chunk = shares.shape[1] - rows
    per_z = 6 * chunk
    for side in range(2):
        for zz in range(4):
            for c in range(6):
                mm = c if c < 2 * zz else c + 2
                at = (side * 3 + zz - (zz > mm // 2)) * chunk
                to = side * 4 * per_z + zz * per_z + c * chunk
                gate_up[:, to : to + chunk] = shares[mm, :rows, at : at + chunk].astype(F32)
    for c in range(6):
        mm = c + 2 * (c >= 2 * z).astype(jnp.int32)
        down[pl.ds(c * chunk, chunk), :] = shares[mm, pl.ds(rows, chunk), :].astype(F32)


def last_kernel(where, own, other, w_in, w_out, long, short, gain, taps, norm_one, norm_two):
    core = where[2]
    rows = w_in.shape[0]
    width = w_out.shape[1]
    half = width // 2
    part = half // 4
    size = rows + RIDE

    def write(out, to, a, b):
        a, b = a.astype(F32), b.astype(F32)
        out[:, to : to + half] = jnp.where(core == 0, a, b)
        out[:, to + half : to + width] = jnp.where(core == 0, b, a)

    for start, at, to, out in (
        (size, 0, 0, w_in),
        (0, 0, width, w_in),
        (0, half, 2 * width, w_in),
        (size, half, 0, w_out),
    ):
        place = (pl.ds(start, rows), slice(at, at + half))
        write(out, to, own[place], other[place])
    for start, out in ((0, norm_one), (size, norm_two)):
        place = pl.ds(start + rows, RIDE)
        out[...] = (own[place, :].astype(F32) + other[place, :].astype(F32))[0:1]
    step = (own.shape[0] - 2 * size) // 4
    length, count = long.shape[0], short.shape[0]

    def filter_rows(ref):
        got = []
        for there in range(4):
            at = pl.ds(2 * size + there * step, step)
            blocks = [ref[at, g * part : (g + 1) * part].astype(F32) for g in range(width // part)]
            got.append(jnp.concatenate(blocks, axis=0))
        return jnp.concatenate(got, axis=1)

    a, b = filter_rows(own), filter_rows(other)
    write(long, 0, a[:length], b[:length])
    write(short, 0, a[length : length + count], b[length : length + count])
    rest = length + count
    write(gain, 0, a[rest : rest + 1], b[rest : rest + 1])
    write(taps, 0, a[rest + 1 : rest + 4], b[rest + 1 : rest + 4])


def body(
    inputs,
    cotangent,
    group,
    lens,
    norm1_gain,
    w_in,
    kernel_long,
    kernel_short,
    conv_weight,
    cond_gain,
    w_out,
    norm2_gain,
    w_gate_up,
    w_down,
):
    nz = lax.axis_size("freq")
    ndp = lax.axis_size("dp")
    z = lax.axis_index("freq")
    d = lax.axis_index("dp")
    core = d % 2
    chip = (d // 2) % 4
    owned, slots, width = inputs.shape
    half = width // 2
    length = owned * nz
    tokens = owned * slots
    rows = w_in.shape[0]
    quarter = rows // 4
    others = ndp // GROUP
    blocks = [[g * GROUP + i for i in range(GROUP)] for g in range(others)]
    same_core = [[g * GROUP + 2 * i + c for i in range(4)] for g in range(others) for c in range(2)]
    across = [[i + GROUP * g for g in range(others)] for i in range(GROUP)]

    def core_swap(x):
        return lax.ppermute(x, "dp", [(i, i ^ 1) for i in range(ndp)])

    def chip_swap(x, m):
        return lax.ppermute(x, "dp", [(i, i ^ (2 * m)) for i in range(ndp)])

    def z_rot(x, k):
        return lax.ppermute(x, "freq", [(i, (i + k) % nz) for i in range(nz)])

    def z_swap(pieces):
        return [pieces[0]] + [z_rot(pieces[k], k) for k in range(1, nz)]

    def near_by(piece):
        return [piece] + [chip_swap(piece, m) for m in (1, 2, 3)]

    def exchanged(parts):
        return [parts[0]] + [chip_swap(parts[m], m) for m in (1, 2, 3)]

    def over_groups(x):
        if others > 1:
            return lax.psum(x, "dp", axis_index_groups=across)
        return x

    where = jnp.stack([z, chip, core, z]).astype(jnp.int32)
    part = kernel_short.shape[0]
    hidden = w_down.shape[0] * nz
    per_z = w_down.shape[0]
    chunk = per_z // 6
    taken = rows + chunk
    mlp_piece = run(
        feed_pick_kernel,
        "feed_pick",
        [((taken, width), BF)],
        where,
        [w_gate_up, w_down],
    )[0]
    quarter_of = lambda place: place[1]
    near = run(
        near_kernel,
        "near",
        [((quarter, 4 * half), BF)],
        where,
        [Far(w_in, quarter_of, quarter), Far(w_out, quarter_of, quarter)],
        after=(mlp_piece,),
    )[0]
    in_local, out_local, long_half, short_half = run(
        local_kernel,
        "local",
        [((rows, 3 * half), BF), ((rows, half), BF), ((owned, half), BF), ((part, half), BF)],
        where,
        [w_in, w_out, kernel_long, kernel_short],
        after=(near,),
    )
    all_near = [z_rot(near, k) for k in range(1, nz)]

    gain_one = norm1_gain[None]
    gain_two = norm2_gain[None]
    cot_low = run(low_kernel, "cot_low", [((tokens, width), BF)], where, [Far(cotangent)], after=(near,))[0]
    cot_all = lax.all_gather(cot_low, "dp", axis=0, axis_index_groups=same_core, tiled=True)
    cots = [cot_low] + [
        Far(cot_all, lambda place, m=m: place[1] ^ m, tokens) for m in (1, 2, 3)
    ]
    normed = run(
        first_norm_kernel,
        "first_norm",
        [((tokens, width), BF)],
        where,
        [Far(inputs), gain_one],
        after=(cot_low,),
    )[0]
    normed_other = core_swap(normed)
    in_stack, out_near = run(
        hand_on_kernel,
        "hand_on",
        [((3, quarter, 3 * half), BF), ((3, quarter, half), BF)],
        where,
        all_near,
    )
    in_far = [chip_swap(in_stack, m) for m in (1, 2, 3)]
    mlp_got = lax.all_gather(mlp_piece, "freq", axis=0)

    marks = jnp.concatenate([group[:, None], lens], axis=1).astype(jnp.int32)
    marks_other = core_swap(marks)
    lane = half // nz

    def channels(x):
        own = jnp.where(core == 0, x[:, :half], x[:, half:])
        picked = sum(
            jnp.where(z == i, own[:, i * lane : (i + 1) * lane], 0.0) for i in range(nz)
        )
        return jnp.concatenate([picked] * 4, axis=1)

    gain_lanes = channels(cond_gain[None])
    taps = channels(conv_weight)
    long = jnp.asarray(cosine_table(length), BF)
    long_t = jnp.asarray(cosine_table(length).T, BF)
    short = jnp.asarray(cosine_table(SHORT_LENGTH), BF)
    short_t = jnp.asarray(cosine_table(SHORT_LENGTH).T, BF)

    many = 2 * tokens
    block = (owned + part) // 4
    filler = -block % 16 + block
    piece = ((owned, half), BF)
    *sends, w_in_half, outer, left, right = run(
        project_kernel,
        "project",
        [((owned + filler, half), BF)] * 4
        + [((width, 3 * half), BF, HBM), ((many, half), F32, HBM)]
        + [((many, half), BF, HBM)] * 2,
        where,
        [marks, marks_other, normed, normed_other, in_local, *all_near, *in_far, long_half, short_half],
        [
            pltpu.VMEM((many, half), BF),
            pltpu.VMEM((nz, owned, half), BF),
            pltpu.VMEM((nz, filler, half), F32),
        ],
    )
    came = z_swap(sends)
    out_far = [chip_swap(out_near, m) for m in (1, 2, 3)]
    full = (length, half)
    *sends, vals, spectrum, cond_spec, base = run(
        fold_kernel,
        "fold",
        [piece] * 4 + [(full, BF, HBM), (full, F32, HBM), (full, F32, HBM), (full, BF, HBM)],
        where,
        [marks, marks_other, *came, long, long_t, short, short_t, gain_lanes, taps],
        [
            pltpu.VMEM((length, lane), F32),
            pltpu.VMEM((part * nz, lane), F32),
            pltpu.VMEM(full, BF),
        ],
        after=out_far,
    )
    came = z_swap(sends)
    w_keep, w_send = run(
        out_rows_kernel,
        "out_rows",
        [((half, half), BF)] * 2,
        where,
        [out_local, out_near, *out_far],
        [pltpu.VMEM((width, half), BF)],
        after=(sends[0],),
    )
    w_gu, w_dn = run(
        feed_place_kernel,
        "feed_place",
        [((2, width, width), BF, VMEM), ((2, half, width), BF, VMEM)],
        where,
        [mlp_got, core_swap(mlp_got)],
    )
    part_own, part_other, conv, mixed, w_out_rows = run(
        mix_kernel,
        "mix",
        [((tokens, width), F32), ((tokens, width), BF), ((many, half), BF, HBM)]
        + [((many, half), BF), ((half, width), BF, HBM)],
        where,
        [Far(outer), *came, w_keep, core_swap(w_send)],
        [pltpu.VMEM((nz, owned, half), BF)],
        after=(cot_all,),
    )
    normed_two, residual = run(
        second_kernel,
        "second_norm",
        [((tokens, width), BF), ((tokens, width), F32, HBM)],
        where,
        [Far(inputs), part_own, core_swap(part_other), gain_two],
    )

    arrived = near_by(normed_two)
    acts, grads_gu, sums, layers = [None] * 4, [None] * 4, [None] * 4, [None] * 4
    order = ()
    for m in range(4):
        grad, layer, act, grad_gu = run(
            feed_kernel,
            "feed",
            [
                ((tokens, width), BF if m else F32),
                ((tokens, width), BF if m else F32),
                ((tokens, width), BF, VMEM),
                ((tokens, 2 * width), BF, VMEM),
            ],
            where,
            [arrived[m], cots[m], Held(w_gu), Held(w_dn)],
            after=order,
        )
        order = (grad,)
        acts[m], grads_gu[m], sums[m], layers[m] = Held(act), Held(grad_gu), grad, layer
    backs = [chip_swap(sums[m], m) for m in (1, 2, 3)]

    mlp_send, mlp_keep = run(
        feed_weight_kernel,
        "feed_weights",
        [((nz, taken, width), BF), ((nz, taken, width), BF, VMEM)],
        where,
        [*acts, *grads_gu, *arrived, *cots],
    )
    mlp_grads = run(
        add_kernel,
        "add",
        [((nz, taken, width), BF)],
        where,
        [Held(mlp_keep), core_swap(mlp_send)],
    )[0]
    mlp_share = lax.psum_scatter(mlp_grads, "freq", scatter_dimension=0, tiled=False)
    grad_mix, grad_gain_two, grad_residual = run(
        second_back_kernel,
        "second_norm_back",
        [((tokens, width), BF), ((1, width), F32), ((tokens, width), F32, HBM)],
        where,
        [Far(residual), gain_two, Far(cotangent), sums[0], *backs],
        after=(mlp_grads,),
    )
    grad_mix_other = core_swap(grad_mix)
    *got, grad_outer = run(
        mix_back_kernel,
        "mix_back",
        [piece] * 4 + [((rows, width), BF)] * 4 + [((many, half), BF, HBM)],
        where,
        [
            grad_mix,
            grad_mix_other,
            Far(w_out_rows),
            Far(outer),
            Far(conv),
            normed,
            normed_other,
            mixed,
            core_swap(mixed),
        ],
        [
            pltpu.VMEM((many, half), BF),
            pltpu.VMEM((nz, owned, half), BF),
            pltpu.VMEM((width, width), BF),
        ],
    )
    came = z_swap(got[:4])
    early_all = exchanged(got[4:])

    mlp_mine = run(
        copy_kernel, "share_mlp", [((taken, width), BF)], where, [mlp_share], after=(grad_outer,)
    )[0]
    size = -(-(length + SHORT_LENGTH + 4) // (16 * width // lane)) * 16
    *sends, filt = run(
        fold_back_kernel,
        "fold_back",
        [piece] * 4 + [((size, width), BF)],
        where,
        [
            marks,
            marks_other,
            *came,
            long,
            short,
            Far(spectrum),
            Far(cond_spec),
            Far(base),
            gain_lanes,
            taps,
            Far(vals),
            long_t,
            short_t,
        ],
        [pltpu.VMEM(full, BF)],
        after=(*early_all[1:], mlp_mine),
    )
    came = z_swap(sends)
    layer_far = [chip_swap(layers[m], m) for m in (1, 2, 3)]
    *got, late = run(
        late_kernel,
        "late_weights",
        [((rows, width), BF)] * 4 + [((quarter + RIDE, width), BF)] * 4 + [((many, width), BF)],
        where,
        [
            marks,
            marks_other,
            *came,
            Far(left),
            Far(right),
            normed,
            normed_other,
            *early_all,
            grad_gain_two,
        ],
        [
            pltpu.VMEM((many, half), BF),
            pltpu.VMEM((nz, owned, half), BF),
            pltpu.VMEM((width, width), BF),
            pltpu.VMEM((rows, width), BF),
        ],
        after=layer_far[:2],
    )
    own, other = run(
        first_grad_kernel,
        "first_grad",
        [((tokens, width), F32), ((tokens, width), BF)],
        where,
        [Far(grad_outer), late, Far(w_in_half)],
    )
    grad_gain_one, grad_inputs = run(
        first_back_kernel,
        "first_norm_back",
        [((1, width), F32), ((owned, slots, width), F32, HBM)],
        where,
        [Far(inputs), gain_one, Far(grad_residual), own, core_swap(other)],
    )
    mlp_sum = lax.all_gather(over_groups(mlp_mine), "dp", axis=0, axis_index_groups=blocks)
    *late_sends, early = run(
        late_share_kernel,
        "late_share",
        [((quarter + RIDE, width), BF)] * 4 + [((quarter + RIDE + size, width), BF)],
        where,
        [*exchanged(got[:4]), grad_gain_one, filt, *z_swap(got[4:])],
        [pltpu.VMEM((rows, width), BF)],
    )
    grad_w_gate_up, grad_w_down = run(
        feed_order_kernel,
        "feed_order",
        [((rows, 2 * hidden), F32), ((per_z, width), F32)],
        where,
        [mlp_sum],
    )
    late_piece, early, filt = run(
        late_sum_kernel,
        "late_sum",
        [((quarter + RIDE, width), BF), ((rows + RIDE, width), BF), ((size, width), BF)],
        where,
        [*z_swap(late_sends), *near_by(over_groups(early))],
        after=(grad_w_down,),
    )
    gathered = run(
        gather_kernel,
        "gather",
        [((2 * (rows + RIDE) + nz * size, width), BF)],
        where,
        [*near_by(over_groups(late_piece)), *z_swap([filt] * nz), early],
        after=(layer_far[2],),
    )[0]
    layer_out = run(
        layer_out_kernel,
        "layer_out",
        [((owned, slots, width), F32, HBM)],
        where,
        [Far(residual), layers[0], *layer_far],
    )[0]
    grad_w_in, grad_w_out, grad_long, grad_short, grad_cond, grad_taps, grad_one, grad_two = run(
        last_kernel,
        "last",
        [
            ((rows, 3 * width), F32),
            ((rows, width), F32),
            ((length, width), F32),
            ((SHORT_LENGTH, width), F32),
            ((1, width), F32),
            ((3, width), F32),
            ((1, width), F32),
            ((1, width), F32),
        ],
        where,
        [gathered, core_swap(gathered)],
    )

    return (
        layer_out,
        grad_inputs,
        grad_one.reshape(width),
        grad_w_in,
        grad_long,
        grad_short,
        grad_taps,
        grad_cond.reshape(width),
        grad_w_out,
        grad_two.reshape(width),
        grad_w_gate_up,
        grad_w_down,
    )


def solution(mesh):
    return jax.shard_map(
        body,
        mesh=mesh,
        in_specs=(
            P("freq", "dp", None),
            P("freq", "dp", None),
            P("dp"),
            P("dp", None),
            P(),
            P("freq", None),
            P("freq", None),
            P("freq", None),
            P(),
            P(),
            P("freq", None),
            P(),
            P("freq", None),
            P("freq", None),
        ),
        out_specs=(
            P("freq", "dp", None),
            P("freq", "dp", None),
            P(),
            P("freq", None),
            P(),
            P(),
            P(),
            P(),
            P("freq", None),
            P(),
            P("freq", None),
            P("freq", None),
        ),
        check_vma=False,
    )
```

```python
import math

import jax
import jax.numpy as jnp
import numpy as np
from jax import lax
from jax.experimental import pallas as pl
from jax.experimental.pallas import tpu as pltpu
from jax.sharding import PartitionSpec as P

SHORT_LENGTH = 128
EPSILON = 1e-05
BF = jnp.bfloat16
F32 = jnp.float32
GROUP = 8
RIDE = 16
COSTS = {
    "early_weights": 0,
    "near": 3,
    "first_norm": 3,
    "hand_on": 15,
    "project": 25,
    "fold": 20,
    "out_rows": 2,
    "mix": 15,
    "second_norm": 4,
    "feed": 5,
    "feed_place": 3,
    "down": 4,
    "feed_weights": 8,
    "second_norm_back": 12,
    "mix_back": 6,
    "fold_back": 10,
    "early_share": 1,
    "late_weights": 45,
    "first_grad": 0,
    "first_norm_back": 0,
    "late_share": 10,
    "late_sum": 10,
    "gather": 10,
    "last": 6,
    "feed_order": 4,
}
VMEM, HBM = pltpu.VMEM, pltpu.HBM
GELU_A = math.sqrt(2.0 / math.pi)
GELU_B = 0.044715


def cosine_table(length):
    freq = np.arange(length)[:, None]
    posit = np.arange(length)[None, :]
    phase = (2 * posit + 1) * freq % (4 * length)
    weight = np.where(freq == 0, 1.0, 2.0) / length
    return (np.cos(phase * (math.pi / (2 * length))) * np.sqrt(weight)).astype(np.float32)


def dot(a, b):
    return lax.dot_general(a, b, (((1,), (0,)), ((), ())), preferred_element_type=F32)


def dot_nt(a, b):
    return lax.dot_general(a, b, (((1,), (1,)), ((), ())), preferred_element_type=F32)


def dot_tn(a, b):
    return lax.dot_general(a, b, (((0,), (0,)), ((), ())), preferred_element_type=F32)


def norm_parts(values):
    center = values - jnp.mean(values, axis=-1, keepdims=True)
    spread = jnp.mean(center * center, axis=-1, keepdims=True)
    inv = lax.rsqrt(spread + EPSILON)
    return center * inv, inv


def norm_pull(hat, inv, gain, grad):
    scaled = grad * gain
    mean_one = jnp.mean(scaled, axis=-1, keepdims=True)
    mean_two = jnp.mean(scaled * hat, axis=-1, keepdims=True)
    return inv * (scaled - mean_one - hat * mean_two), jnp.sum(grad * hat, axis=0, keepdims=True)


def pick(stacked, index):
    return lax.dynamic_index_in_dim(stacked, index, axis=0, keepdims=False)


class Far:
    def __init__(self, array, start=None, size=None):
        self.array = pltpu.with_memory_space_constraint(array, pltpu.HBM)
        self.start = start
        self.shape = array.shape if start is None else (size, *array.shape[1:])

    def source(self, ref, where):
        return ref if self.start is None else ref.at[rows_at(self.start(where), self.shape[0])]


class Held:
    def __init__(self, array):
        self.array = pltpu.with_memory_space_constraint(array, pltpu.VMEM)


class Fetched:
    def __init__(self, ref, copy):
        self.ref, self.copy, self.shape = ref, copy, ref.shape

    def ready(self):
        if self.copy is not None:
            self.copy.wait()
            self.copy = None
        return self.ref

    def __getitem__(self, place):
        return self.ready()[place]

    @property
    def at(self):
        return self.ready().at


class Kept:
    def __init__(self, ref, copy):
        self.ref, self.copy, self.shape, self.dtype = ref, copy, ref.shape, ref.dtype
        self.started = False

    def __getitem__(self, place):
        return self.ref[place]

    def __setitem__(self, place, value):
        self.ref[place] = value

    def flush(self):
        if not self.started:
            self.copy.start()
            self.started = True


def run(kernel, name, outs, where, ins, scratch=(), after=()):
    arrays = [x.array if isinstance(x, (Far, Held)) else x for x in ins]
    far_in = [isinstance(x, Far) for x in ins]
    far_out = [o[2:] == (HBM,) for o in outs]
    shapes = [o[2](*o[:2]) if len(o) > 2 else jax.ShapeDtypeStruct(*o) for o in outs]
    outs = [o[:2] for o in outs]
    n_in, n_after, n_out, n_scratch = len(ins), len(after), len(outs), len(scratch)
    buffers = [pltpu.VMEM(x.shape, x.array.dtype) for x in ins if isinstance(x, Far)]
    buffers += [pltpu.VMEM(s, t) for (s, t), far in zip(outs, far_out) if far]

    def wrapped(*refs):
        where_ref, in_refs = refs[0], list(refs[1 : 1 + n_in])
        rest = list(refs[1 + n_in + n_after :])
        out_refs, rest = rest[:n_out], rest[n_out:]
        own, held = rest[:n_scratch], rest[n_scratch:]
        if not buffers:
            kernel(where_ref, *in_refs, *out_refs, *own)
            return
        held, sems = held[:-1], held[-1]
        number = 0
        for i in range(n_in):
            if far_in[i]:
                source = ins[i].source(in_refs[i], where_ref)
                copy = pltpu.make_async_copy(source, held[number], sems.at[number])
                copy.start()
                in_refs[i] = Fetched(held[number], copy)
                number += 1
        kept = []
        for i in range(n_out):
            if far_out[i]:
                copy = pltpu.make_async_copy(held[number], out_refs[i], sems.at[number])
                out_refs[i] = Kept(held[number], copy)
                kept.append(out_refs[i])
                number += 1
        kernel(where_ref, *in_refs, *out_refs, *own)
        for ref in kept:
            ref.flush()
        for ref in kept:
            ref.copy.wait()
        for ref in in_refs:
            if isinstance(ref, Fetched):
                ref.ready()

    size = sum(x.size * x.dtype.itemsize for x in arrays)
    size += sum(math.prod(s) * jnp.dtype(t).itemsize for s, t in outs)
    far = pl.BlockSpec(memory_space=pltpu.HBM)
    near = pl.BlockSpec(memory_space=pltpu.VMEM)
    small = pl.BlockSpec(memory_space=pltpu.SMEM)
    return pl.pallas_call(
        wrapped,
        out_shape=shapes,
        in_specs=[small]
        + [far if f else small if x.dtype == jnp.int32 else near for x, f in zip(arrays, far_in)]
        + [pl.BlockSpec(memory_space=pl.ANY)] * n_after,
        out_specs=[far if f else near for f in far_out],
        scratch_shapes=list(scratch)
        + buffers
        + ([pltpu.SemaphoreType.DMA((len(buffers),))] if buffers else []),
        compiler_params=pltpu.CompilerParams(vmem_limit_bytes=24 * 2**20),
        cost_estimate=pl.CostEstimate(
            flops=int(COSTS.get(name, 1) * 1.15e9),
            bytes_accessed=int(size) if COSTS.get(name, 1) else 0,
            transcendentals=0,
        ),
        name=name,
    )(where, *arrays, *after)


def rows_at(index, size):
    return pl.ds(pl.multiple_of(index * size, 16), size)


def first_norm_kernel(where, x, gain, normed):
    owned = x.shape[0]
    for s in range(x.shape[1]):
        hat, _ = norm_parts(x[:, s, :])
        normed[pl.ds(s * owned, owned), :] = (hat * gain[...]).astype(BF)


def low_kernel(where, x, out):
    owned = x.shape[0]
    for s in range(x.shape[1]):
        out[pl.ds(s * owned, owned), :] = x[:, s, :].astype(BF)


def near_kernel(where, w_in, w_out, near):
    core = where[2]
    half = w_out.shape[1] // 2
    for i, ref in enumerate((w_in, w_in, w_in, w_out)):
        at = i % 3 * 2 * half
        near[:, i * half : (i + 1) * half] = jnp.where(
            core == 0, ref[:, at : at + half], ref[:, at + half : at + 2 * half]
        )


def local_kernel(where, w_in, w_out, long, short, local, out_local, long_half, short_half):
    core = where[2]
    width = w_out.shape[1]
    half = width // 2

    def mine(x, start):
        return jnp.where(core == 0, x[:, start : start + half], x[:, start + half : start + width])

    for i in range(3):
        local[:, i * half : (i + 1) * half] = mine(w_in, i * width)
    out_local[...] = mine(w_out, 0)
    long_half[...] = mine(long, 0)
    short_half[...] = mine(short, 0)


def hand_on_kernel(where, n1, n2, n3, stack):
    for k, near in enumerate((n1, n2, n3)):
        stack[k] = near[...]


def feed_pick_kernel(where, w_gate_up, w_down, mlp):
    z, chip, core = where[0], where[1], where[2]
    rows = w_gate_up.shape[0]
    hidden = w_gate_up.shape[1] // 2
    per_z = w_down.shape[0]
    chunk = per_z // 6
    member = 2 * chip + core
    for side in range(2):
        for i in range(3):
            zz = i + (i >= chip).astype(jnp.int32)
            c = jnp.where(member < 2 * zz, member, member - 2)
            start = pl.multiple_of(side * hidden + zz * per_z + c * chunk, 128)
            to = (side * 3 + i) * chunk
            mlp[pl.ds(0, rows), to : to + chunk] = w_gate_up[:, pl.ds(start, chunk)]
    c = jnp.clip(jnp.where(member < 2 * z, member, member - 2), 0, 5)
    mlp[pl.ds(rows, chunk), :] = w_down[rows_at(c, chunk), :]


def valid_rows(marks, s, z, owned):
    total = marks[s, 1] + marks[s, 2] + marks[s, 3] + marks[s, 4]
    return jnp.where(marks[s, 0] == 1, marks[s, 1 + z], total - owned * z)


def split_channels(whole, packs):
    count, owned, lanes = packs.shape
    part = lanes // count
    for there in range(count):
        for s in range(count):
            packs[there, :, s * part : (s + 1) * part] = whole[
                s * owned : (s + 1) * owned, there * part : (there + 1) * part
            ]


def join_channels(z, pieces, packs, whole):
    count, owned, lanes = packs.shape
    part = lanes // count
    for k, piece in enumerate(pieces):
        packs[(z - k) & 3] = piece[...]
    for there in range(count):
        for s in range(count):
            whole[s * owned : (s + 1) * owned, there * part : (there + 1) * part] = packs[
                there, :, s * part : (s + 1) * part
            ]


def project_kernel(where, marks_own, marks_other, na, nb, local, n1, n2, n3, c1, c2, c3, long_in, short_in, v0, v1, v2, v3, w, outer, left, right, vals, packs, folds):
    z, chip = where[0], where[1]
    rows = local.shape[0]
    quarter = rows // 4
    half = outer.shape[1]
    wide = 3 * half
    w[rows_at(z, rows), :] = local[...]
    for k, near in ((1, n1), (2, n2), (3, n3)):
        base = ((z - k) & 3) * 4
        w[rows_at(base + chip, quarter), :] = near[:, :wide]
        for m, far in ((1, c1), (2, c2), (3, c3)):
            w[rows_at(base + (chip ^ m), quarter), :] = far[k - 1, :, :wide]
    w.flush()
    owned = packs.shape[1]
    count = na.shape[0]
    place = lax.broadcasted_iota(jnp.int32, (owned, half), 0)
    for i, (tokens, marks) in enumerate(((na, marks_own), (nb, marks_other))):
        at = pl.ds(i * count, count)
        full = dot(tokens[...], w[...])
        a, b, c = full[:, :half], full[:, half : 2 * half], full[:, 2 * half :]
        outer[at, :] = a
        left[at, :] = b.astype(BF)
        right[at, :] = c.astype(BF)
        for s in range(count // owned):
            valid = valid_rows(marks, s, z, owned)
            low = slice(s * owned, (s + 1) * owned)
            vals[pl.ds(i * count + s * owned, owned), :] = jnp.where(
                place < valid, b[low] * c[low], 0.0
            ).astype(BF)
    for ref in (outer, left, right):
        ref.flush()
    split_channels(vals, packs)
    part = half // 4
    block = (long_in.shape[0] + short_in.shape[0]) // 4
    folds[...] = jnp.zeros(folds.shape, F32)
    for there in range(4):
        lanes = slice(there * part, (there + 1) * part)
        both = jnp.concatenate([long_in[:, lanes], short_in[:, lanes]], axis=0).astype(F32)
        for g in range(4):
            folds[there, pl.ds(0, block), g * part : (g + 1) * part] = both[g * block : (g + 1) * block]
    for k, out in enumerate((v0, v1, v2, v3)):
        out[pl.ds(0, owned), :] = packs[(z + k) & 3]
        rest = out.shape[0] - owned
        out[pl.ds(owned, rest), :] = folds[(z + k) & 3].astype(BF)


def short_lanes(marks_own, marks_other, shape):
    part = shape[1] // 4
    slot = lax.broadcasted_iota(jnp.int32, shape, 1) // part
    groups = [marks_own[0, 0], marks_own[1, 0], marks_other[0, 0], marks_other[1, 0]]
    return sum(jnp.where(slot == s, group, 0) for s, group in enumerate(groups)) == 1


def neighbours(x, short):
    length = x.shape[0]
    place = lax.broadcasted_iota(jnp.int32, x.shape, 0)
    starts = (place == 0) | (short & (place % SHORT_LENGTH == 0))
    ends = (place == length - 1) | (short & (place % SHORT_LENGTH == SHORT_LENGTH - 1))
    earlier = jnp.where(starts, 0.0, pltpu.roll(x, 1, 0))
    later = jnp.where(ends, 0.0, pltpu.roll(x, length - 1, 0))
    return earlier, later


def both_tables(long, short, x, mask):
    whole = dot(long[...], x)
    parts = [
        dot(short[...], x[i * SHORT_LENGTH : (i + 1) * SHORT_LENGTH])
        for i in range(x.shape[0] // SHORT_LENGTH)
    ]
    return jnp.where(mask, jnp.concatenate(parts, axis=0), whole)


def fold_kernel(where, marks_own, marks_other, v0, r1, r2, r3, long, long_t, short, short_t, gain, taps, o0, o1, o2, o3, vals, spectrum, cond_spec, base, low_base, low_short, conv):
    z = where[0]
    length, half = vals.shape
    owned = length // 4
    part = half // 4
    block = (owned + SHORT_LENGTH // 4) // 4
    for k, piece in enumerate((v0, r1, r2, r3)):
        there = (z - k) & 3
        vals[rows_at(there, owned), :] = piece[pl.ds(0, owned), :]
        got = piece[pl.ds(owned, block), :].astype(F32)
        got = jnp.concatenate([got[:, g * part : (g + 1) * part] for g in range(4)], axis=0)
        low_base[rows_at(there, owned), :] = got[:owned]
        low_short[rows_at(there, SHORT_LENGTH // 4), :] = got[owned:]
    vals.flush()
    mask = short_lanes(marks_own, marks_other, (length, half))
    tall = jnp.concatenate([low_short[...]] * (length // SHORT_LENGTH), axis=0)
    base[...] = jnp.where(
        mask, jnp.concatenate([tall] * 4, axis=1), jnp.concatenate([low_base[...]] * 4, axis=1)
    ).astype(BF)
    base.flush()
    wide = vals[...].astype(F32)
    before, after = neighbours(wide, mask)
    cond = taps[0:1, :] * before + taps[1:2, :] * wide + taps[2:3, :] * after
    high = cond.astype(BF)
    low = (cond - high.astype(F32)).astype(BF)
    spec = both_tables(long, short, vals[...], mask)
    spectrum[...] = spec
    spectrum.flush()
    cspec = both_tables(long, short, high, mask) + both_tables(long, short, low, mask)
    cond_spec[...] = cspec
    cond_spec.flush()
    kern = base[...].astype(F32) + gain[...] * (jnp.sqrt(cspec * cspec + 1.0) - 1.0)
    filtered = (kern * spec).astype(BF)
    conv[...] = both_tables(long_t, short_t, filtered, mask).astype(BF)
    for k, out in enumerate((o0, o1, o2, o3)):
        out[...] = conv[rows_at((z + k) & 3, owned), :]


def out_rows_kernel(where, local, n1, n2, n3, c1, c2, c3, keep, send, whole):
    z, chip, core = where[0], where[1], where[2]
    rows, half = local.shape
    quarter = rows // 4
    wide = 3 * half
    whole[rows_at(z, rows), :] = local[...]
    for k, near in ((1, n1), (2, n2), (3, n3)):
        base = ((z - k) & 3) * 4
        whole[rows_at(base + chip, quarter), :] = near[:, wide:]
        for m, far in ((1, c1), (2, c2), (3, c3)):
            whole[rows_at(base + (chip ^ m), quarter), :] = far[k - 1, :, wide:]
    keep[...] = whole[rows_at(core, half), :]
    send[...] = whole[rows_at(1 - core, half), :]


def mix_kernel(where, outer, c0, r1, r2, r3, w_keep, w_came, own, other, conv, mixed, w_rows, packs):
    z, core = where[0], where[2]
    half = outer.shape[1]
    w_rows[:, :half] = jnp.where(core == 0, w_keep[...], w_came[...])
    w_rows[:, half:] = jnp.where(core == 0, w_came[...], w_keep[...])
    w_rows.flush()
    join_channels(z, (c0, r1, r2, r3), packs, conv)
    conv.flush()
    mixed[...] = (outer[...] * conv[...].astype(F32)).astype(BF)
    count = own.shape[0]
    other[...] = dot(mixed[pl.ds(count, count), :], w_rows[...]).astype(BF)
    own[...] = dot(mixed[pl.ds(0, count), :], w_rows[...])


def second_kernel(where, x, own, came, gain, normed, residual):
    owned = x.shape[0]
    for s in range(x.shape[1]):
        at = pl.ds(s * owned, owned)
        total = x[:, s, :] + own[at, :] + came[at, :].astype(F32)
        residual[at, :] = total
        hat, _ = norm_parts(total)
        normed[at, :] = (hat * gain[...]).astype(BF)


def feed_place_kernel(where, own, other, w_gu, w_dn):
    chip = where[1]
    rows = w_gu.shape[1] // 4
    chunk = own.shape[1] - rows
    for p, part in enumerate((own, other)):
        for i in range(4):
            w_gu[p, pl.ds(i * rows, rows), :] = part[i, pl.ds(0, rows), :]
        for i in range(3):
            at = i + (i >= chip).astype(jnp.int32)
            w_dn[p, pl.ds(i * chunk, chunk), :] = part[at, pl.ds(rows, chunk), :]


def feed_kernel(where, second, cot, w_gu, w_dn, out, layer, act, grads):
    half = w_dn.shape[1]
    width = second.shape[1]
    for p in range(2):
        gate_up = dot(second[...], w_gu[p])
        gate, upward = gate_up[:, :half], gate_up[:, half:]
        grad_act = dot_nt(cot[...], w_dn[p])
        square = gate * gate
        tanh = jnp.tanh(GELU_A * gate * (1.0 + GELU_B * square))
        cdf = 0.5 * (1.0 + tanh)
        unit = gate * cdf
        slope = cdf + 0.5 * gate * (1.0 - tanh * tanh) * (GELU_A * (1.0 + 3.0 * GELU_B * square))
        act[:, p * half : (p + 1) * half] = (unit * upward).astype(BF)
        grads[:, p * width : p * width + half] = (grad_act * upward * slope).astype(BF)
        grads[:, p * width + half : (p + 1) * width] = (grad_act * unit).astype(BF)
    total = dot_nt(grads[:, :width], w_gu[0]) + dot_nt(grads[:, width:], w_gu[1])
    out[...] = total.astype(out.dtype)
    total = dot(act[:, :half], w_dn[0]) + dot(act[:, half:], w_dn[1])
    layer[...] = total.astype(layer.dtype)


def feed_weight_kernel(where, a0, a1, a2, a3, g0, g1, g2, g3, s0, s1, s2, s3, c0, c1, c2, c3, send, keep):
    chip = where[1]
    width = s0.shape[1]
    half = width // 2
    nz, piece, _ = keep.shape
    chunk = half // 3
    rows = piece - chunk
    for p, out in ((1, send), (0, keep)):
        total = None
        for s, g in ((s0, g0), (s1, g1), (s2, g2), (s3, g3)):
            part = dot_tn(s[...], g[:, p * width : (p + 1) * width])
            total = part if total is None else total + part
        for i in range(nz):
            out[i, pl.ds(0, rows), :] = total[i * rows : (i + 1) * rows].astype(BF)
        down = None
        for a, c in ((a0, c0), (a1, c1), (a2, c2), (a3, c3)):
            part = dot_tn(a[:, p * half : (p + 1) * half], c[...])
            down = part if down is None else down + part
        out[chip, pl.ds(rows, chunk), :] = jnp.zeros((chunk, width), BF)
        for i in range(3):
            to = i + (i >= chip).astype(jnp.int32)
            out[to, pl.ds(rows, chunk), :] = down[i * chunk : (i + 1) * chunk].astype(BF)


def add_kernel(where, a, b, out):
    out[...] = (a[...].astype(F32) + b[...].astype(F32)).astype(BF)


def layer_out_kernel(where, residual, own, r1, r2, r3, out):
    owned = out.shape[0]
    for s in range(out.shape[1]):
        at = pl.ds(s * owned, owned)
        out[:, s, :] = residual[at, :] + added([x.at[at] for x in (own, r1, r2, r3)])


def second_back_kernel(where, residual, gain, cot, own, r1, r2, r3, low, grad_gain, grad_residual):
    owned = cot.shape[0]
    grad = own[...] + r1[...].astype(F32) + r2[...].astype(F32) + r3[...].astype(F32)
    hat, inv = norm_parts(residual[...])
    pulled, grad_gain[...] = norm_pull(hat, inv, gain[...], grad)
    for s in range(cot.shape[1]):
        at = pl.ds(s * owned, owned)
        total = cot[:, s, :] + pulled[s * owned : (s + 1) * owned]
        grad_residual[at, :] = total
        low[at, :] = total.astype(BF)


def write_pieces(whole, outs, chip):
    rows = whole.shape[0] // 4
    quarter = rows // 4
    for m, out in enumerate(outs):
        for i in range(4):
            out[pl.ds(i * quarter, quarter), :] = whole[rows_at(i * 4 + (chip ^ m), quarter), :]


def mix_back_kernel(where, ga, gb, w_rows, outer, conv, o0, o1, o2, o3, grad_outer, grad_conv, packs):
    z = where[0]
    count = ga.shape[0]
    half = outer.shape[1]
    for i, grad in enumerate((ga, gb)):
        at = pl.ds(i * count, count)
        grad_mixed = dot_nt(grad[...], w_rows[...])
        grad_outer[at, :] = (grad_mixed * conv[at, :].astype(F32)).astype(BF)
        grad_conv[at, :] = (grad_mixed * outer[at, :]).astype(BF)
    grad_outer.flush()
    split_channels(grad_conv, packs)
    for k, out in enumerate((o0, o1, o2, o3)):
        out[...] = packs[(z + k) & 3]


def early_kernel(where, na, nb, grad_outer, mixed, other_mixed, ga, gb, p0, p1, p2, p3, whole):
    chip, core = where[1], where[2]
    count, half = na.shape[0], mixed.shape[1]
    first = jnp.where(core == 0, ga[:, :half], ga[:, half:])
    second = jnp.where(core == 0, gb[:, :half], gb[:, half:])
    mine = dot_tn(mixed[pl.ds(0, count), :], first) + dot_tn(mixed[pl.ds(count, count), :], second)
    theirs = dot_tn(other_mixed[pl.ds(count, count), :], first)
    theirs = theirs + dot_tn(other_mixed[pl.ds(0, count), :], second)
    whole[rows_at(core, half), half:] = mine.astype(BF)
    whole[rows_at(1 - core, half), half:] = theirs.astype(BF)
    total = dot_tn(na[...], grad_outer[pl.ds(0, count), :])
    total = total + dot_tn(nb[...], grad_outer[pl.ds(count, count), :])
    whole[:, :half] = total.astype(BF)
    write_pieces(whole, (p0, p1, p2, p3), chip)


def fold_back_kernel(where, marks_own, marks_other, g0, r1, r2, r3, long, short, spectrum, cond_spec, base, gain, taps, vals, long_t, short_t, o0, o1, o2, o3, filt, grads):
    z = where[0]
    length, half = grads.shape
    owned = length // 4
    part = half // 4
    for k, piece in enumerate((g0, r1, r2, r3)):
        grads[rows_at((z - k) & 3, owned), :] = piece[...]
    mask = short_lanes(marks_own, marks_other, (length, half))
    gf = both_tables(long, short, grads[...], mask)
    cspec = cond_spec[...]
    root = jnp.sqrt(cspec * cspec + 1.0)
    above = root - 1.0
    grad_base = gf * spectrum[...]
    grad_spec = (gf * (base[...].astype(F32) + gain[...] * above)).astype(BF)
    grad_cspec = (grad_base * gain[...] * (cspec / root)).astype(BF)
    grad_cond = both_tables(long_t, short_t, grad_cspec, mask)
    direct = both_tables(long_t, short_t, grad_spec, mask)
    wide = vals[...].astype(F32)
    before, after = neighbours(wide, mask)
    grad_before, grad_after = neighbours(grad_cond, mask)
    grads[...] = (
        direct + taps[0:1, :] * grad_after + taps[1:2, :] * grad_cond + taps[2:3, :] * grad_before
    ).astype(BF)
    for k, out in enumerate((o0, o1, o2, o3)):
        out[...] = grads[rows_at((z + k) & 3, owned), :]

    def over_slots(x):
        return sum(x[:, s * part : (s + 1) * part] for s in range(4))

    shorts = jnp.where(mask, grad_base, 0.0)
    small = [
        jnp.sum(x, axis=0, keepdims=True)
        for x in (grad_base * above, grad_cond * before, grad_cond * wide, grad_cond * after)
    ]
    folded = sum(
        shorts[i * SHORT_LENGTH : (i + 1) * SHORT_LENGTH] for i in range(length // SHORT_LENGTH)
    )
    fill = filt.shape[0] * (filt.shape[1] // part) - length - SHORT_LENGTH - 4
    found = jnp.concatenate(
        [
            over_slots(grad_base - shorts),
            over_slots(folded),
            over_slots(jnp.concatenate(small, axis=0)),
            jnp.zeros((fill, part), F32),
        ],
        axis=0,
    )
    size = filt.shape[0]
    blocks = [found[g * size : (g + 1) * size] for g in range(filt.shape[1] // part)]
    filt[...] = jnp.concatenate(blocks, axis=1).astype(BF)


def late_kernel(where, marks_own, marks_other, g0, r1, r2, r3, left, right, na, nb, p0, p1, p2, p3, late, grads, packs, whole):
    z, chip = where[0], where[1]
    half = left.shape[1]
    owned = packs.shape[1]
    join_channels(z, (g0, r1, r2, r3), packs, grads)
    count = na.shape[0]
    place = lax.broadcasted_iota(jnp.int32, (owned, half), 0)
    for i, marks in enumerate((marks_own, marks_other)):
        for s in range(count // owned):
            at = pl.ds(i * count + s * owned, owned)
            valid = valid_rows(marks, s, z, owned)
            grad = jnp.where(place < valid, grads[at, :].astype(F32), 0.0)
            late[at, :half] = (grad * right[at, :].astype(F32)).astype(BF)
            late[at, half:] = (grad * left[at, :].astype(F32)).astype(BF)
    total = dot_tn(na[...], late[pl.ds(0, count), :]) + dot_tn(nb[...], late[pl.ds(count, count), :])
    whole[...] = total.astype(BF)
    write_pieces(whole, (p0, p1, p2, p3), chip)


def first_grad_kernel(where, grad_outer, late, w, own, other):
    half = grad_outer.shape[1]
    count = own.shape[0]
    for i, out in ((1, other), (0, own)):
        at = pl.ds(i * count, count)
        total = dot_nt(grad_outer[at, :], w[:, :half]) + dot_nt(late[at, :], w[:, half:])
        out[...] = total.astype(out.dtype)


def first_back_kernel(where, x, gain, grad_residual, own, came, grad_gain, grad_inputs):
    owned = x.shape[0]
    riding = None
    for s in range(x.shape[1]):
        at = pl.ds(s * owned, owned)
        hat, inv = norm_parts(x[:, s, :])
        pulled, part = norm_pull(hat, inv, gain[...], own[at, :] + came[at, :].astype(F32))
        grad_inputs[:, s, :] = grad_residual[at, :] + pulled
        riding = part if riding is None else riding + part
    grad_gain[...] = riding


def added(pieces):
    total = pieces[0][...].astype(F32)
    for piece in pieces[1:]:
        total = total + piece[...].astype(F32)
    return total


def late_share_kernel(where, p0, r1, r2, r3, e0, e1, e2, e3, one, two, o0, o1, o2, o3, late, early):
    z = where[0]
    late[...] = added((p0, r1, r2, r3)).astype(BF)
    early[...] = added((e0, e1, e2, e3)).astype(BF)
    quarter = p0.shape[0] // 4
    width = p0.shape[1]
    place = lax.broadcasted_iota(jnp.int32, (RIDE, width), 0)
    extra = jnp.where(place == 0, jnp.broadcast_to(one[...], (RIDE, width)), 0.0)
    extra = jnp.where(place == 1, jnp.broadcast_to(two[...], (RIDE, width)), extra).astype(BF)
    for k, out in enumerate((o0, o1, o2, o3)):
        at = rows_at((z + k) & 3, quarter)
        out[pl.ds(0, quarter), :] = late[at, :]
        out[pl.ds(quarter, quarter), :] = early[at, :]
        out[pl.ds(2 * quarter, RIDE), :] = extra


def late_sum_kernel(where, s0, r1, r2, r3, f0, f1, f2, f3, piece, filt):
    piece[...] = added((s0, r1, r2, r3)).astype(BF)
    filt[...] = added((f0, f1, f2, f3)).astype(BF)


def gather_kernel(where, s0, r1, r2, r3, f0, f1, f2, f3, out):
    z, chip = where[0], where[1]
    quarter = (s0.shape[0] - RIDE) // 2
    parts = (s0, r1, r2, r3)
    for m, piece in enumerate(parts):
        for i in range(2):
            out[rows_at(i * 4 + (chip ^ m), quarter), :] = piece[pl.ds(i * quarter, quarter), :]
    riding = added([piece[pl.ds(2 * quarter, RIDE), :] for piece in parts])
    top = 8 * quarter
    out[pl.ds(top, RIDE), :] = riding.astype(BF)
    step = f0.shape[0]
    for k, piece in enumerate((f0, f1, f2, f3)):
        at = top + RIDE + ((z - k) & 3) * step
        out[pl.ds(pl.multiple_of(at, 16), step), :] = piece[...]


def feed_order_kernel(where, shares, gate_up, down):
    z = where[0]
    rows = gate_up.shape[0]
    chunk = shares.shape[1] - rows
    per_z = 6 * chunk
    for side in range(2):
        for zz in range(4):
            for c in range(6):
                mm = c if c < 2 * zz else c + 2
                at = (side * 3 + zz - (zz > mm // 2)) * chunk
                to = side * 4 * per_z + zz * per_z + c * chunk
                gate_up[:, to : to + chunk] = shares[mm, :rows, at : at + chunk].astype(F32)
    for c in range(6):
        mm = c + 2 * (c >= 2 * z).astype(jnp.int32)
        down[pl.ds(c * chunk, chunk), :] = shares[mm, pl.ds(rows, chunk), :].astype(F32)


def last_kernel(where, own, other, w_in, w_out, long, short, gain, taps, norm_one, norm_two):
    core = where[2]
    rows = w_in.shape[0]
    width = w_out.shape[1]
    half = width // 2
    part = half // 4
    top = 2 * rows

    def write(out, to, a, b):
        a, b = a.astype(F32), b.astype(F32)
        out[:, to : to + half] = jnp.where(core == 0, a, b)
        out[:, to + half : to + width] = jnp.where(core == 0, b, a)

    for start, at, to, out in (
        (rows, 0, 0, w_in),
        (0, 0, width, w_in),
        (0, half, 2 * width, w_in),
        (rows, half, 0, w_out),
    ):
        place = (pl.ds(start, rows), slice(at, at + half))
        write(out, to, own[place], other[place])
    place = pl.ds(top, RIDE)
    riding = own[place, :].astype(F32) + other[place, :].astype(F32)
    norm_one[...] = riding[0]
    norm_two[...] = riding[1]
    step = (own.shape[0] - top - RIDE) // 4
    length, count = long.shape[0], short.shape[0]

    def filter_rows(ref):
        got = []
        for there in range(4):
            at = pl.ds(top + RIDE + there * step, step)
            blocks = [ref[at, g * part : (g + 1) * part].astype(F32) for g in range(width // part)]
            got.append(jnp.concatenate(blocks, axis=0))
        return jnp.concatenate(got, axis=1)

    a, b = filter_rows(own), filter_rows(other)
    write(long, 0, a[:length], b[:length])
    write(short, 0, a[length : length + count], b[length : length + count])
    rest = length + count
    a_row, b_row = a[rest], b[rest]
    gain[pl.ds(0, half)] = jnp.where(core == 0, a_row, b_row)
    gain[pl.ds(half, half)] = jnp.where(core == 0, b_row, a_row)
    write(taps, 0, a[rest + 1 : rest + 4], b[rest + 1 : rest + 4])


def body(
    inputs,
    cotangent,
    group,
    lens,
    norm1_gain,
    w_in,
    kernel_long,
    kernel_short,
    conv_weight,
    cond_gain,
    w_out,
    norm2_gain,
    w_gate_up,
    w_down,
):
    nz = lax.axis_size("freq")
    ndp = lax.axis_size("dp")
    z = lax.axis_index("freq")
    d = lax.axis_index("dp")
    core = d % 2
    chip = (d // 2) % 4
    owned, slots, width = inputs.shape
    half = width // 2
    length = owned * nz
    tokens = owned * slots
    rows = w_in.shape[0]
    quarter = rows // 4
    others = ndp // GROUP
    blocks = [[g * GROUP + i for i in range(GROUP)] for g in range(others)]
    same_core = [[g * GROUP + 2 * i + c for i in range(4)] for g in range(others) for c in range(2)]
    across = [[i + GROUP * g for g in range(others)] for i in range(GROUP)]

    def core_swap(x):
        return lax.ppermute(x, "dp", [(i, i ^ 1) for i in range(ndp)])

    def chip_swap(x, m):
        return lax.ppermute(x, "dp", [(i, i ^ (2 * m)) for i in range(ndp)])

    def z_rot(x, k):
        return lax.ppermute(x, "freq", [(i, (i + k) % nz) for i in range(nz)])

    def z_swap(pieces):
        return [pieces[0]] + [z_rot(pieces[k], k) for k in range(1, nz)]

    def own_far(pieces):
        got = z_swap(pieces)
        return [Far(got[0])] + got[1:]

    def near_by(piece):
        return [piece] + [chip_swap(piece, m) for m in (1, 2, 3)]

    def exchanged(parts):
        return [parts[0]] + [chip_swap(parts[m], m) for m in (1, 2, 3)]

    def over_groups(x):
        if others > 1:
            return lax.psum(x, "dp", axis_index_groups=across)
        return x

    where = jnp.stack([z, chip, core, z]).astype(jnp.int32)
    part = kernel_short.shape[0]
    hidden = w_down.shape[0] * nz
    per_z = w_down.shape[0]
    chunk = per_z // 6
    taken = rows + chunk
    quarter_of = lambda place: place[1]
    near = run(
        near_kernel,
        "near",
        [((quarter, 4 * half), BF)],
        where,
        [Far(w_in, quarter_of, quarter), Far(w_out, quarter_of, quarter)],
    )[0]
    in_local, out_local, long_half, short_half = run(
        local_kernel,
        "local",
        [((rows, 3 * half), BF), ((rows, half), BF), ((owned, half), BF), ((part, half), BF)],
        where,
        [w_in, w_out, kernel_long, kernel_short],
        after=(near,),
    )
    all_near = [z_rot(near, k) for k in range(1, nz)]

    gain_one = norm1_gain[None]
    gain_two = norm2_gain[None]
    cot_low = run(low_kernel, "cot_low", [((tokens, width), BF)], where, [Far(cotangent)], after=(near,))[0]
    cots = [cot_low] + [chip_swap(cot_low, m) for m in (1, 2, 3)]
    normed = run(
        first_norm_kernel,
        "first_norm",
        [((tokens, width), BF)],
        where,
        [Far(inputs), gain_one],
        after=(cot_low,),
    )[0]
    normed_other = core_swap(normed)
    in_stack = run(
        hand_on_kernel,
        "hand_on",
        [((3, quarter, 4 * half), BF)],
        where,
        all_near,
    )[0]
    mlp_piece = run(
        feed_pick_kernel,
        "feed_pick",
        [((taken, width), BF)],
        where,
        [w_gate_up, w_down],
        after=(near,),
    )[0]
    in_far = [chip_swap(in_stack, m) for m in (1, 2, 3)]
    mlp_got = lax.all_gather(mlp_piece, "freq", axis=0)

    marks = jnp.concatenate([group[:, None], lens], axis=1).astype(jnp.int32)
    marks_other = core_swap(marks)
    lane = half // nz

    def channels(x):
        own = jnp.where(core == 0, x[:, :half], x[:, half:])
        picked = sum(
            jnp.where(z == i, own[:, i * lane : (i + 1) * lane], 0.0) for i in range(nz)
        )
        return jnp.concatenate([picked] * 4, axis=1)

    gain_lanes = channels(cond_gain[None])
    taps = channels(conv_weight)
    long = jnp.asarray(cosine_table(length), BF)
    long_t = jnp.asarray(cosine_table(length).T, BF)
    short = jnp.asarray(cosine_table(SHORT_LENGTH), BF)
    short_t = jnp.asarray(cosine_table(SHORT_LENGTH).T, BF)

    many = 2 * tokens
    block = (owned + part) // 4
    filler = -block % 16 + block
    piece = ((owned, half), BF)
    *sends, w_in_half, outer, left, right = run(
        project_kernel,
        "project",
        [((owned + filler, half), BF, HBM)]
        + [((owned + filler, half), BF)] * 3
        + [((width, 3 * half), BF, HBM), ((many, half), F32, HBM)]
        + [((many, half), BF, HBM)] * 2,
        where,
        [marks, marks_other, normed, normed_other, in_local, *all_near, *in_far, long_half, short_half],
        [
            pltpu.VMEM((many, half), BF),
            pltpu.VMEM((nz, owned, half), BF),
            pltpu.VMEM((nz, filler, half), F32),
        ],
    )
    came = own_far(sends)
    full = (length, half)
    *sends, vals, spectrum, cond_spec, base = run(
        fold_kernel,
        "fold",
        [(*piece, HBM)] + [piece] * 3 + [(full, BF, HBM), (full, F32, HBM), (full, F32, HBM), (full, BF, HBM)],
        where,
        [marks, marks_other, *came, long, long_t, short, short_t, gain_lanes, taps],
        [
            pltpu.VMEM((length, lane), F32),
            pltpu.VMEM((part * nz, lane), F32),
            pltpu.VMEM(full, BF),
        ],
        after=cots[1:3],
    )
    came = own_far(sends)
    w_keep, w_send = run(
        out_rows_kernel,
        "out_rows",
        [((half, half), BF, HBM), ((half, half), BF)],
        where,
        [out_local, *all_near, *in_far],
        [pltpu.VMEM((width, half), BF)],
        after=(sends[0],),
    )
    w_gu, w_dn = run(
        feed_place_kernel,
        "feed_place",
        [((2, width, width), BF, VMEM), ((2, half, width), BF, VMEM)],
        where,
        [mlp_got, core_swap(mlp_got)],
    )
    part_own, part_other, conv, mixed, w_out_rows = run(
        mix_kernel,
        "mix",
        [((tokens, width), F32), ((tokens, width), BF), ((many, half), BF, HBM)]
        + [((many, half), BF), ((half, width), BF, HBM)],
        where,
        [Far(outer), *came, Far(w_keep), core_swap(w_send)],
        [pltpu.VMEM((nz, owned, half), BF)],
        after=(cots[3],),
    )
    normed_two, residual = run(
        second_kernel,
        "second_norm",
        [((tokens, width), BF), ((tokens, width), F32, HBM)],
        where,
        [Far(inputs), part_own, core_swap(part_other), gain_two],
    )

    arrived = near_by(normed_two)
    acts, grads_gu, sums, layers = [None] * 4, [None] * 4, [None] * 4, [None] * 4
    order = ()
    for m in range(4):
        grad, layer, act, grad_gu = run(
            feed_kernel,
            "feed",
            [
                ((tokens, width), BF if m else F32),
                ((tokens, width), BF if m else F32),
                ((tokens, width), BF, VMEM),
                ((tokens, 2 * width), BF, VMEM),
            ],
            where,
            [arrived[m], cots[m], Held(w_gu), Held(w_dn)],
            after=order,
        )
        order = (grad,)
        acts[m], grads_gu[m], sums[m], layers[m] = Held(act), Held(grad_gu), grad, layer
    backs = [chip_swap(sums[m], m) for m in (1, 2, 3)]

    mlp_send, mlp_keep = run(
        feed_weight_kernel,
        "feed_weights",
        [((nz, taken, width), BF), ((nz, taken, width), BF, VMEM)],
        where,
        [*acts, *grads_gu, *arrived, *cots],
    )
    mlp_grads = run(
        add_kernel,
        "add",
        [((nz, taken, width), BF)],
        where,
        [Held(mlp_keep), core_swap(mlp_send)],
    )[0]
    mlp_share = lax.psum_scatter(mlp_grads, "freq", scatter_dimension=0, tiled=False)
    grad_mix, grad_gain_two, grad_residual = run(
        second_back_kernel,
        "second_norm_back",
        [((tokens, width), BF), ((1, width), F32), ((tokens, width), F32, HBM)],
        where,
        [Far(residual), gain_two, Far(cotangent), sums[0], *backs],
        after=(mlp_grads,),
    )
    grad_mix_other = core_swap(grad_mix)
    *got, grad_outer = run(
        mix_back_kernel,
        "mix_back",
        [(*piece, HBM)] + [piece] * 3 + [((many, half), BF, HBM)],
        where,
        [grad_mix, grad_mix_other, Far(w_out_rows), Far(outer), Far(conv)],
        [pltpu.VMEM((many, half), BF), pltpu.VMEM((nz, owned, half), BF)],
    )
    came = own_far(got)
    early_all = exchanged(
        run(
            early_kernel,
            "early_weights",
            [((rows, width), BF)] * 4,
            where,
            [
                normed,
                normed_other,
                Far(grad_outer),
                mixed,
                core_swap(mixed),
                grad_mix,
                grad_mix_other,
            ],
            [pltpu.VMEM((width, width), BF)],
        )
    )

    layer_far = [chip_swap(layers[m], m) for m in (1, 2, 3)]

    size = -(-(length + SHORT_LENGTH + 4) // (16 * width // lane)) * 16
    *sends, filt = run(
        fold_back_kernel,
        "fold_back",
        [(*piece, HBM)] + [piece] * 3 + [((size, width), BF)],
        where,
        [
            marks,
            marks_other,
            *came,
            long,
            short,
            Far(spectrum),
            Far(cond_spec),
            Far(base),
            gain_lanes,
            taps,
            Far(vals),
            long_t,
            short_t,
        ],
        [pltpu.VMEM(full, BF)],
        after=layer_far[:2],
    )
    came = own_far(sends)
    *parts, late = run(
        late_kernel,
        "late_weights",
        [((rows, width), BF)] * 4 + [((many, width), BF)],
        where,
        [
            marks,
            marks_other,
            *came,
            Far(left),
            Far(right),
            normed,
            normed_other,
        ],
        [
            pltpu.VMEM((many, half), BF),
            pltpu.VMEM((nz, owned, half), BF),
            pltpu.VMEM((width, width), BF),
        ],
        after=(*early_all[1:], mlp_share),
    )
    own, other = run(
        first_grad_kernel,
        "first_grad",
        [((tokens, width), F32), ((tokens, width), BF)],
        where,
        [Far(grad_outer), late, Far(w_in_half)],
    )
    grad_gain_one, grad_inputs = run(
        first_back_kernel,
        "first_norm_back",
        [((1, width), F32), ((owned, slots, width), F32, HBM)],
        where,
        [Far(inputs), gain_one, Far(grad_residual), own, core_swap(other)],
    )
    mlp_sum = lax.all_gather(over_groups(mlp_share), "dp", axis=0, axis_index_groups=blocks)
    late_sends = run(
        late_share_kernel,
        "late_share",
        [((2 * quarter + RIDE, width), BF)] * 4,
        where,
        [
            *exchanged(parts),
            early_all[0],
            *[Far(x) for x in early_all[1:]],
            grad_gain_one,
            grad_gain_two,
        ],
        [pltpu.VMEM((rows, width), BF)] * 2,
    )
    late_piece, filt = run(
        late_sum_kernel,
        "late_sum",
        [((2 * quarter + RIDE, width), BF), ((size, width), BF)],
        where,
        [*z_swap(late_sends), *near_by(over_groups(filt))],
    )
    grad_w_gate_up, grad_w_down = run(
        feed_order_kernel,
        "feed_order",
        [((rows, 2 * hidden), F32, HBM), ((per_z, width), F32, HBM)],
        where,
        [Far(mlp_sum)],
        after=(late_piece,),
    )
    gathered = run(
        gather_kernel,
        "gather",
        [((2 * rows + RIDE + nz * size, width), BF)],
        where,
        [*near_by(over_groups(late_piece)), *z_swap([filt] * nz)],
        after=(layer_far[2], grad_w_down),
    )[0]
    layer_out = run(
        layer_out_kernel,
        "layer_out",
        [((owned, slots, width), F32, HBM)],
        where,
        [Far(residual), Far(layers[0]), *[Far(x) for x in layer_far]],
    )[0]
    grad_w_in, grad_w_out, grad_long, grad_short, grad_cond, grad_taps, grad_one, grad_two = run(
        last_kernel,
        "last",
        [
            ((rows, 3 * width), F32),
            ((rows, width), F32),
            ((length, width), F32),
            ((SHORT_LENGTH, width), F32),
            ((width,), F32),
            ((3, width), F32),
            ((width,), F32),
            ((width,), F32),
        ],
        where,
        [gathered, core_swap(gathered)],
    )

    return (
        layer_out,
        grad_inputs,
        grad_one,
        grad_w_in,
        grad_long,
        grad_short,
        grad_taps,
        grad_cond,
        grad_w_out,
        grad_two,
        grad_w_gate_up,
        grad_w_down,
    )


def solution(mesh):
    return jax.shard_map(
        body,
        mesh=mesh,
        in_specs=(
            P("freq", "dp", None),
            P("freq", "dp", None),
            P("dp"),
            P("dp", None),
            P(),
            P("freq", None),
            P("freq", None),
            P("freq", None),
            P(),
            P(),
            P("freq", None),
            P(),
            P("freq", None),
            P("freq", None),
        ),
        out_specs=(
            P("freq", "dp", None),
            P("freq", "dp", None),
            P(),
            P("freq", None),
            P(),
            P(),
            P(),
            P(),
            P("freq", None),
            P(),
            P("freq", None),
            P("freq", None),
        ),
        check_vma=False,
    )
```

```python
import math

import jax
import jax.numpy as jnp
import numpy as np
from jax import lax
from jax.experimental import pallas as pl
from jax.experimental.pallas import tpu as pltpu
from jax.sharding import PartitionSpec as P

SHORT_LENGTH = 128
EPSILON = 1e-05
BF = jnp.bfloat16
F32 = jnp.float32
GROUP = 8
RIDE = 16
COSTS = {
    "early_weights": 0,
    "near": 3,
    "first_norm": 3,
    "hand_on": 15,
    "project": 25,
    "fold": 20,
    "out_rows": 2,
    "mix": 15,
    "second_norm": 4,
    "feed": 5,
    "feed_place": 3,
    "down": 4,
    "feed_weights": 8,
    "second_norm_back": 12,
    "mix_back": 6,
    "fold_back": 10,
    "early_share": 1,
    "late_weights": 45,
    "first_grad": 0,
    "first_norm_back": 0,
    "late_share": 10,
    "late_sum": 10,
    "gather": 10,
    "last": 6,
    "feed_order": 4,
}
VMEM, HBM = pltpu.VMEM, pltpu.HBM
GELU_A = math.sqrt(2.0 / math.pi)
GELU_B = 0.044715


def cosine_table(length):
    freq = np.arange(length)[:, None]
    posit = np.arange(length)[None, :]
    phase = (2 * posit + 1) * freq % (4 * length)
    weight = np.where(freq == 0, 1.0, 2.0) / length
    return (np.cos(phase * (math.pi / (2 * length))) * np.sqrt(weight)).astype(np.float32)


def dot(a, b):
    return lax.dot_general(a, b, (((1,), (0,)), ((), ())), preferred_element_type=F32)


def dot_nt(a, b):
    return lax.dot_general(a, b, (((1,), (1,)), ((), ())), preferred_element_type=F32)


def dot_tn(a, b):
    return lax.dot_general(a, b, (((0,), (0,)), ((), ())), preferred_element_type=F32)


def norm_parts(values):
    center = values - jnp.mean(values, axis=-1, keepdims=True)
    spread = jnp.mean(center * center, axis=-1, keepdims=True)
    inv = lax.rsqrt(spread + EPSILON)
    return center * inv, inv


def norm_pull(hat, inv, gain, grad):
    scaled = grad * gain
    mean_one = jnp.mean(scaled, axis=-1, keepdims=True)
    mean_two = jnp.mean(scaled * hat, axis=-1, keepdims=True)
    return inv * (scaled - mean_one - hat * mean_two), jnp.sum(grad * hat, axis=0, keepdims=True)


def pick(stacked, index):
    return lax.dynamic_index_in_dim(stacked, index, axis=0, keepdims=False)


class Far:
    def __init__(self, array, start=None, size=None):
        self.array = pltpu.with_memory_space_constraint(array, pltpu.HBM)
        self.start = start
        self.shape = array.shape if start is None else (size, *array.shape[1:])

    def source(self, ref, where):
        return ref if self.start is None else ref.at[rows_at(self.start(where), self.shape[0])]


class Held:
    def __init__(self, array):
        self.array = pltpu.with_memory_space_constraint(array, pltpu.VMEM)


class Fetched:
    def __init__(self, ref, copy):
        self.ref, self.copy, self.shape = ref, copy, ref.shape

    def ready(self):
        if self.copy is not None:
            self.copy.wait()
            self.copy = None
        return self.ref

    def __getitem__(self, place):
        return self.ready()[place]

    @property
    def at(self):
        return self.ready().at


class Kept:
    def __init__(self, ref, copy):
        self.ref, self.copy, self.shape, self.dtype = ref, copy, ref.shape, ref.dtype
        self.started = False

    def __getitem__(self, place):
        return self.ref[place]

    def __setitem__(self, place, value):
        self.ref[place] = value

    def flush(self):
        if not self.started:
            self.copy.start()
            self.started = True


def run(kernel, name, outs, where, ins, scratch=(), after=()):
    arrays = [x.array if isinstance(x, (Far, Held)) else x for x in ins]
    far_in = [isinstance(x, Far) for x in ins]
    far_out = [o[2:] == (HBM,) for o in outs]
    shapes = [o[2](*o[:2]) if len(o) > 2 else jax.ShapeDtypeStruct(*o) for o in outs]
    outs = [o[:2] for o in outs]
    after = [x.array if isinstance(x, Far) else x for x in after]
    n_in, n_after, n_out, n_scratch = len(ins), len(after), len(outs), len(scratch)
    buffers = [pltpu.VMEM(x.shape, x.array.dtype) for x in ins if isinstance(x, Far)]
    buffers += [pltpu.VMEM(s, t) for (s, t), far in zip(outs, far_out) if far]

    def wrapped(*refs):
        where_ref, in_refs = refs[0], list(refs[1 : 1 + n_in])
        rest = list(refs[1 + n_in + n_after :])
        out_refs, rest = rest[:n_out], rest[n_out:]
        own, held = rest[:n_scratch], rest[n_scratch:]
        if not buffers:
            kernel(where_ref, *in_refs, *out_refs, *own)
            return
        held, sems = held[:-1], held[-1]
        number = 0
        for i in range(n_in):
            if far_in[i]:
                source = ins[i].source(in_refs[i], where_ref)
                copy = pltpu.make_async_copy(source, held[number], sems.at[number])
                copy.start()
                in_refs[i] = Fetched(held[number], copy)
                number += 1
        kept = []
        for i in range(n_out):
            if far_out[i]:
                copy = pltpu.make_async_copy(held[number], out_refs[i], sems.at[number])
                out_refs[i] = Kept(held[number], copy)
                kept.append(out_refs[i])
                number += 1
        kernel(where_ref, *in_refs, *out_refs, *own)
        for ref in kept:
            ref.flush()
        for ref in kept:
            ref.copy.wait()
        for ref in in_refs:
            if isinstance(ref, Fetched):
                ref.ready()

    size = sum(x.size * x.dtype.itemsize for x in arrays)
    size += sum(math.prod(s) * jnp.dtype(t).itemsize for s, t in outs)
    far = pl.BlockSpec(memory_space=pltpu.HBM)
    near = pl.BlockSpec(memory_space=pltpu.VMEM)
    small = pl.BlockSpec(memory_space=pltpu.SMEM)
    return pl.pallas_call(
        wrapped,
        out_shape=shapes,
        in_specs=[small]
        + [far if f else small if x.dtype == jnp.int32 else near for x, f in zip(arrays, far_in)]
        + [pl.BlockSpec(memory_space=pl.ANY)] * n_after,
        out_specs=[far if f else near for f in far_out],
        scratch_shapes=list(scratch)
        + buffers
        + ([pltpu.SemaphoreType.DMA((len(buffers),))] if buffers else []),
        compiler_params=pltpu.CompilerParams(vmem_limit_bytes=24 * 2**20),
        cost_estimate=pl.CostEstimate(
            flops=int(COSTS.get(name, 1) * 1.15e9),
            bytes_accessed=int(size) if COSTS.get(name, 1) else 0,
            transcendentals=0,
        ),
        name=name,
    )(where, *arrays, *after)


def rows_at(index, size):
    return pl.ds(pl.multiple_of(index * size, 16), size)


def first_norm_kernel(where, x, gain, normed):
    owned = x.shape[0]
    for s in range(x.shape[1]):
        hat, _ = norm_parts(x[:, s, :])
        normed[pl.ds(s * owned, owned), :] = (hat * gain[...]).astype(BF)


def low_kernel(where, x, out):
    owned = x.shape[0]
    for s in range(x.shape[1]):
        out[pl.ds(s * owned, owned), :] = x[:, s, :].astype(BF)


def near_kernel(where, w_in, w_out, near):
    core = where[2]
    half = w_out.shape[1] // 2
    for i, ref in enumerate((w_in, w_in, w_in, w_out)):
        at = i % 3 * 2 * half
        near[:, i * half : (i + 1) * half] = jnp.where(
            core == 0, ref[:, at : at + half], ref[:, at + half : at + 2 * half]
        )


def local_kernel(where, w_in, w_out, long, short, local, out_local, long_half, short_half):
    core = where[2]
    width = w_out.shape[1]
    half = width // 2

    def mine(x, start):
        return jnp.where(core == 0, x[:, start : start + half], x[:, start + half : start + width])

    for i in range(3):
        local[:, i * half : (i + 1) * half] = mine(w_in, i * width)
    out_local[...] = mine(w_out, 0)
    long_half[...] = mine(long, 0)
    short_half[...] = mine(short, 0)


def hand_on_kernel(where, n1, n2, n3, stack):
    for k, near in enumerate((n1, n2, n3)):
        stack[k] = near[...]


def feed_pick_kernel(where, w_gate_up, w_down, mlp):
    z, chip, core = where[0], where[1], where[2]
    rows = w_gate_up.shape[0]
    hidden = w_gate_up.shape[1] // 2
    per_z = w_down.shape[0]
    chunk = per_z // 6
    member = 2 * chip + core
    for side in range(2):
        for i in range(3):
            zz = i + (i >= chip).astype(jnp.int32)
            c = jnp.where(member < 2 * zz, member, member - 2)
            start = pl.multiple_of(side * hidden + zz * per_z + c * chunk, 128)
            to = (side * 3 + i) * chunk
            mlp[pl.ds(0, rows), to : to + chunk] = w_gate_up[:, pl.ds(start, chunk)]
    c = jnp.clip(jnp.where(member < 2 * z, member, member - 2), 0, 5)
    mlp[pl.ds(rows, chunk), :] = w_down[rows_at(c, chunk), :]


def valid_rows(marks, s, z, owned):
    total = marks[s, 1] + marks[s, 2] + marks[s, 3] + marks[s, 4]
    return jnp.where(marks[s, 0] == 1, marks[s, 1 + z], total - owned * z)


def split_channels(whole, packs):
    count, owned, lanes = packs.shape
    part = lanes // count
    for there in range(count):
        for s in range(count):
            packs[there, :, s * part : (s + 1) * part] = whole[
                s * owned : (s + 1) * owned, there * part : (there + 1) * part
            ]


def join_channels(z, pieces, packs, whole):
    count, owned, lanes = packs.shape
    part = lanes // count
    for k, piece in enumerate(pieces):
        packs[(z - k) & 3] = piece[...]
    for there in range(count):
        for s in range(count):
            whole[s * owned : (s + 1) * owned, there * part : (there + 1) * part] = packs[
                there, :, s * part : (s + 1) * part
            ]


def project_kernel(where, marks_own, marks_other, na, nb, local, n1, n2, n3, c1, c2, c3, long_in, short_in, v0, v1, v2, v3, w, outer, left, right, vals, packs, folds):
    z, chip = where[0], where[1]
    rows = local.shape[0]
    quarter = rows // 4
    half = outer.shape[1]
    wide = 3 * half
    w[rows_at(z, rows), :] = local[...]
    for k, near in ((1, n1), (2, n2), (3, n3)):
        base = ((z - k) & 3) * 4
        w[rows_at(base + chip, quarter), :] = near[:, :wide]
        for m, far in ((1, c1), (2, c2), (3, c3)):
            w[rows_at(base + (chip ^ m), quarter), :] = far[k - 1, :, :wide]
    w.flush()
    owned = packs.shape[1]
    count = na.shape[0]
    place = lax.broadcasted_iota(jnp.int32, (owned, half), 0)
    for i, (tokens, marks) in enumerate(((na, marks_own), (nb, marks_other))):
        at = pl.ds(i * count, count)
        full = dot(tokens[...], w[...])
        a, b, c = full[:, :half], full[:, half : 2 * half], full[:, 2 * half :]
        outer[at, :] = a
        left[at, :] = b.astype(BF)
        right[at, :] = c.astype(BF)
        for s in range(count // owned):
            valid = valid_rows(marks, s, z, owned)
            low = slice(s * owned, (s + 1) * owned)
            vals[pl.ds(i * count + s * owned, owned), :] = jnp.where(
                place < valid, b[low] * c[low], 0.0
            ).astype(BF)
    for ref in (outer, left, right):
        ref.flush()
    split_channels(vals, packs)
    part = half // 4
    block = (long_in.shape[0] + short_in.shape[0]) // 4
    folds[...] = jnp.zeros(folds.shape, F32)
    for there in range(4):
        lanes = slice(there * part, (there + 1) * part)
        both = jnp.concatenate([long_in[:, lanes], short_in[:, lanes]], axis=0).astype(F32)
        for g in range(4):
            folds[there, pl.ds(0, block), g * part : (g + 1) * part] = both[g * block : (g + 1) * block]
    for k, out in enumerate((v0, v1, v2, v3)):
        out[pl.ds(0, owned), :] = packs[(z + k) & 3]
        rest = out.shape[0] - owned
        out[pl.ds(owned, rest), :] = folds[(z + k) & 3].astype(BF)


def short_lanes(marks_own, marks_other, shape):
    part = shape[1] // 4
    slot = lax.broadcasted_iota(jnp.int32, shape, 1) // part
    groups = [marks_own[0, 0], marks_own[1, 0], marks_other[0, 0], marks_other[1, 0]]
    return sum(jnp.where(slot == s, group, 0) for s, group in enumerate(groups)) == 1


def neighbours(x, short):
    length = x.shape[0]
    place = lax.broadcasted_iota(jnp.int32, x.shape, 0)
    starts = (place == 0) | (short & (place % SHORT_LENGTH == 0))
    ends = (place == length - 1) | (short & (place % SHORT_LENGTH == SHORT_LENGTH - 1))
    earlier = jnp.where(starts, 0.0, pltpu.roll(x, 1, 0))
    later = jnp.where(ends, 0.0, pltpu.roll(x, length - 1, 0))
    return earlier, later


def both_tables(long, short, x, mask):
    whole = dot(long[...], x)
    parts = [
        dot(short[...], x[i * SHORT_LENGTH : (i + 1) * SHORT_LENGTH])
        for i in range(x.shape[0] // SHORT_LENGTH)
    ]
    return jnp.where(mask, jnp.concatenate(parts, axis=0), whole)


def fold_kernel(where, marks_own, marks_other, v0, r1, r2, r3, long, long_t, short, short_t, gain, taps, o0, o1, o2, o3, vals, spectrum, cond_spec, base, low_base, low_short, conv):
    z = where[0]
    length, half = vals.shape
    owned = length // 4
    part = half // 4
    block = (owned + SHORT_LENGTH // 4) // 4
    for k, piece in enumerate((v0, r1, r2, r3)):
        there = (z - k) & 3
        vals[rows_at(there, owned), :] = piece[pl.ds(0, owned), :]
        got = piece[pl.ds(owned, block), :].astype(F32)
        got = jnp.concatenate([got[:, g * part : (g + 1) * part] for g in range(4)], axis=0)
        low_base[rows_at(there, owned), :] = got[:owned]
        low_short[rows_at(there, SHORT_LENGTH // 4), :] = got[owned:]
    vals.flush()
    mask = short_lanes(marks_own, marks_other, (length, half))
    tall = jnp.concatenate([low_short[...]] * (length // SHORT_LENGTH), axis=0)
    base[...] = jnp.where(
        mask, jnp.concatenate([tall] * 4, axis=1), jnp.concatenate([low_base[...]] * 4, axis=1)
    ).astype(BF)
    base.flush()
    wide = vals[...].astype(F32)
    before, after = neighbours(wide, mask)
    cond = taps[0:1, :] * before + taps[1:2, :] * wide + taps[2:3, :] * after
    high = cond.astype(BF)
    low = (cond - high.astype(F32)).astype(BF)
    spec = both_tables(long, short, vals[...], mask)
    spectrum[...] = spec
    spectrum.flush()
    cspec = both_tables(long, short, high, mask) + both_tables(long, short, low, mask)
    cond_spec[...] = cspec
    cond_spec.flush()
    kern = base[...].astype(F32) + gain[...] * (jnp.sqrt(cspec * cspec + 1.0) - 1.0)
    filtered = (kern * spec).astype(BF)
    conv[...] = both_tables(long_t, short_t, filtered, mask).astype(BF)
    for k, out in enumerate((o0, o1, o2, o3)):
        out[...] = conv[rows_at((z + k) & 3, owned), :]


def out_rows_kernel(where, local, n1, n2, n3, c1, c2, c3, keep, send, whole):
    z, chip, core = where[0], where[1], where[2]
    rows, half = local.shape
    quarter = rows // 4
    wide = 3 * half
    whole[rows_at(z, rows), :] = local[...]
    for k, near in ((1, n1), (2, n2), (3, n3)):
        base = ((z - k) & 3) * 4
        whole[rows_at(base + chip, quarter), :] = near[:, wide:]
        for m, far in ((1, c1), (2, c2), (3, c3)):
            whole[rows_at(base + (chip ^ m), quarter), :] = far[k - 1, :, wide:]
    keep[...] = whole[rows_at(core, half), :]
    send[...] = whole[rows_at(1 - core, half), :]


def mix_kernel(where, outer, c0, r1, r2, r3, w_keep, w_came, own, other, conv, mixed, w_rows, packs):
    z, core = where[0], where[2]
    half = outer.shape[1]
    w_rows[:, :half] = jnp.where(core == 0, w_keep[...], w_came[...])
    w_rows[:, half:] = jnp.where(core == 0, w_came[...], w_keep[...])
    w_rows.flush()
    join_channels(z, (c0, r1, r2, r3), packs, conv)
    conv.flush()
    mixed[...] = (outer[...] * conv[...].astype(F32)).astype(BF)
    count = own.shape[0]
    other[...] = dot(mixed[pl.ds(count, count), :], w_rows[...]).astype(BF)
    own[...] = dot(mixed[pl.ds(0, count), :], w_rows[...])


def second_kernel(where, x, own, came, gain, normed, residual):
    owned = x.shape[0]
    for s in range(x.shape[1]):
        at = pl.ds(s * owned, owned)
        total = x[:, s, :] + own[at, :] + came[at, :].astype(F32)
        residual[at, :] = total
        hat, _ = norm_parts(total)
        normed[at, :] = (hat * gain[...]).astype(BF)


def feed_place_kernel(where, own, other, w_gu, w_dn):
    chip = where[1]
    rows = w_gu.shape[1] // 4
    chunk = own.shape[1] - rows
    for p, part in enumerate((own, other)):
        for i in range(4):
            w_gu[p, pl.ds(i * rows, rows), :] = part[i, pl.ds(0, rows), :]
        for i in range(3):
            at = i + (i >= chip).astype(jnp.int32)
            w_dn[p, pl.ds(i * chunk, chunk), :] = part[at, pl.ds(rows, chunk), :]


def feed_kernel(where, second, cot, w_gu, w_dn, out, layer, act, grads):
    half = w_dn.shape[1]
    width = second.shape[1]
    for p in range(2):
        gate_up = dot(second[...], w_gu[p])
        gate, upward = gate_up[:, :half], gate_up[:, half:]
        grad_act = dot_nt(cot[...], w_dn[p])
        square = gate * gate
        tanh = jnp.tanh(GELU_A * gate * (1.0 + GELU_B * square))
        cdf = 0.5 * (1.0 + tanh)
        unit = gate * cdf
        slope = cdf + 0.5 * gate * (1.0 - tanh * tanh) * (GELU_A * (1.0 + 3.0 * GELU_B * square))
        act[:, p * half : (p + 1) * half] = (unit * upward).astype(BF)
        grads[:, p * width : p * width + half] = (grad_act * upward * slope).astype(BF)
        grads[:, p * width + half : (p + 1) * width] = (grad_act * unit).astype(BF)
    total = dot_nt(grads[:, :width], w_gu[0]) + dot_nt(grads[:, width:], w_gu[1])
    out[...] = total.astype(out.dtype)
    total = dot(act[:, :half], w_dn[0]) + dot(act[:, half:], w_dn[1])
    layer[...] = total.astype(layer.dtype)


def feed_weight_kernel(where, a0, a1, a2, a3, g0, g1, g2, g3, s0, s1, s2, s3, c0, c1, c2, c3, send, keep):
    chip = where[1]
    width = s0.shape[1]
    half = width // 2
    nz, piece, _ = keep.shape
    chunk = half // 3
    rows = piece - chunk
    for p, out in ((1, send), (0, keep)):
        total = None
        for s, g in ((s0, g0), (s1, g1), (s2, g2), (s3, g3)):
            part = dot_tn(s[...], g[:, p * width : (p + 1) * width])
            total = part if total is None else total + part
        for i in range(nz):
            out[i, pl.ds(0, rows), :] = total[i * rows : (i + 1) * rows].astype(BF)
        down = None
        for a, c in ((a0, c0), (a1, c1), (a2, c2), (a3, c3)):
            part = dot_tn(a[:, p * half : (p + 1) * half], c[...])
            down = part if down is None else down + part
        out[chip, pl.ds(rows, chunk), :] = jnp.zeros((chunk, width), BF)
        for i in range(3):
            to = i + (i >= chip).astype(jnp.int32)
            out[to, pl.ds(rows, chunk), :] = down[i * chunk : (i + 1) * chunk].astype(BF)


def add_kernel(where, a, b, out):
    out[...] = (a[...].astype(F32) + b[...].astype(F32)).astype(BF)


def layer_out_kernel(where, residual, own, r1, r2, r3, out):
    owned = out.shape[0]
    for s in range(out.shape[1]):
        at = pl.ds(s * owned, owned)
        out[:, s, :] = residual[at, :] + added([x.at[at] for x in (own, r1, r2, r3)])


def second_back_kernel(where, residual, gain, cot, own, r1, r2, r3, low, grad_gain, grad_residual):
    owned = cot.shape[0]
    grad = own[...] + r1[...].astype(F32) + r2[...].astype(F32) + r3[...].astype(F32)
    hat, inv = norm_parts(residual[...])
    pulled, grad_gain[...] = norm_pull(hat, inv, gain[...], grad)
    for s in range(cot.shape[1]):
        at = pl.ds(s * owned, owned)
        total = cot[:, s, :] + pulled[s * owned : (s + 1) * owned]
        grad_residual[at, :] = total
        low[at, :] = total.astype(BF)


def write_pieces(whole, outs, chip):
    rows = whole.shape[0] // 4
    quarter = rows // 4
    for m, out in enumerate(outs):
        for i in range(4):
            out[pl.ds(i * quarter, quarter), :] = whole[rows_at(i * 4 + (chip ^ m), quarter), :]


def mix_back_kernel(where, ga, gb, w_rows, outer, conv, o0, o1, o2, o3, grad_outer, grad_conv, packs):
    z = where[0]
    count = ga.shape[0]
    half = outer.shape[1]
    for i, grad in enumerate((ga, gb)):
        at = pl.ds(i * count, count)
        grad_mixed = dot_nt(grad[...], w_rows[...])
        grad_outer[at, :] = (grad_mixed * conv[at, :].astype(F32)).astype(BF)
        grad_conv[at, :] = (grad_mixed * outer[at, :]).astype(BF)
    grad_outer.flush()
    split_channels(grad_conv, packs)
    for k, out in enumerate((o0, o1, o2, o3)):
        out[...] = packs[(z + k) & 3]


def early_kernel(where, na, nb, grad_outer, mixed, other_mixed, ga, gb, p0, p1, p2, p3, whole):
    chip, core = where[1], where[2]
    count, half = na.shape[0], mixed.shape[1]
    first = jnp.where(core == 0, ga[:, :half], ga[:, half:])
    second = jnp.where(core == 0, gb[:, :half], gb[:, half:])
    mine = dot_tn(mixed[pl.ds(0, count), :], first) + dot_tn(mixed[pl.ds(count, count), :], second)
    theirs = dot_tn(other_mixed[pl.ds(count, count), :], first)
    theirs = theirs + dot_tn(other_mixed[pl.ds(0, count), :], second)
    whole[rows_at(core, half), half:] = mine.astype(BF)
    whole[rows_at(1 - core, half), half:] = theirs.astype(BF)
    total = dot_tn(na[...], grad_outer[pl.ds(0, count), :])
    total = total + dot_tn(nb[...], grad_outer[pl.ds(count, count), :])
    whole[:, :half] = total.astype(BF)
    write_pieces(whole, (p0, p1, p2, p3), chip)


def fold_back_kernel(where, marks_own, marks_other, g0, r1, r2, r3, long, short, spectrum, cond_spec, base, gain, taps, vals, long_t, short_t, o0, o1, o2, o3, filt, grads):
    z = where[0]
    length, half = grads.shape
    owned = length // 4
    part = half // 4
    for k, piece in enumerate((g0, r1, r2, r3)):
        grads[rows_at((z - k) & 3, owned), :] = piece[...]
    mask = short_lanes(marks_own, marks_other, (length, half))
    gf = both_tables(long, short, grads[...], mask)
    cspec = cond_spec[...]
    root = jnp.sqrt(cspec * cspec + 1.0)
    above = root - 1.0
    grad_base = gf * spectrum[...]
    grad_spec = (gf * (base[...].astype(F32) + gain[...] * above)).astype(BF)
    grad_cspec = (grad_base * gain[...] * (cspec / root)).astype(BF)
    grad_cond = both_tables(long_t, short_t, grad_cspec, mask)
    direct = both_tables(long_t, short_t, grad_spec, mask)
    wide = vals[...].astype(F32)
    before, after = neighbours(wide, mask)
    grad_before, grad_after = neighbours(grad_cond, mask)
    grads[...] = (
        direct + taps[0:1, :] * grad_after + taps[1:2, :] * grad_cond + taps[2:3, :] * grad_before
    ).astype(BF)
    for k, out in enumerate((o0, o1, o2, o3)):
        out[...] = grads[rows_at((z + k) & 3, owned), :]

    def over_slots(x):
        return sum(x[:, s * part : (s + 1) * part] for s in range(4))

    shorts = jnp.where(mask, grad_base, 0.0)
    small = [
        jnp.sum(x, axis=0, keepdims=True)
        for x in (grad_base * above, grad_cond * before, grad_cond * wide, grad_cond * after)
    ]
    folded = sum(
        shorts[i * SHORT_LENGTH : (i + 1) * SHORT_LENGTH] for i in range(length // SHORT_LENGTH)
    )
    fill = filt.shape[0] * (filt.shape[1] // part) - length - SHORT_LENGTH - 4
    found = jnp.concatenate(
        [
            over_slots(grad_base - shorts),
            over_slots(folded),
            over_slots(jnp.concatenate(small, axis=0)),
            jnp.zeros((fill, part), F32),
        ],
        axis=0,
    )
    size = filt.shape[0]
    blocks = [found[g * size : (g + 1) * size] for g in range(filt.shape[1] // part)]
    filt[...] = jnp.concatenate(blocks, axis=1).astype(BF)


def late_kernel(where, marks_own, marks_other, g0, r1, r2, r3, left, right, na, nb, p0, p1, p2, p3, late, grads, packs, whole):
    z, chip = where[0], where[1]
    half = left.shape[1]
    owned = packs.shape[1]
    join_channels(z, (g0, r1, r2, r3), packs, grads)
    count = na.shape[0]
    place = lax.broadcasted_iota(jnp.int32, (owned, half), 0)
    for i, marks in enumerate((marks_own, marks_other)):
        for s in range(count // owned):
            at = pl.ds(i * count + s * owned, owned)
            valid = valid_rows(marks, s, z, owned)
            grad = jnp.where(place < valid, grads[at, :].astype(F32), 0.0)
            late[at, :half] = (grad * right[at, :].astype(F32)).astype(BF)
            late[at, half:] = (grad * left[at, :].astype(F32)).astype(BF)
    total = dot_tn(na[...], late[pl.ds(0, count), :]) + dot_tn(nb[...], late[pl.ds(count, count), :])
    whole[...] = total.astype(BF)
    write_pieces(whole, (p0, p1, p2, p3), chip)


def first_grad_kernel(where, grad_outer, late, w, own, other):
    half = grad_outer.shape[1]
    count = own.shape[0]
    for i, out in ((1, other), (0, own)):
        at = pl.ds(i * count, count)
        total = dot_nt(grad_outer[at, :], w[:, :half]) + dot_nt(late[at, :], w[:, half:])
        out[...] = total.astype(out.dtype)


def first_back_kernel(where, x, gain, grad_residual, own, came, grad_gain, grad_inputs):
    owned = x.shape[0]
    riding = None
    for s in range(x.shape[1]):
        at = pl.ds(s * owned, owned)
        hat, inv = norm_parts(x[:, s, :])
        pulled, part = norm_pull(hat, inv, gain[...], own[at, :] + came[at, :].astype(F32))
        grad_inputs[:, s, :] = grad_residual[at, :] + pulled
        riding = part if riding is None else riding + part
    grad_gain[...] = riding


def added(pieces):
    total = pieces[0][...].astype(F32)
    for piece in pieces[1:]:
        total = total + piece[...].astype(F32)
    return total


def late_share_kernel(where, p0, r1, r2, r3, e0, e1, e2, e3, one, two, o0, o1, o2, o3, late, early):
    z = where[0]
    late[...] = added((p0, r1, r2, r3)).astype(BF)
    early[...] = added((e0, e1, e2, e3)).astype(BF)
    quarter = p0.shape[0] // 4
    width = p0.shape[1]
    place = lax.broadcasted_iota(jnp.int32, (RIDE, width), 0)
    extra = jnp.where(place == 0, jnp.broadcast_to(one[...], (RIDE, width)), 0.0)
    extra = jnp.where(place == 1, jnp.broadcast_to(two[...], (RIDE, width)), extra).astype(BF)
    for k, out in enumerate((o0, o1, o2, o3)):
        at = rows_at((z + k) & 3, quarter)
        out[pl.ds(0, quarter), :] = late[at, :]
        out[pl.ds(quarter, quarter), :] = early[at, :]
        out[pl.ds(2 * quarter, RIDE), :] = extra


def late_sum_kernel(where, s0, r1, r2, r3, f0, f1, f2, f3, piece, filt):
    piece[...] = added((s0, r1, r2, r3)).astype(BF)
    filt[...] = added((f0, f1, f2, f3)).astype(BF)


def gather_kernel(where, s0, r1, r2, r3, f0, f1, f2, f3, out):
    z, chip = where[0], where[1]
    quarter = (s0.shape[0] - RIDE) // 2
    parts = (s0, r1, r2, r3)
    for m, piece in enumerate(parts):
        for i in range(2):
            out[rows_at(i * 4 + (chip ^ m), quarter), :] = piece[pl.ds(i * quarter, quarter), :]
    riding = added([piece[pl.ds(2 * quarter, RIDE), :] for piece in parts])
    top = 8 * quarter
    out[pl.ds(top, RIDE), :] = riding.astype(BF)
    step = f0.shape[0]
    for k, piece in enumerate((f0, f1, f2, f3)):
        at = top + RIDE + ((z - k) & 3) * step
        out[pl.ds(pl.multiple_of(at, 16), step), :] = piece[...]


def feed_order_kernel(where, shares, gate_up, down):
    z = where[0]
    rows = gate_up.shape[0]
    chunk = shares.shape[1] - rows
    per_z = 6 * chunk
    for side in range(2):
        for zz in range(4):
            for c in range(6):
                mm = c if c < 2 * zz else c + 2
                at = (side * 3 + zz - (zz > mm // 2)) * chunk
                to = side * 4 * per_z + zz * per_z + c * chunk
                gate_up[:, to : to + chunk] = shares[mm, :rows, at : at + chunk].astype(F32)
    for c in range(6):
        mm = c + 2 * (c >= 2 * z).astype(jnp.int32)
        down[pl.ds(c * chunk, chunk), :] = shares[mm, pl.ds(rows, chunk), :].astype(F32)


def last_kernel(where, own, other, w_in, w_out, long, short, gain, taps, norm_one, norm_two):
    core = where[2]
    rows = w_in.shape[0]
    width = w_out.shape[1]
    half = width // 2
    part = half // 4
    top = 2 * rows

    def write(out, to, a, b):
        a, b = a.astype(F32), b.astype(F32)
        out[:, to : to + half] = jnp.where(core == 0, a, b)
        out[:, to + half : to + width] = jnp.where(core == 0, b, a)

    for start, at, to, out in (
        (rows, 0, 0, w_in),
        (0, 0, width, w_in),
        (0, half, 2 * width, w_in),
        (rows, half, 0, w_out),
    ):
        place = (pl.ds(start, rows), slice(at, at + half))
        write(out, to, own[place], other[place])
    place = pl.ds(top, RIDE)
    riding = own[place, :].astype(F32) + other[place, :].astype(F32)
    norm_one[...] = riding[0]
    norm_two[...] = riding[1]
    step = (own.shape[0] - top - RIDE) // 4
    length, count = long.shape[0], short.shape[0]

    def filter_rows(ref):
        got = []
        for there in range(4):
            at = pl.ds(top + RIDE + there * step, step)
            blocks = [ref[at, g * part : (g + 1) * part].astype(F32) for g in range(width // part)]
            got.append(jnp.concatenate(blocks, axis=0))
        return jnp.concatenate(got, axis=1)

    a, b = filter_rows(own), filter_rows(other)
    write(long, 0, a[:length], b[:length])
    write(short, 0, a[length : length + count], b[length : length + count])
    rest = length + count
    a_row, b_row = a[rest], b[rest]
    gain[pl.ds(0, half)] = jnp.where(core == 0, a_row, b_row)
    gain[pl.ds(half, half)] = jnp.where(core == 0, b_row, a_row)
    write(taps, 0, a[rest + 1 : rest + 4], b[rest + 1 : rest + 4])


def body(
    inputs,
    cotangent,
    group,
    lens,
    norm1_gain,
    w_in,
    kernel_long,
    kernel_short,
    conv_weight,
    cond_gain,
    w_out,
    norm2_gain,
    w_gate_up,
    w_down,
):
    nz = lax.axis_size("freq")
    ndp = lax.axis_size("dp")
    z = lax.axis_index("freq")
    d = lax.axis_index("dp")
    core = d % 2
    chip = (d // 2) % 4
    owned, slots, width = inputs.shape
    half = width // 2
    length = owned * nz
    tokens = owned * slots
    rows = w_in.shape[0]
    quarter = rows // 4
    others = ndp // GROUP
    blocks = [[g * GROUP + i for i in range(GROUP)] for g in range(others)]
    same_core = [[g * GROUP + 2 * i + c for i in range(4)] for g in range(others) for c in range(2)]
    across = [[i + GROUP * g for g in range(others)] for i in range(GROUP)]

    def core_swap(x):
        return lax.ppermute(x, "dp", [(i, i ^ 1) for i in range(ndp)])

    def chip_swap(x, m):
        return lax.ppermute(x, "dp", [(i, i ^ (2 * m)) for i in range(ndp)])

    def z_rot(x, k):
        return lax.ppermute(x, "freq", [(i, (i + k) % nz) for i in range(nz)])

    def z_swap(pieces):
        return [pieces[0]] + [z_rot(pieces[k], k) for k in range(1, nz)]

    def own_far(pieces):
        got = z_swap(pieces)
        return [Far(got[0])] + got[1:]

    def near_by(piece):
        return [piece] + [chip_swap(piece, m) for m in (1, 2, 3)]

    def exchanged(parts):
        return [parts[0]] + [chip_swap(parts[m], m) for m in (1, 2, 3)]

    def over_groups(x):
        if others > 1:
            return lax.psum(x, "dp", axis_index_groups=across)
        return x

    where = jnp.stack([z, chip, core, z]).astype(jnp.int32)
    part = kernel_short.shape[0]
    hidden = w_down.shape[0] * nz
    per_z = w_down.shape[0]
    chunk = per_z // 6
    taken = rows + chunk
    quarter_of = lambda place: place[1]
    near = run(
        near_kernel,
        "near",
        [((quarter, 4 * half), BF)],
        where,
        [Far(w_in, quarter_of, quarter), Far(w_out, quarter_of, quarter)],
    )[0]
    in_local, out_local, long_half, short_half = run(
        local_kernel,
        "local",
        [((rows, 3 * half), BF), ((rows, half), BF), ((owned, half), BF), ((part, half), BF)],
        where,
        [w_in, w_out, kernel_long, kernel_short],
        after=(near,),
    )
    all_near = [z_rot(near, k) for k in range(1, nz)]

    gain_one = norm1_gain[None]
    gain_two = norm2_gain[None]
    cot_low = run(low_kernel, "cot_low", [((tokens, width), BF)], where, [Far(cotangent)], after=(near,))[0]
    cots = [cot_low] + [chip_swap(cot_low, m) for m in (1, 2, 3)]
    normed = run(
        first_norm_kernel,
        "first_norm",
        [((tokens, width), BF)],
        where,
        [Far(inputs), gain_one],
        after=(cot_low,),
    )[0]
    normed_other = core_swap(normed)
    in_stack = run(
        hand_on_kernel,
        "hand_on",
        [((3, quarter, 4 * half), BF)],
        where,
        all_near,
    )[0]
    mlp_piece = run(
        feed_pick_kernel,
        "feed_pick",
        [((taken, width), BF)],
        where,
        [w_gate_up, w_down],
        after=(near,),
    )[0]
    in_far = [chip_swap(in_stack, m) for m in (1, 2, 3)]
    mlp_got = lax.all_gather(mlp_piece, "freq", axis=0)

    marks = jnp.concatenate([group[:, None], lens], axis=1).astype(jnp.int32)
    marks_other = core_swap(marks)
    lane = half // nz

    def channels(x):
        own = jnp.where(core == 0, x[:, :half], x[:, half:])
        picked = sum(
            jnp.where(z == i, own[:, i * lane : (i + 1) * lane], 0.0) for i in range(nz)
        )
        return jnp.concatenate([picked] * 4, axis=1)

    gain_lanes = channels(cond_gain[None])
    taps = channels(conv_weight)
    long = jnp.asarray(cosine_table(length), BF)
    long_t = jnp.asarray(cosine_table(length).T, BF)
    short = jnp.asarray(cosine_table(SHORT_LENGTH), BF)
    short_t = jnp.asarray(cosine_table(SHORT_LENGTH).T, BF)

    many = 2 * tokens
    block = (owned + part) // 4
    filler = -block % 16 + block
    piece = ((owned, half), BF)
    *sends, w_in_half, outer, left, right = run(
        project_kernel,
        "project",
        [((owned + filler, half), BF, HBM)]
        + [((owned + filler, half), BF)] * 3
        + [((width, 3 * half), BF, HBM), ((many, half), F32, HBM)]
        + [((many, half), BF, HBM)] * 2,
        where,
        [marks, marks_other, normed, normed_other, in_local, *all_near, *in_far, long_half, short_half],
        [
            pltpu.VMEM((many, half), BF),
            pltpu.VMEM((nz, owned, half), BF),
            pltpu.VMEM((nz, filler, half), F32),
        ],
    )
    came = own_far(sends)
    full = (length, half)
    *sends, vals, spectrum, cond_spec, base = run(
        fold_kernel,
        "fold",
        [(*piece, HBM)] + [piece] * 3 + [(full, BF, HBM), (full, F32, HBM), (full, F32, HBM), (full, BF, HBM)],
        where,
        [marks, marks_other, *came, long, long_t, short, short_t, gain_lanes, taps],
        [
            pltpu.VMEM((length, lane), F32),
            pltpu.VMEM((part * nz, lane), F32),
            pltpu.VMEM(full, BF),
        ],
        after=cots[1:3],
    )
    came = own_far(sends)
    w_keep, w_send = run(
        out_rows_kernel,
        "out_rows",
        [((half, half), BF, HBM), ((half, half), BF)],
        where,
        [out_local, *all_near, *in_far],
        [pltpu.VMEM((width, half), BF)],
        after=(sends[0],),
    )
    w_gu, w_dn = run(
        feed_place_kernel,
        "feed_place",
        [((2, width, width), BF, VMEM), ((2, half, width), BF, VMEM)],
        where,
        [mlp_got, core_swap(mlp_got)],
    )
    part_own, part_other, conv, mixed, w_out_rows = run(
        mix_kernel,
        "mix",
        [((tokens, width), F32), ((tokens, width), BF), ((many, half), BF, HBM)]
        + [((many, half), BF), ((half, width), BF, HBM)],
        where,
        [Far(outer), *came, Far(w_keep), core_swap(w_send)],
        [pltpu.VMEM((nz, owned, half), BF)],
        after=(cots[3],),
    )
    normed_two, residual = run(
        second_kernel,
        "second_norm",
        [((tokens, width), BF), ((tokens, width), F32, HBM)],
        where,
        [Far(inputs), part_own, core_swap(part_other), gain_two],
    )

    arrived = near_by(normed_two)
    acts, grads_gu, sums, layers = [None] * 4, [None] * 4, [None] * 4, [None] * 4
    order = ()
    for m in range(4):
        grad, layer, act, grad_gu = run(
            feed_kernel,
            "feed",
            [
                ((tokens, width), BF if m else F32),
                ((tokens, width), BF if m else F32),
                ((tokens, width), BF, VMEM),
                ((tokens, 2 * width), BF, VMEM),
            ],
            where,
            [arrived[m], cots[m], Held(w_gu), Held(w_dn)],
            after=order,
        )
        order = (grad,)
        acts[m], grads_gu[m], sums[m], layers[m] = Held(act), Held(grad_gu), grad, layer
    backs = [chip_swap(sums[m], m) for m in (1, 2, 3)]

    mlp_send, mlp_keep = run(
        feed_weight_kernel,
        "feed_weights",
        [((nz, taken, width), BF), ((nz, taken, width), BF, VMEM)],
        where,
        [*acts, *grads_gu, *arrived, *cots],
    )
    mlp_grads = run(
        add_kernel,
        "add",
        [((nz, taken, width), BF)],
        where,
        [Held(mlp_keep), core_swap(mlp_send)],
    )[0]
    mlp_share = lax.psum_scatter(mlp_grads, "freq", scatter_dimension=0, tiled=False)
    grad_mix, grad_gain_two, grad_residual = run(
        second_back_kernel,
        "second_norm_back",
        [((tokens, width), BF), ((1, width), F32), ((tokens, width), F32, HBM)],
        where,
        [Far(residual), gain_two, Far(cotangent), sums[0], *backs],
        after=(mlp_grads,),
    )
    grad_mix_other = core_swap(grad_mix)
    *got, grad_outer = run(
        mix_back_kernel,
        "mix_back",
        [(*piece, HBM)] + [piece] * 3 + [((many, half), BF, HBM)],
        where,
        [grad_mix, grad_mix_other, Far(w_out_rows), Far(outer), Far(conv)],
        [pltpu.VMEM((many, half), BF), pltpu.VMEM((nz, owned, half), BF)],
    )
    came = own_far(got)
    early_all = exchanged(
        run(
            early_kernel,
            "early_weights",
            [((rows, width), BF)] * 4,
            where,
            [
                normed,
                normed_other,
                Far(grad_outer),
                mixed,
                core_swap(mixed),
                grad_mix,
                grad_mix_other,
            ],
            [pltpu.VMEM((width, width), BF)],
        )
    )

    layer_far = [chip_swap(layers[m], m) for m in (1, 2, 3)]

    size = -(-(length + SHORT_LENGTH + 4) // (16 * width // lane)) * 16
    *sends, filt = run(
        fold_back_kernel,
        "fold_back",
        [(*piece, HBM)] + [piece] * 3 + [((size, width), BF)],
        where,
        [
            marks,
            marks_other,
            *came,
            long,
            short,
            Far(spectrum),
            Far(cond_spec),
            Far(base),
            gain_lanes,
            taps,
            Far(vals),
            long_t,
            short_t,
        ],
        [pltpu.VMEM(full, BF)],
        after=[Far(x) for x in layer_far],
    )
    came = own_far(sends)
    *parts, late = run(
        late_kernel,
        "late_weights",
        [((rows, width), BF)] * 4 + [((many, width), BF)],
        where,
        [
            marks,
            marks_other,
            *came,
            Far(left),
            Far(right),
            normed,
            normed_other,
        ],
        [
            pltpu.VMEM((many, half), BF),
            pltpu.VMEM((nz, owned, half), BF),
            pltpu.VMEM((width, width), BF),
        ],
        after=[Far(x) for x in (*early_all[1:], mlp_share)],
    )
    own, other = run(
        first_grad_kernel,
        "first_grad",
        [((tokens, width), F32), ((tokens, width), BF)],
        where,
        [Far(grad_outer), late, Far(w_in_half)],
    )
    grad_gain_one, grad_inputs = run(
        first_back_kernel,
        "first_norm_back",
        [((1, width), F32), ((owned, slots, width), F32, HBM)],
        where,
        [Far(inputs), gain_one, Far(grad_residual), own, core_swap(other)],
    )
    mlp_sum = lax.all_gather(over_groups(mlp_share), "dp", axis=0, axis_index_groups=blocks)
    late_sends = run(
        late_share_kernel,
        "late_share",
        [((2 * quarter + RIDE, width), BF)] * 4,
        where,
        [
            *exchanged(parts),
            early_all[0],
            *[Far(x) for x in early_all[1:]],
            grad_gain_one,
            grad_gain_two,
        ],
        [pltpu.VMEM((rows, width), BF)] * 2,
    )
    late_piece, filt = run(
        late_sum_kernel,
        "late_sum",
        [((2 * quarter + RIDE, width), BF), ((size, width), BF)],
        where,
        [*z_swap(late_sends), *near_by(over_groups(filt))],
    )
    grad_w_gate_up, grad_w_down = run(
        feed_order_kernel,
        "feed_order",
        [((rows, 2 * hidden), F32, HBM), ((per_z, width), F32, HBM)],
        where,
        [Far(mlp_sum)],
        after=(late_piece,),
    )
    gathered = run(
        gather_kernel,
        "gather",
        [((2 * rows + RIDE + nz * size, width), BF)],
        where,
        [*near_by(over_groups(late_piece)), *z_swap([filt] * nz)],
        after=[Far(grad_w_down)],
    )[0]
    layer_out = run(
        layer_out_kernel,
        "layer_out",
        [((owned, slots, width), F32, HBM)],
        where,
        [Far(residual), Far(layers[0]), *[Far(x) for x in layer_far]],
    )[0]
    grad_w_in, grad_w_out, grad_long, grad_short, grad_cond, grad_taps, grad_one, grad_two = run(
        last_kernel,
        "last",
        [
            ((rows, 3 * width), F32),
            ((rows, width), F32),
            ((length, width), F32),
            ((SHORT_LENGTH, width), F32),
            ((width,), F32),
            ((3, width), F32),
            ((width,), F32),
            ((width,), F32),
        ],
        where,
        [gathered, core_swap(gathered)],
    )

    return (
        layer_out,
        grad_inputs,
        grad_one,
        grad_w_in,
        grad_long,
        grad_short,
        grad_taps,
        grad_cond,
        grad_w_out,
        grad_two,
        grad_w_gate_up,
        grad_w_down,
    )


def solution(mesh):
    return jax.shard_map(
        body,
        mesh=mesh,
        in_specs=(
            P("freq", "dp", None),
            P("freq", "dp", None),
            P("dp"),
            P("dp", None),
            P(),
            P("freq", None),
            P("freq", None),
            P("freq", None),
            P(),
            P(),
            P("freq", None),
            P(),
            P("freq", None),
            P("freq", None),
        ),
        out_specs=(
            P("freq", "dp", None),
            P("freq", "dp", None),
            P(),
            P("freq", None),
            P(),
            P(),
            P(),
            P(),
            P("freq", None),
            P(),
            P("freq", None),
            P("freq", None),
        ),
        check_vma=False,
    )
```

```python
import math

import jax
import jax.numpy as jnp
import numpy as np
from jax import lax
from jax.experimental import pallas as pl
from jax.experimental.pallas import tpu as pltpu
from jax.sharding import PartitionSpec as P

SHORT_LENGTH = 128
EPSILON = 1e-05
BF = jnp.bfloat16
F32 = jnp.float32
GROUP = 8
RIDE = 16
COSTS = {
    "layer_out": 0,
    "early_weights": 0,
    "near": 3,
    "first_norm": 3,
    "hand_on": 15,
    "project": 25,
    "fold": 20,
    "out_rows": 2,
    "mix": 15,
    "second_norm": 4,
    "feed": 5,
    "feed_place": 3,
    "down": 4,
    "feed_weights": 8,
    "second_norm_back": 12,
    "mix_back": 6,
    "fold_back": 10,
    "early_share": 1,
    "late_weights": 45,
    "first_grad": 0,
    "first_norm_back": 0,
    "late_share": 10,
    "late_sum": 10,
    "gather": 10,
    "last": 6,
    "feed_order": 4,
}
VMEM, HBM = pltpu.VMEM, pltpu.HBM
GELU_A = math.sqrt(2.0 / math.pi)
GELU_B = 0.044715


def cosine_table(length):
    freq = np.arange(length)[:, None]
    posit = np.arange(length)[None, :]
    phase = (2 * posit + 1) * freq % (4 * length)
    weight = np.where(freq == 0, 1.0, 2.0) / length
    return (np.cos(phase * (math.pi / (2 * length))) * np.sqrt(weight)).astype(np.float32)


def dot(a, b):
    return lax.dot_general(a, b, (((1,), (0,)), ((), ())), preferred_element_type=F32)


def dot_nt(a, b):
    return lax.dot_general(a, b, (((1,), (1,)), ((), ())), preferred_element_type=F32)


def dot_tn(a, b):
    return lax.dot_general(a, b, (((0,), (0,)), ((), ())), preferred_element_type=F32)


def norm_parts(values):
    center = values - jnp.mean(values, axis=-1, keepdims=True)
    spread = jnp.mean(center * center, axis=-1, keepdims=True)
    inv = lax.rsqrt(spread + EPSILON)
    return center * inv, inv


def norm_pull(hat, inv, gain, grad):
    scaled = grad * gain
    mean_one = jnp.mean(scaled, axis=-1, keepdims=True)
    mean_two = jnp.mean(scaled * hat, axis=-1, keepdims=True)
    return inv * (scaled - mean_one - hat * mean_two), jnp.sum(grad * hat, axis=0, keepdims=True)


def pick(stacked, index):
    return lax.dynamic_index_in_dim(stacked, index, axis=0, keepdims=False)


class Far:
    def __init__(self, array, start=None, size=None):
        self.array = pltpu.with_memory_space_constraint(array, pltpu.HBM)
        self.start = start
        self.shape = array.shape if start is None else (size, *array.shape[1:])

    def source(self, ref, where):
        return ref if self.start is None else ref.at[rows_at(self.start(where), self.shape[0])]


class Held:
    def __init__(self, array):
        self.array = pltpu.with_memory_space_constraint(array, pltpu.VMEM)


class Fetched:
    def __init__(self, ref, copy):
        self.ref, self.copy, self.shape = ref, copy, ref.shape

    def ready(self):
        if self.copy is not None:
            self.copy.wait()
            self.copy = None
        return self.ref

    def __getitem__(self, place):
        return self.ready()[place]

    @property
    def at(self):
        return self.ready().at


class Kept:
    def __init__(self, ref, copy):
        self.ref, self.copy, self.shape, self.dtype = ref, copy, ref.shape, ref.dtype
        self.started = False

    def __getitem__(self, place):
        return self.ref[place]

    def __setitem__(self, place, value):
        self.ref[place] = value

    def flush(self):
        if not self.started:
            self.copy.start()
            self.started = True


def run(kernel, name, outs, where, ins, scratch=(), after=()):
    arrays = [x.array if isinstance(x, (Far, Held)) else x for x in ins]
    far_in = [isinstance(x, Far) for x in ins]
    far_out = [o[2:] == (HBM,) for o in outs]
    shapes = [o[2](*o[:2]) if len(o) > 2 else jax.ShapeDtypeStruct(*o) for o in outs]
    outs = [o[:2] for o in outs]
    after = [x.array if isinstance(x, Far) else x for x in after]
    n_in, n_after, n_out, n_scratch = len(ins), len(after), len(outs), len(scratch)
    buffers = [pltpu.VMEM(x.shape, x.array.dtype) for x in ins if isinstance(x, Far)]
    buffers += [pltpu.VMEM(s, t) for (s, t), far in zip(outs, far_out) if far]

    def wrapped(*refs):
        where_ref, in_refs = refs[0], list(refs[1 : 1 + n_in])
        rest = list(refs[1 + n_in + n_after :])
        out_refs, rest = rest[:n_out], rest[n_out:]
        own, held = rest[:n_scratch], rest[n_scratch:]
        if not buffers:
            kernel(where_ref, *in_refs, *out_refs, *own)
            return
        held, sems = held[:-1], held[-1]
        number = 0
        for i in range(n_in):
            if far_in[i]:
                source = ins[i].source(in_refs[i], where_ref)
                copy = pltpu.make_async_copy(source, held[number], sems.at[number])
                copy.start()
                in_refs[i] = Fetched(held[number], copy)
                number += 1
        kept = []
        for i in range(n_out):
            if far_out[i]:
                copy = pltpu.make_async_copy(held[number], out_refs[i], sems.at[number])
                out_refs[i] = Kept(held[number], copy)
                kept.append(out_refs[i])
                number += 1
        kernel(where_ref, *in_refs, *out_refs, *own)
        for ref in kept:
            ref.flush()
        for ref in kept:
            ref.copy.wait()
        for ref in in_refs:
            if isinstance(ref, Fetched):
                ref.ready()

    size = sum(x.size * x.dtype.itemsize for x in arrays)
    size += sum(math.prod(s) * jnp.dtype(t).itemsize for s, t in outs)
    far = pl.BlockSpec(memory_space=pltpu.HBM)
    near = pl.BlockSpec(memory_space=pltpu.VMEM)
    small = pl.BlockSpec(memory_space=pltpu.SMEM)
    return pl.pallas_call(
        wrapped,
        out_shape=shapes,
        in_specs=[small]
        + [far if f else small if x.dtype == jnp.int32 else near for x, f in zip(arrays, far_in)]
        + [pl.BlockSpec(memory_space=pl.ANY)] * n_after,
        out_specs=[far if f else near for f in far_out],
        scratch_shapes=list(scratch)
        + buffers
        + ([pltpu.SemaphoreType.DMA((len(buffers),))] if buffers else []),
        compiler_params=pltpu.CompilerParams(vmem_limit_bytes=24 * 2**20),
        cost_estimate=pl.CostEstimate(
            flops=int(COSTS.get(name, 1) * 1.15e9),
            bytes_accessed=int(size) if COSTS.get(name, 1) else 0,
            transcendentals=0,
        ),
        name=name,
    )(where, *arrays, *after)


def rows_at(index, size):
    return pl.ds(pl.multiple_of(index * size, 16), size)


def first_norm_kernel(where, x, gain, normed):
    owned = x.shape[0]
    for s in range(x.shape[1]):
        hat, _ = norm_parts(x[:, s, :])
        normed[pl.ds(s * owned, owned), :] = (hat * gain[...]).astype(BF)


def low_kernel(where, x, out):
    owned = x.shape[0]
    for s in range(x.shape[1]):
        out[pl.ds(s * owned, owned), :] = x[:, s, :].astype(BF)


def near_kernel(where, w_in, w_out, near):
    core = where[2]
    half = w_out.shape[1] // 2
    for i, ref in enumerate((w_in, w_in, w_in, w_out)):
        at = i % 3 * 2 * half
        near[:, i * half : (i + 1) * half] = jnp.where(
            core == 0, ref[:, at : at + half], ref[:, at + half : at + 2 * half]
        )


def local_kernel(where, w_in, w_out, long, short, local, out_local, long_half, short_half):
    core = where[2]
    width = w_out.shape[1]
    half = width // 2

    def mine(x, start):
        return jnp.where(core == 0, x[:, start : start + half], x[:, start + half : start + width])

    for i in range(3):
        local[:, i * half : (i + 1) * half] = mine(w_in, i * width)
    out_local[...] = mine(w_out, 0)
    long_half[...] = mine(long, 0)
    short_half[...] = mine(short, 0)


def hand_on_kernel(where, n1, n2, n3, stack):
    for k, near in enumerate((n1, n2, n3)):
        stack[k] = near[...]


def feed_pick_kernel(where, w_gate_up, w_down, mlp):
    z, chip, core = where[0], where[1], where[2]
    rows = w_gate_up.shape[0]
    hidden = w_gate_up.shape[1] // 2
    per_z = w_down.shape[0]
    chunk = per_z // 6
    member = 2 * chip + core
    for side in range(2):
        for i in range(3):
            zz = i + (i >= chip).astype(jnp.int32)
            c = jnp.where(member < 2 * zz, member, member - 2)
            start = pl.multiple_of(side * hidden + zz * per_z + c * chunk, 128)
            to = (side * 3 + i) * chunk
            mlp[pl.ds(0, rows), to : to + chunk] = w_gate_up[:, pl.ds(start, chunk)]
    c = jnp.clip(jnp.where(member < 2 * z, member, member - 2), 0, 5)
    mlp[pl.ds(rows, chunk), :] = w_down[rows_at(c, chunk), :]


def valid_rows(marks, s, z, owned):
    total = marks[s, 1] + marks[s, 2] + marks[s, 3] + marks[s, 4]
    return jnp.where(marks[s, 0] == 1, marks[s, 1 + z], total - owned * z)


def split_channels(whole, packs):
    count, owned, lanes = packs.shape
    part = lanes // count
    for there in range(count):
        for s in range(count):
            packs[there, :, s * part : (s + 1) * part] = whole[
                s * owned : (s + 1) * owned, there * part : (there + 1) * part
            ]


def join_channels(z, pieces, packs, whole):
    count, owned, lanes = packs.shape
    part = lanes // count
    for k, piece in enumerate(pieces):
        packs[(z - k) & 3] = piece[...]
    for there in range(count):
        for s in range(count):
            whole[s * owned : (s + 1) * owned, there * part : (there + 1) * part] = packs[
                there, :, s * part : (s + 1) * part
            ]


def project_kernel(where, marks_own, marks_other, na, nb, local, n1, n2, n3, c1, c2, c3, long_in, short_in, v0, v1, v2, v3, w, outer, left, right, vals, packs, folds):
    z, chip = where[0], where[1]
    rows = local.shape[0]
    quarter = rows // 4
    half = outer.shape[1]
    wide = 3 * half
    w[rows_at(z, rows), :] = local[...]
    for k, near in ((1, n1), (2, n2), (3, n3)):
        base = ((z - k) & 3) * 4
        w[rows_at(base + chip, quarter), :] = near[:, :wide]
        for m, far in ((1, c1), (2, c2), (3, c3)):
            w[rows_at(base + (chip ^ m), quarter), :] = far[k - 1, :, :wide]
    w.flush()
    owned = packs.shape[1]
    count = na.shape[0]
    place = lax.broadcasted_iota(jnp.int32, (owned, half), 0)
    for i, (tokens, marks) in enumerate(((na, marks_own), (nb, marks_other))):
        at = pl.ds(i * count, count)
        full = dot(tokens[...], w[...])
        a, b, c = full[:, :half], full[:, half : 2 * half], full[:, 2 * half :]
        outer[at, :] = a
        left[at, :] = b.astype(BF)
        right[at, :] = c.astype(BF)
        for s in range(count // owned):
            valid = valid_rows(marks, s, z, owned)
            low = slice(s * owned, (s + 1) * owned)
            vals[pl.ds(i * count + s * owned, owned), :] = jnp.where(
                place < valid, b[low] * c[low], 0.0
            ).astype(BF)
    for ref in (outer, left, right):
        ref.flush()
    split_channels(vals, packs)
    part = half // 4
    block = (long_in.shape[0] + short_in.shape[0]) // 4
    folds[...] = jnp.zeros(folds.shape, F32)
    for there in range(4):
        lanes = slice(there * part, (there + 1) * part)
        both = jnp.concatenate([long_in[:, lanes], short_in[:, lanes]], axis=0).astype(F32)
        for g in range(4):
            folds[there, pl.ds(0, block), g * part : (g + 1) * part] = both[g * block : (g + 1) * block]
    for k, out in enumerate((v0, v1, v2, v3)):
        out[pl.ds(0, owned), :] = packs[(z + k) & 3]
        rest = out.shape[0] - owned
        out[pl.ds(owned, rest), :] = folds[(z + k) & 3].astype(BF)


def short_lanes(marks_own, marks_other, shape):
    part = shape[1] // 4
    slot = lax.broadcasted_iota(jnp.int32, shape, 1) // part
    groups = [marks_own[0, 0], marks_own[1, 0], marks_other[0, 0], marks_other[1, 0]]
    return sum(jnp.where(slot == s, group, 0) for s, group in enumerate(groups)) == 1


def neighbours(x, short):
    length = x.shape[0]
    place = lax.broadcasted_iota(jnp.int32, x.shape, 0)
    starts = (place == 0) | (short & (place % SHORT_LENGTH == 0))
    ends = (place == length - 1) | (short & (place % SHORT_LENGTH == SHORT_LENGTH - 1))
    earlier = jnp.where(starts, 0.0, pltpu.roll(x, 1, 0))
    later = jnp.where(ends, 0.0, pltpu.roll(x, length - 1, 0))
    return earlier, later


def both_tables(long, short, x, mask):
    whole = dot(long[...], x)
    parts = [
        dot(short[...], x[i * SHORT_LENGTH : (i + 1) * SHORT_LENGTH])
        for i in range(x.shape[0] // SHORT_LENGTH)
    ]
    return jnp.where(mask, jnp.concatenate(parts, axis=0), whole)


def fold_kernel(where, marks_own, marks_other, v0, r1, r2, r3, long, long_t, short, short_t, gain, taps, o0, o1, o2, o3, vals, spectrum, cond_spec, base, low_base, low_short, conv):
    z = where[0]
    length, half = vals.shape
    owned = length // 4
    part = half // 4
    block = (owned + SHORT_LENGTH // 4) // 4
    for k, piece in enumerate((v0, r1, r2, r3)):
        there = (z - k) & 3
        vals[rows_at(there, owned), :] = piece[pl.ds(0, owned), :]
        got = piece[pl.ds(owned, block), :].astype(F32)
        got = jnp.concatenate([got[:, g * part : (g + 1) * part] for g in range(4)], axis=0)
        low_base[rows_at(there, owned), :] = got[:owned]
        low_short[rows_at(there, SHORT_LENGTH // 4), :] = got[owned:]
    vals.flush()
    mask = short_lanes(marks_own, marks_other, (length, half))
    tall = jnp.concatenate([low_short[...]] * (length // SHORT_LENGTH), axis=0)
    base[...] = jnp.where(
        mask, jnp.concatenate([tall] * 4, axis=1), jnp.concatenate([low_base[...]] * 4, axis=1)
    ).astype(BF)
    base.flush()
    wide = vals[...].astype(F32)
    before, after = neighbours(wide, mask)
    cond = taps[0:1, :] * before + taps[1:2, :] * wide + taps[2:3, :] * after
    high = cond.astype(BF)
    low = (cond - high.astype(F32)).astype(BF)
    spec = both_tables(long, short, vals[...], mask)
    spectrum[...] = spec
    spectrum.flush()
    cspec = both_tables(long, short, high, mask) + both_tables(long, short, low, mask)
    cond_spec[...] = cspec
    cond_spec.flush()
    kern = base[...].astype(F32) + gain[...] * (jnp.sqrt(cspec * cspec + 1.0) - 1.0)
    filtered = (kern * spec).astype(BF)
    conv[...] = both_tables(long_t, short_t, filtered, mask).astype(BF)
    for k, out in enumerate((o0, o1, o2, o3)):
        out[...] = conv[rows_at((z + k) & 3, owned), :]


def out_rows_kernel(where, local, n1, n2, n3, c1, c2, c3, keep, send, whole):
    z, chip, core = where[0], where[1], where[2]
    rows, half = local.shape
    quarter = rows // 4
    wide = 3 * half
    whole[rows_at(z, rows), :] = local[...]
    for k, near in ((1, n1), (2, n2), (3, n3)):
        base = ((z - k) & 3) * 4
        whole[rows_at(base + chip, quarter), :] = near[:, wide:]
        for m, far in ((1, c1), (2, c2), (3, c3)):
            whole[rows_at(base + (chip ^ m), quarter), :] = far[k - 1, :, wide:]
    keep[...] = whole[rows_at(core, half), :]
    send[...] = whole[rows_at(1 - core, half), :]


def mix_kernel(where, outer, c0, r1, r2, r3, w_keep, w_came, own, other, conv, mixed, w_rows, packs):
    z, core = where[0], where[2]
    half = outer.shape[1]
    w_rows[:, :half] = jnp.where(core == 0, w_keep[...], w_came[...])
    w_rows[:, half:] = jnp.where(core == 0, w_came[...], w_keep[...])
    w_rows.flush()
    join_channels(z, (c0, r1, r2, r3), packs, conv)
    conv.flush()
    mixed[...] = (outer[...] * conv[...].astype(F32)).astype(BF)
    count = own.shape[0]
    other[...] = dot(mixed[pl.ds(count, count), :], w_rows[...]).astype(BF)
    own[...] = dot(mixed[pl.ds(0, count), :], w_rows[...])


def second_kernel(where, x, own, came, gain, normed, residual):
    owned = x.shape[0]
    for s in range(x.shape[1]):
        at = pl.ds(s * owned, owned)
        total = x[:, s, :] + own[at, :] + came[at, :].astype(F32)
        residual[at, :] = total
        hat, _ = norm_parts(total)
        normed[at, :] = (hat * gain[...]).astype(BF)


def feed_place_kernel(where, own, other, w_gu, w_dn):
    chip = where[1]
    rows = w_gu.shape[1] // 4
    chunk = own.shape[1] - rows
    for p, part in enumerate((own, other)):
        for i in range(4):
            w_gu[p, pl.ds(i * rows, rows), :] = part[i, pl.ds(0, rows), :]
        for i in range(3):
            at = i + (i >= chip).astype(jnp.int32)
            w_dn[p, pl.ds(i * chunk, chunk), :] = part[at, pl.ds(rows, chunk), :]


def feed_kernel(where, second, cot, w_gu, w_dn, out, layer, act, grads):
    half = w_dn.shape[1]
    width = second.shape[1]
    for p in range(2):
        gate_up = dot(second[...], w_gu[p])
        gate, upward = gate_up[:, :half], gate_up[:, half:]
        grad_act = dot_nt(cot[...], w_dn[p])
        square = gate * gate
        tanh = jnp.tanh(GELU_A * gate * (1.0 + GELU_B * square))
        cdf = 0.5 * (1.0 + tanh)
        unit = gate * cdf
        slope = cdf + 0.5 * gate * (1.0 - tanh * tanh) * (GELU_A * (1.0 + 3.0 * GELU_B * square))
        act[:, p * half : (p + 1) * half] = (unit * upward).astype(BF)
        grads[:, p * width : p * width + half] = (grad_act * upward * slope).astype(BF)
        grads[:, p * width + half : (p + 1) * width] = (grad_act * unit).astype(BF)
    total = dot_nt(grads[:, :width], w_gu[0]) + dot_nt(grads[:, width:], w_gu[1])
    out[...] = total.astype(out.dtype)
    total = dot(act[:, :half], w_dn[0]) + dot(act[:, half:], w_dn[1])
    layer[...] = total.astype(layer.dtype)


def feed_weight_kernel(where, a0, a1, a2, a3, g0, g1, g2, g3, s0, s1, s2, s3, c0, c1, c2, c3, send, keep):
    chip = where[1]
    width = s0.shape[1]
    half = width // 2
    nz, piece, _ = keep.shape
    chunk = half // 3
    rows = piece - chunk
    for p, out in ((1, send), (0, keep)):
        total = None
        for s, g in ((s0, g0), (s1, g1), (s2, g2), (s3, g3)):
            part = dot_tn(s[...], g[:, p * width : (p + 1) * width])
            total = part if total is None else total + part
        for i in range(nz):
            out[i, pl.ds(0, rows), :] = total[i * rows : (i + 1) * rows].astype(BF)
        down = None
        for a, c in ((a0, c0), (a1, c1), (a2, c2), (a3, c3)):
            part = dot_tn(a[:, p * half : (p + 1) * half], c[...])
            down = part if down is None else down + part
        out[chip, pl.ds(rows, chunk), :] = jnp.zeros((chunk, width), BF)
        for i in range(3):
            to = i + (i >= chip).astype(jnp.int32)
            out[to, pl.ds(rows, chunk), :] = down[i * chunk : (i + 1) * chunk].astype(BF)


def add_kernel(where, a, b, out):
    out[...] = (a[...].astype(F32) + b[...].astype(F32)).astype(BF)


def layer_out_kernel(where, residual, own, r1, r2, r3, out):
    owned = out.shape[0]
    for s in range(out.shape[1]):
        at = pl.ds(s * owned, owned)
        out[:, s, :] = residual[at, :] + added([x.at[at] for x in (own, r1, r2, r3)])


def second_back_kernel(where, residual, gain, cot, own, r1, r2, r3, low, grad_gain, grad_residual):
    owned = cot.shape[0]
    grad = own[...] + r1[...].astype(F32) + r2[...].astype(F32) + r3[...].astype(F32)
    hat, inv = norm_parts(residual[...])
    pulled, grad_gain[...] = norm_pull(hat, inv, gain[...], grad)
    for s in range(cot.shape[1]):
        at = pl.ds(s * owned, owned)
        total = cot[:, s, :] + pulled[s * owned : (s + 1) * owned]
        grad_residual[at, :] = total
        low[at, :] = total.astype(BF)


def write_pieces(whole, outs, chip):
    rows = whole.shape[0] // 4
    quarter = rows // 4
    for m, out in enumerate(outs):
        for i in range(4):
            out[pl.ds(i * quarter, quarter), :] = whole[rows_at(i * 4 + (chip ^ m), quarter), :]


def mix_back_kernel(where, ga, gb, w_rows, outer, conv, o0, o1, o2, o3, grad_outer, grad_conv, packs):
    z = where[0]
    count = ga.shape[0]
    half = outer.shape[1]
    for i, grad in enumerate((ga, gb)):
        at = pl.ds(i * count, count)
        grad_mixed = dot_nt(grad[...], w_rows[...])
        grad_outer[at, :] = (grad_mixed * conv[at, :].astype(F32)).astype(BF)
        grad_conv[at, :] = (grad_mixed * outer[at, :]).astype(BF)
    grad_outer.flush()
    split_channels(grad_conv, packs)
    for k, out in enumerate((o0, o1, o2, o3)):
        out[...] = packs[(z + k) & 3]


def early_kernel(where, na, nb, grad_outer, mixed, other_mixed, ga, gb, p0, p1, p2, p3, whole):
    chip, core = where[1], where[2]
    count, half = na.shape[0], mixed.shape[1]
    first = jnp.where(core == 0, ga[:, :half], ga[:, half:])
    second = jnp.where(core == 0, gb[:, :half], gb[:, half:])
    mine = dot_tn(mixed[pl.ds(0, count), :], first) + dot_tn(mixed[pl.ds(count, count), :], second)
    theirs = dot_tn(other_mixed[pl.ds(count, count), :], first)
    theirs = theirs + dot_tn(other_mixed[pl.ds(0, count), :], second)
    whole[rows_at(core, half), half:] = mine.astype(BF)
    whole[rows_at(1 - core, half), half:] = theirs.astype(BF)
    total = dot_tn(na[...], grad_outer[pl.ds(0, count), :])
    total = total + dot_tn(nb[...], grad_outer[pl.ds(count, count), :])
    whole[:, :half] = total.astype(BF)
    write_pieces(whole, (p0, p1, p2, p3), chip)


def fold_back_kernel(where, marks_own, marks_other, g0, r1, r2, r3, long, short, spectrum, cond_spec, base, gain, taps, vals, long_t, short_t, o0, o1, o2, o3, filt, grads):
    z = where[0]
    length, half = grads.shape
    owned = length // 4
    part = half // 4
    for k, piece in enumerate((g0, r1, r2, r3)):
        grads[rows_at((z - k) & 3, owned), :] = piece[...]
    mask = short_lanes(marks_own, marks_other, (length, half))
    gf = both_tables(long, short, grads[...], mask)
    cspec = cond_spec[...]
    root = jnp.sqrt(cspec * cspec + 1.0)
    above = root - 1.0
    grad_base = gf * spectrum[...]
    grad_spec = (gf * (base[...].astype(F32) + gain[...] * above)).astype(BF)
    grad_cspec = (grad_base * gain[...] * (cspec / root)).astype(BF)
    grad_cond = both_tables(long_t, short_t, grad_cspec, mask)
    direct = both_tables(long_t, short_t, grad_spec, mask)
    wide = vals[...].astype(F32)
    before, after = neighbours(wide, mask)
    grad_before, grad_after = neighbours(grad_cond, mask)
    grads[...] = (
        direct + taps[0:1, :] * grad_after + taps[1:2, :] * grad_cond + taps[2:3, :] * grad_before
    ).astype(BF)
    for k, out in enumerate((o0, o1, o2, o3)):
        out[...] = grads[rows_at((z + k) & 3, owned), :]

    def over_slots(x):
        return sum(x[:, s * part : (s + 1) * part] for s in range(4))

    shorts = jnp.where(mask, grad_base, 0.0)
    small = [
        jnp.sum(x, axis=0, keepdims=True)
        for x in (grad_base * above, grad_cond * before, grad_cond * wide, grad_cond * after)
    ]
    folded = sum(
        shorts[i * SHORT_LENGTH : (i + 1) * SHORT_LENGTH] for i in range(length // SHORT_LENGTH)
    )
    fill = filt.shape[0] * (filt.shape[1] // part) - length - SHORT_LENGTH - 4
    found = jnp.concatenate(
        [
            over_slots(grad_base - shorts),
            over_slots(folded),
            over_slots(jnp.concatenate(small, axis=0)),
            jnp.zeros((fill, part), F32),
        ],
        axis=0,
    )
    size = filt.shape[0]
    blocks = [found[g * size : (g + 1) * size] for g in range(filt.shape[1] // part)]
    filt[...] = jnp.concatenate(blocks, axis=1).astype(BF)


def late_kernel(where, marks_own, marks_other, g0, r1, r2, r3, left, right, na, nb, p0, p1, p2, p3, late, grads, packs, whole):
    z, chip = where[0], where[1]
    half = left.shape[1]
    owned = packs.shape[1]
    join_channels(z, (g0, r1, r2, r3), packs, grads)
    count = na.shape[0]
    place = lax.broadcasted_iota(jnp.int32, (owned, half), 0)
    for i, marks in enumerate((marks_own, marks_other)):
        for s in range(count // owned):
            at = pl.ds(i * count + s * owned, owned)
            valid = valid_rows(marks, s, z, owned)
            grad = jnp.where(place < valid, grads[at, :].astype(F32), 0.0)
            late[at, :half] = (grad * right[at, :].astype(F32)).astype(BF)
            late[at, half:] = (grad * left[at, :].astype(F32)).astype(BF)
    total = dot_tn(na[...], late[pl.ds(0, count), :]) + dot_tn(nb[...], late[pl.ds(count, count), :])
    whole[...] = total.astype(BF)
    write_pieces(whole, (p0, p1, p2, p3), chip)


def first_grad_kernel(where, grad_outer, late, w, own, other):
    half = grad_outer.shape[1]
    count = own.shape[0]
    for i, out in ((1, other), (0, own)):
        at = pl.ds(i * count, count)
        total = dot_nt(grad_outer[at, :], w[:, :half]) + dot_nt(late[at, :], w[:, half:])
        out[...] = total.astype(out.dtype)


def first_back_kernel(where, x, gain, grad_residual, own, came, grad_gain, grad_inputs):
    owned = x.shape[0]
    riding = None
    for s in range(x.shape[1]):
        at = pl.ds(s * owned, owned)
        hat, inv = norm_parts(x[:, s, :])
        pulled, part = norm_pull(hat, inv, gain[...], own[at, :] + came[at, :].astype(F32))
        grad_inputs[:, s, :] = grad_residual[at, :] + pulled
        riding = part if riding is None else riding + part
    grad_gain[...] = riding


def added(pieces):
    total = pieces[0][...].astype(F32)
    for piece in pieces[1:]:
        total = total + piece[...].astype(F32)
    return total


def late_share_kernel(where, p0, r1, r2, r3, e0, e1, e2, e3, one, two, o0, o1, o2, o3, late, early):
    z = where[0]
    late[...] = added((p0, r1, r2, r3)).astype(BF)
    early[...] = added((e0, e1, e2, e3)).astype(BF)
    quarter = p0.shape[0] // 4
    width = p0.shape[1]
    place = lax.broadcasted_iota(jnp.int32, (RIDE, width), 0)
    extra = jnp.where(place == 0, jnp.broadcast_to(one[...], (RIDE, width)), 0.0)
    extra = jnp.where(place == 1, jnp.broadcast_to(two[...], (RIDE, width)), extra).astype(BF)
    for k, out in enumerate((o0, o1, o2, o3)):
        at = rows_at((z + k) & 3, quarter)
        out[pl.ds(0, quarter), :] = late[at, :]
        out[pl.ds(quarter, quarter), :] = early[at, :]
        out[pl.ds(2 * quarter, RIDE), :] = extra


def late_sum_kernel(where, s0, r1, r2, r3, f0, f1, f2, f3, piece, filt):
    piece[...] = added((s0, r1, r2, r3)).astype(BF)
    filt[...] = added((f0, f1, f2, f3)).astype(BF)


def gather_kernel(where, s0, r1, r2, r3, f0, f1, f2, f3, out):
    z, chip = where[0], where[1]
    quarter = (s0.shape[0] - RIDE) // 2
    parts = (s0, r1, r2, r3)
    for m, piece in enumerate(parts):
        for i in range(2):
            out[rows_at(i * 4 + (chip ^ m), quarter), :] = piece[pl.ds(i * quarter, quarter), :]
    riding = added([piece[pl.ds(2 * quarter, RIDE), :] for piece in parts])
    top = 8 * quarter
    out[pl.ds(top, RIDE), :] = riding.astype(BF)
    step = f0.shape[0]
    for k, piece in enumerate((f0, f1, f2, f3)):
        at = top + RIDE + ((z - k) & 3) * step
        out[pl.ds(pl.multiple_of(at, 16), step), :] = piece[...]


def feed_order_kernel(where, shares, gate_up, down):
    z = where[0]
    rows = gate_up.shape[0]
    chunk = shares.shape[1] - rows
    per_z = 6 * chunk
    for side in range(2):
        for zz in range(4):
            for c in range(6):
                mm = c if c < 2 * zz else c + 2
                at = (side * 3 + zz - (zz > mm // 2)) * chunk
                to = side * 4 * per_z + zz * per_z + c * chunk
                gate_up[:, to : to + chunk] = shares[mm, :rows, at : at + chunk].astype(F32)
    for c in range(6):
        mm = c + 2 * (c >= 2 * z).astype(jnp.int32)
        down[pl.ds(c * chunk, chunk), :] = shares[mm, pl.ds(rows, chunk), :].astype(F32)


def last_kernel(where, own, other, w_in, w_out, long, short, gain, taps, norm_one, norm_two):
    core = where[2]
    rows = w_in.shape[0]
    width = w_out.shape[1]
    half = width // 2
    part = half // 4
    top = 2 * rows

    def write(out, to, a, b):
        a, b = a.astype(F32), b.astype(F32)
        out[:, to : to + half] = jnp.where(core == 0, a, b)
        out[:, to + half : to + width] = jnp.where(core == 0, b, a)

    for start, at, to, out in (
        (rows, 0, 0, w_in),
        (0, 0, width, w_in),
        (0, half, 2 * width, w_in),
        (rows, half, 0, w_out),
    ):
        place = (pl.ds(start, rows), slice(at, at + half))
        write(out, to, own[place], other[place])
    place = pl.ds(top, RIDE)
    riding = own[place, :].astype(F32) + other[place, :].astype(F32)
    norm_one[...] = riding[0]
    norm_two[...] = riding[1]
    step = (own.shape[0] - top - RIDE) // 4
    length, count = long.shape[0], short.shape[0]

    def filter_rows(ref):
        got = []
        for there in range(4):
            at = pl.ds(top + RIDE + there * step, step)
            blocks = [ref[at, g * part : (g + 1) * part].astype(F32) for g in range(width // part)]
            got.append(jnp.concatenate(blocks, axis=0))
        return jnp.concatenate(got, axis=1)

    a, b = filter_rows(own), filter_rows(other)
    write(long, 0, a[:length], b[:length])
    write(short, 0, a[length : length + count], b[length : length + count])
    rest = length + count
    a_row, b_row = a[rest], b[rest]
    gain[pl.ds(0, half)] = jnp.where(core == 0, a_row, b_row)
    gain[pl.ds(half, half)] = jnp.where(core == 0, b_row, a_row)
    write(taps, 0, a[rest + 1 : rest + 4], b[rest + 1 : rest + 4])


def body(
    inputs,
    cotangent,
    group,
    lens,
    norm1_gain,
    w_in,
    kernel_long,
    kernel_short,
    conv_weight,
    cond_gain,
    w_out,
    norm2_gain,
    w_gate_up,
    w_down,
):
    nz = lax.axis_size("freq")
    ndp = lax.axis_size("dp")
    z = lax.axis_index("freq")
    d = lax.axis_index("dp")
    core = d % 2
    chip = (d // 2) % 4
    owned, slots, width = inputs.shape
    half = width // 2
    length = owned * nz
    tokens = owned * slots
    rows = w_in.shape[0]
    quarter = rows // 4
    others = ndp // GROUP
    blocks = [[g * GROUP + i for i in range(GROUP)] for g in range(others)]
    same_core = [[g * GROUP + 2 * i + c for i in range(4)] for g in range(others) for c in range(2)]
    across = [[i + GROUP * g for g in range(others)] for i in range(GROUP)]

    def core_swap(x):
        return lax.ppermute(x, "dp", [(i, i ^ 1) for i in range(ndp)])

    def chip_swap(x, m):
        return lax.ppermute(x, "dp", [(i, i ^ (2 * m)) for i in range(ndp)])

    def z_rot(x, k):
        return lax.ppermute(x, "freq", [(i, (i + k) % nz) for i in range(nz)])

    def z_swap(pieces):
        return [pieces[0]] + [z_rot(pieces[k], k) for k in range(1, nz)]

    def own_far(pieces):
        got = z_swap(pieces)
        return [Far(got[0])] + got[1:]

    def near_by(piece):
        return [piece] + [chip_swap(piece, m) for m in (1, 2, 3)]

    def exchanged(parts):
        return [parts[0]] + [chip_swap(parts[m], m) for m in (1, 2, 3)]

    def over_groups(x):
        if others > 1:
            return lax.psum(x, "dp", axis_index_groups=across)
        return x

    where = jnp.stack([z, chip, core, z]).astype(jnp.int32)
    part = kernel_short.shape[0]
    hidden = w_down.shape[0] * nz
    per_z = w_down.shape[0]
    chunk = per_z // 6
    taken = rows + chunk
    quarter_of = lambda place: place[1]
    near = run(
        near_kernel,
        "near",
        [((quarter, 4 * half), BF)],
        where,
        [Far(w_in, quarter_of, quarter), Far(w_out, quarter_of, quarter)],
    )[0]
    in_local, out_local, long_half, short_half = run(
        local_kernel,
        "local",
        [((rows, 3 * half), BF), ((rows, half), BF), ((owned, half), BF), ((part, half), BF)],
        where,
        [w_in, w_out, kernel_long, kernel_short],
        after=(near,),
    )
    all_near = [z_rot(near, k) for k in range(1, nz)]

    gain_one = norm1_gain[None]
    gain_two = norm2_gain[None]
    cot_low = run(low_kernel, "cot_low", [((tokens, width), BF)], where, [Far(cotangent)], after=(near,))[0]
    cots = [cot_low] + [chip_swap(cot_low, m) for m in (1, 2, 3)]
    normed = run(
        first_norm_kernel,
        "first_norm",
        [((tokens, width), BF)],
        where,
        [Far(inputs), gain_one],
        after=(cot_low,),
    )[0]
    normed_other = core_swap(normed)
    in_stack = run(
        hand_on_kernel,
        "hand_on",
        [((3, quarter, 4 * half), BF)],
        where,
        all_near,
    )[0]
    mlp_piece = run(
        feed_pick_kernel,
        "feed_pick",
        [((taken, width), BF)],
        where,
        [w_gate_up, w_down],
        after=(near,),
    )[0]
    in_far = [chip_swap(in_stack, m) for m in (1, 2, 3)]
    mlp_got = lax.all_gather(mlp_piece, "freq", axis=0)

    marks = jnp.concatenate([group[:, None], lens], axis=1).astype(jnp.int32)
    marks_other = core_swap(marks)
    lane = half // nz

    def channels(x):
        own = jnp.where(core == 0, x[:, :half], x[:, half:])
        picked = sum(
            jnp.where(z == i, own[:, i * lane : (i + 1) * lane], 0.0) for i in range(nz)
        )
        return jnp.concatenate([picked] * 4, axis=1)

    gain_lanes = channels(cond_gain[None])
    taps = channels(conv_weight)
    long = jnp.asarray(cosine_table(length), BF)
    long_t = jnp.asarray(cosine_table(length).T, BF)
    short = jnp.asarray(cosine_table(SHORT_LENGTH), BF)
    short_t = jnp.asarray(cosine_table(SHORT_LENGTH).T, BF)

    many = 2 * tokens
    block = (owned + part) // 4
    filler = -block % 16 + block
    piece = ((owned, half), BF)
    *sends, w_in_half, outer, left, right = run(
        project_kernel,
        "project",
        [((owned + filler, half), BF, HBM)]
        + [((owned + filler, half), BF)] * 3
        + [((width, 3 * half), BF, HBM), ((many, half), F32, HBM)]
        + [((many, half), BF, HBM)] * 2,
        where,
        [marks, marks_other, normed, normed_other, in_local, *all_near, *in_far, long_half, short_half],
        [
            pltpu.VMEM((many, half), BF),
            pltpu.VMEM((nz, owned, half), BF),
            pltpu.VMEM((nz, filler, half), F32),
        ],
    )
    came = own_far(sends)
    full = (length, half)
    *sends, vals, spectrum, cond_spec, base = run(
        fold_kernel,
        "fold",
        [(*piece, HBM)] + [piece] * 3 + [(full, BF, HBM), (full, F32, HBM), (full, F32, HBM), (full, BF, HBM)],
        where,
        [marks, marks_other, *came, long, long_t, short, short_t, gain_lanes, taps],
        [
            pltpu.VMEM((length, lane), F32),
            pltpu.VMEM((part * nz, lane), F32),
            pltpu.VMEM(full, BF),
        ],
        after=cots[1:3],
    )
    came = own_far(sends)
    w_keep, w_send = run(
        out_rows_kernel,
        "out_rows",
        [((half, half), BF, HBM), ((half, half), BF)],
        where,
        [out_local, *all_near, *in_far],
        [pltpu.VMEM((width, half), BF)],
        after=(sends[0],),
    )
    w_gu, w_dn = run(
        feed_place_kernel,
        "feed_place",
        [((2, width, width), BF, VMEM), ((2, half, width), BF, VMEM)],
        where,
        [mlp_got, core_swap(mlp_got)],
    )
    part_own, part_other, conv, mixed, w_out_rows = run(
        mix_kernel,
        "mix",
        [((tokens, width), F32), ((tokens, width), BF), ((many, half), BF, HBM)]
        + [((many, half), BF), ((half, width), BF, HBM)],
        where,
        [Far(outer), *came, Far(w_keep), core_swap(w_send)],
        [pltpu.VMEM((nz, owned, half), BF)],
        after=(cots[3],),
    )
    normed_two, residual = run(
        second_kernel,
        "second_norm",
        [((tokens, width), BF), ((tokens, width), F32, HBM)],
        where,
        [Far(inputs), part_own, core_swap(part_other), gain_two],
    )

    arrived = near_by(normed_two)
    acts, grads_gu, sums, layers = [None] * 4, [None] * 4, [None] * 4, [None] * 4
    order = ()
    for m in range(4):
        grad, layer, act, grad_gu = run(
            feed_kernel,
            "feed",
            [
                ((tokens, width), BF if m else F32),
                ((tokens, width), BF if m else F32),
                ((tokens, width), BF, VMEM),
                ((tokens, 2 * width), BF, VMEM),
            ],
            where,
            [arrived[m], cots[m], Held(w_gu), Held(w_dn)],
            after=order,
        )
        order = (grad,)
        acts[m], grads_gu[m], sums[m], layers[m] = Held(act), Held(grad_gu), grad, layer
    backs = [chip_swap(sums[m], m) for m in (1, 2, 3)]

    mlp_send, mlp_keep = run(
        feed_weight_kernel,
        "feed_weights",
        [((nz, taken, width), BF), ((nz, taken, width), BF, VMEM)],
        where,
        [*acts, *grads_gu, *arrived, *cots],
    )
    mlp_grads = run(
        add_kernel,
        "add",
        [((nz, taken, width), BF)],
        where,
        [Held(mlp_keep), core_swap(mlp_send)],
    )[0]
    mlp_share = lax.psum_scatter(mlp_grads, "freq", scatter_dimension=0, tiled=False)
    grad_mix, grad_gain_two, grad_residual = run(
        second_back_kernel,
        "second_norm_back",
        [((tokens, width), BF), ((1, width), F32), ((tokens, width), F32, HBM)],
        where,
        [Far(residual), gain_two, Far(cotangent), sums[0], *backs],
        after=(mlp_grads,),
    )
    grad_mix_other = core_swap(grad_mix)
    *got, grad_outer = run(
        mix_back_kernel,
        "mix_back",
        [(*piece, HBM)] + [piece] * 3 + [((many, half), BF, HBM)],
        where,
        [grad_mix, grad_mix_other, Far(w_out_rows), Far(outer), Far(conv)],
        [pltpu.VMEM((many, half), BF), pltpu.VMEM((nz, owned, half), BF)],
    )
    came = own_far(got)
    early_all = exchanged(
        run(
            early_kernel,
            "early_weights",
            [((rows, width), BF)] * 4,
            where,
            [
                normed,
                normed_other,
                Far(grad_outer),
                mixed,
                core_swap(mixed),
                grad_mix,
                grad_mix_other,
            ],
            [pltpu.VMEM((width, width), BF)],
        )
    )

    layer_far = [chip_swap(layers[m], m) for m in (1, 2, 3)]

    size = -(-(length + SHORT_LENGTH + 4) // (16 * width // lane)) * 16
    *sends, filt = run(
        fold_back_kernel,
        "fold_back",
        [(*piece, HBM)] + [piece] * 3 + [((size, width), BF)],
        where,
        [
            marks,
            marks_other,
            *came,
            long,
            short,
            Far(spectrum),
            Far(cond_spec),
            Far(base),
            gain_lanes,
            taps,
            Far(vals),
            long_t,
            short_t,
        ],
        [pltpu.VMEM(full, BF)],
        after=[Far(x) for x in layer_far],
    )
    came = own_far(sends)
    *parts, late = run(
        late_kernel,
        "late_weights",
        [((rows, width), BF)] * 4 + [((many, width), BF)],
        where,
        [
            marks,
            marks_other,
            *came,
            Far(left),
            Far(right),
            normed,
            normed_other,
        ],
        [
            pltpu.VMEM((many, half), BF),
            pltpu.VMEM((nz, owned, half), BF),
            pltpu.VMEM((width, width), BF),
        ],
        after=[Far(x) for x in (*early_all[1:], mlp_share)],
    )
    own, other = run(
        first_grad_kernel,
        "first_grad",
        [((tokens, width), F32), ((tokens, width), BF)],
        where,
        [Far(grad_outer), late, Far(w_in_half)],
    )
    grad_gain_one, grad_inputs = run(
        first_back_kernel,
        "first_norm_back",
        [((1, width), F32), ((owned, slots, width), F32, HBM)],
        where,
        [Far(inputs), gain_one, Far(grad_residual), own, core_swap(other)],
    )
    mlp_sum = lax.all_gather(over_groups(mlp_share), "dp", axis=0, axis_index_groups=blocks)
    layer_out = run(
        layer_out_kernel,
        "layer_out",
        [((owned, slots, width), F32, HBM)],
        where,
        [Far(residual), Far(layers[0]), *[Far(x) for x in layer_far]],
    )[0]
    late_sends = run(
        late_share_kernel,
        "late_share",
        [((2 * quarter + RIDE, width), BF)] * 4,
        where,
        [
            *exchanged(parts),
            early_all[0],
            *[Far(x) for x in early_all[1:]],
            grad_gain_one,
            grad_gain_two,
        ],
        [pltpu.VMEM((rows, width), BF)] * 2,
        after=(Far(layer_out),),
    )
    late_piece, filt = run(
        late_sum_kernel,
        "late_sum",
        [((2 * quarter + RIDE, width), BF), ((size, width), BF)],
        where,
        [*z_swap(late_sends), *near_by(over_groups(filt))],
    )
    grad_w_gate_up, grad_w_down = run(
        feed_order_kernel,
        "feed_order",
        [((rows, 2 * hidden), F32, HBM), ((per_z, width), F32, HBM)],
        where,
        [Far(mlp_sum)],
        after=(late_piece,),
    )
    gathered = run(
        gather_kernel,
        "gather",
        [((2 * rows + RIDE + nz * size, width), BF)],
        where,
        [*near_by(over_groups(late_piece)), *z_swap([filt] * nz)],
        after=[Far(grad_w_down)],
    )[0]
    grad_w_in, grad_w_out, grad_long, grad_short, grad_cond, grad_taps, grad_one, grad_two = run(
        last_kernel,
        "last",
        [
            ((rows, 3 * width), F32),
            ((rows, width), F32),
            ((length, width), F32),
            ((SHORT_LENGTH, width), F32),
            ((width,), F32),
            ((3, width), F32),
            ((width,), F32),
            ((width,), F32),
        ],
        where,
        [gathered, core_swap(gathered)],
    )

    return (
        layer_out,
        grad_inputs,
        grad_one,
        grad_w_in,
        grad_long,
        grad_short,
        grad_taps,
        grad_cond,
        grad_w_out,
        grad_two,
        grad_w_gate_up,
        grad_w_down,
    )


def solution(mesh):
    return jax.shard_map(
        body,
        mesh=mesh,
        in_specs=(
            P("freq", "dp", None),
            P("freq", "dp", None),
            P("dp"),
            P("dp", None),
            P(),
            P("freq", None),
            P("freq", None),
            P("freq", None),
            P(),
            P(),
            P("freq", None),
            P(),
            P("freq", None),
            P("freq", None),
        ),
        out_specs=(
            P("freq", "dp", None),
            P("freq", "dp", None),
            P(),
            P("freq", None),
            P(),
            P(),
            P(),
            P(),
            P("freq", None),
            P(),
            P("freq", None),
            P("freq", None),
        ),
        check_vma=False,
    )
```

```python
import math

import jax
import jax.numpy as jnp
import numpy as np
from jax import lax
from jax.experimental import pallas as pl
from jax.experimental.pallas import tpu as pltpu
from jax.sharding import PartitionSpec as P

SHORT_LENGTH = 128
EPSILON = 1e-05
BF = jnp.bfloat16
F32 = jnp.float32
GROUP = 8
RIDE = 16
COSTS = {
    "layer_out": 0,
    "early_weights": 0,
    "near": 3,
    "first_norm": 3,
    "hand_on": 15,
    "project": 25,
    "fold": 20,
    "out_rows": 2,
    "mix": 15,
    "second_norm": 4,
    "feed": 5,
    "feed_place": 3,
    "down": 4,
    "feed_weights": 8,
    "second_norm_back": 12,
    "mix_back": 6,
    "fold_back": 10,
    "early_share": 1,
    "late_weights": 45,
    "first_grad": 0,
    "first_norm_back": 0,
    "late_share": 10,
    "late_sum": 10,
    "gather": 10,
    "last": 6,
    "feed_order": 4,
}
VMEM, HBM = pltpu.VMEM, pltpu.HBM
GELU_A = math.sqrt(2.0 / math.pi)
GELU_B = 0.044715


def cosine_table(length):
    freq = np.arange(length)[:, None]
    posit = np.arange(length)[None, :]
    phase = (2 * posit + 1) * freq % (4 * length)
    weight = np.where(freq == 0, 1.0, 2.0) / length
    return (np.cos(phase * (math.pi / (2 * length))) * np.sqrt(weight)).astype(np.float32)


def dot(a, b):
    return lax.dot_general(a, b, (((1,), (0,)), ((), ())), preferred_element_type=F32)


def dot_nt(a, b):
    return lax.dot_general(a, b, (((1,), (1,)), ((), ())), preferred_element_type=F32)


def dot_tn(a, b):
    return lax.dot_general(a, b, (((0,), (0,)), ((), ())), preferred_element_type=F32)


def norm_parts(values):
    center = values - jnp.mean(values, axis=-1, keepdims=True)
    spread = jnp.mean(center * center, axis=-1, keepdims=True)
    inv = lax.rsqrt(spread + EPSILON)
    return center * inv, inv


def norm_pull(hat, inv, gain, grad):
    scaled = grad * gain
    mean_one = jnp.mean(scaled, axis=-1, keepdims=True)
    mean_two = jnp.mean(scaled * hat, axis=-1, keepdims=True)
    return inv * (scaled - mean_one - hat * mean_two), jnp.sum(grad * hat, axis=0, keepdims=True)


def pick(stacked, index):
    return lax.dynamic_index_in_dim(stacked, index, axis=0, keepdims=False)


class Far:
    def __init__(self, array, start=None, size=None):
        self.array = pltpu.with_memory_space_constraint(array, pltpu.HBM)
        self.start = start
        self.shape = array.shape if start is None else (size, *array.shape[1:])

    def source(self, ref, where):
        return ref if self.start is None else ref.at[rows_at(self.start(where), self.shape[0])]


class Held:
    def __init__(self, array):
        self.array = pltpu.with_memory_space_constraint(array, pltpu.VMEM)


class Fetched:
    def __init__(self, ref, copy):
        self.ref, self.copy, self.shape = ref, copy, ref.shape

    def ready(self):
        if self.copy is not None:
            self.copy.wait()
            self.copy = None
        return self.ref

    def __getitem__(self, place):
        return self.ready()[place]

    @property
    def at(self):
        return self.ready().at


class Kept:
    def __init__(self, ref, copy):
        self.ref, self.copy, self.shape, self.dtype = ref, copy, ref.shape, ref.dtype
        self.started = False

    def __getitem__(self, place):
        return self.ref[place]

    def __setitem__(self, place, value):
        self.ref[place] = value

    def flush(self):
        if not self.started:
            self.copy.start()
            self.started = True


def run(kernel, name, outs, where, ins, scratch=(), after=()):
    arrays = [x.array if isinstance(x, (Far, Held)) else x for x in ins]
    far_in = [isinstance(x, Far) for x in ins]
    far_out = [o[2:] == (HBM,) for o in outs]
    shapes = [o[2](*o[:2]) if len(o) > 2 else jax.ShapeDtypeStruct(*o) for o in outs]
    outs = [o[:2] for o in outs]
    after = [x.array if isinstance(x, Far) else x for x in after]
    n_in, n_after, n_out, n_scratch = len(ins), len(after), len(outs), len(scratch)
    buffers = [pltpu.VMEM(x.shape, x.array.dtype) for x in ins if isinstance(x, Far)]
    buffers += [pltpu.VMEM(s, t) for (s, t), far in zip(outs, far_out) if far]

    def wrapped(*refs):
        where_ref, in_refs = refs[0], list(refs[1 : 1 + n_in])
        rest = list(refs[1 + n_in + n_after :])
        out_refs, rest = rest[:n_out], rest[n_out:]
        own, held = rest[:n_scratch], rest[n_scratch:]
        if not buffers:
            kernel(where_ref, *in_refs, *out_refs, *own)
            return
        held, sems = held[:-1], held[-1]
        number = 0
        for i in range(n_in):
            if far_in[i]:
                source = ins[i].source(in_refs[i], where_ref)
                copy = pltpu.make_async_copy(source, held[number], sems.at[number])
                copy.start()
                in_refs[i] = Fetched(held[number], copy)
                number += 1
        kept = []
        for i in range(n_out):
            if far_out[i]:
                copy = pltpu.make_async_copy(held[number], out_refs[i], sems.at[number])
                out_refs[i] = Kept(held[number], copy)
                kept.append(out_refs[i])
                number += 1
        kernel(where_ref, *in_refs, *out_refs, *own)
        for ref in kept:
            ref.flush()
        for ref in kept:
            ref.copy.wait()
        for ref in in_refs:
            if isinstance(ref, Fetched):
                ref.ready()

    size = sum(x.size * x.dtype.itemsize for x in arrays)
    size += sum(math.prod(s) * jnp.dtype(t).itemsize for s, t in outs)
    far = pl.BlockSpec(memory_space=pltpu.HBM)
    near = pl.BlockSpec(memory_space=pltpu.VMEM)
    small = pl.BlockSpec(memory_space=pltpu.SMEM)
    return pl.pallas_call(
        wrapped,
        out_shape=shapes,
        in_specs=[small]
        + [far if f else small if x.dtype == jnp.int32 else near for x, f in zip(arrays, far_in)]
        + [pl.BlockSpec(memory_space=pl.ANY)] * n_after,
        out_specs=[far if f else near for f in far_out],
        scratch_shapes=list(scratch)
        + buffers
        + ([pltpu.SemaphoreType.DMA((len(buffers),))] if buffers else []),
        compiler_params=pltpu.CompilerParams(vmem_limit_bytes=24 * 2**20),
        cost_estimate=pl.CostEstimate(
            flops=int(COSTS.get(name, 1) * 1.15e9),
            bytes_accessed=int(size) if COSTS.get(name, 1) else 0,
            transcendentals=0,
        ),
        name=name,
    )(where, *arrays, *after)


def rows_at(index, size):
    return pl.ds(pl.multiple_of(index * size, 16), size)


def first_norm_kernel(where, x, gain, normed):
    owned = x.shape[0]
    for s in range(x.shape[1]):
        hat, _ = norm_parts(x[:, s, :])
        normed[pl.ds(s * owned, owned), :] = (hat * gain[...]).astype(BF)


def low_kernel(where, x, out):
    owned = x.shape[0]
    for s in range(x.shape[1]):
        out[pl.ds(s * owned, owned), :] = x[:, s, :].astype(BF)


def near_kernel(where, w_in, w_out, near):
    core = where[2]
    half = w_out.shape[1] // 2
    for i, ref in enumerate((w_in, w_in, w_in, w_out)):
        at = i % 3 * 2 * half
        near[:, i * half : (i + 1) * half] = jnp.where(
            core == 0, ref[:, at : at + half], ref[:, at + half : at + 2 * half]
        )


def local_kernel(where, w_in, w_out, long, short, local, out_local, long_half, short_half):
    core = where[2]
    width = w_out.shape[1]
    half = width // 2

    def mine(x, start):
        return jnp.where(core == 0, x[:, start : start + half], x[:, start + half : start + width])

    for i in range(3):
        local[:, i * half : (i + 1) * half] = mine(w_in, i * width)
    out_local[...] = mine(w_out, 0)
    long_half[...] = mine(long, 0)
    short_half[...] = mine(short, 0)


def hand_on_kernel(where, n1, n2, n3, stack):
    for k, near in enumerate((n1, n2, n3)):
        stack[k] = near[...]


def feed_pick_kernel(where, w_gate_up, w_down, mlp):
    z, chip, core = where[0], where[1], where[2]
    rows = w_gate_up.shape[0]
    hidden = w_gate_up.shape[1] // 2
    per_z = w_down.shape[0]
    chunk = per_z // 6
    member = 2 * chip + core
    for side in range(2):
        for i in range(3):
            zz = i + (i >= chip).astype(jnp.int32)
            c = jnp.where(member < 2 * zz, member, member - 2)
            start = pl.multiple_of(side * hidden + zz * per_z + c * chunk, 128)
            to = (side * 3 + i) * chunk
            mlp[pl.ds(0, rows), to : to + chunk] = w_gate_up[:, pl.ds(start, chunk)]
    c = jnp.clip(jnp.where(member < 2 * z, member, member - 2), 0, 5)
    mlp[pl.ds(rows, chunk), :] = w_down[rows_at(c, chunk), :]


def valid_rows(marks, s, z, owned):
    total = marks[s, 1] + marks[s, 2] + marks[s, 3] + marks[s, 4]
    return jnp.where(marks[s, 0] == 1, marks[s, 1 + z], total - owned * z)


def split_channels(whole, packs):
    count, owned, lanes = packs.shape
    part = lanes // count
    for there in range(count):
        for s in range(count):
            packs[there, :, s * part : (s + 1) * part] = whole[
                s * owned : (s + 1) * owned, there * part : (there + 1) * part
            ]


def join_channels(z, pieces, packs, whole):
    count, owned, lanes = packs.shape
    part = lanes // count
    for k, piece in enumerate(pieces):
        packs[(z - k) & 3] = piece[...]
    for there in range(count):
        for s in range(count):
            whole[s * owned : (s + 1) * owned, there * part : (there + 1) * part] = packs[
                there, :, s * part : (s + 1) * part
            ]


def project_kernel(where, marks_own, marks_other, na, nb, local, n1, n2, n3, c1, c2, c3, long_in, short_in, v0, v1, v2, v3, w, outer, left, right, vals, packs, folds):
    z, chip = where[0], where[1]
    rows = local.shape[0]
    quarter = rows // 4
    half = outer.shape[1]
    wide = 3 * half
    w[rows_at(z, rows), :] = local[...]
    for k, near in ((1, n1), (2, n2), (3, n3)):
        base = ((z - k) & 3) * 4
        w[rows_at(base + chip, quarter), :] = near[:, :wide]
        for m, far in ((1, c1), (2, c2), (3, c3)):
            w[rows_at(base + (chip ^ m), quarter), :] = far[k - 1, :, :wide]
    w.flush()
    owned = packs.shape[1]
    count = na.shape[0]
    place = lax.broadcasted_iota(jnp.int32, (owned, half), 0)
    for i, (tokens, marks) in enumerate(((na, marks_own), (nb, marks_other))):
        at = pl.ds(i * count, count)
        full = dot(tokens[...], w[...])
        a, b, c = full[:, :half], full[:, half : 2 * half], full[:, 2 * half :]
        outer[at, :] = a.astype(BF)
        left[at, :] = b.astype(BF)
        right[at, :] = c.astype(BF)
        for s in range(count // owned):
            valid = valid_rows(marks, s, z, owned)
            low = slice(s * owned, (s + 1) * owned)
            vals[pl.ds(i * count + s * owned, owned), :] = jnp.where(
                place < valid, b[low] * c[low], 0.0
            ).astype(BF)
    for ref in (outer, left, right):
        ref.flush()
    split_channels(vals, packs)
    part = half // 4
    block = (long_in.shape[0] + short_in.shape[0]) // 4
    folds[...] = jnp.zeros(folds.shape, F32)
    for there in range(4):
        lanes = slice(there * part, (there + 1) * part)
        both = jnp.concatenate([long_in[:, lanes], short_in[:, lanes]], axis=0).astype(F32)
        for g in range(4):
            folds[there, pl.ds(0, block), g * part : (g + 1) * part] = both[g * block : (g + 1) * block]
    for k, out in enumerate((v0, v1, v2, v3)):
        out[pl.ds(0, owned), :] = packs[(z + k) & 3]
        rest = out.shape[0] - owned
        out[pl.ds(owned, rest), :] = folds[(z + k) & 3].astype(BF)


def short_lanes(marks_own, marks_other, shape):
    part = shape[1] // 4
    slot = lax.broadcasted_iota(jnp.int32, shape, 1) // part
    groups = [marks_own[0, 0], marks_own[1, 0], marks_other[0, 0], marks_other[1, 0]]
    return sum(jnp.where(slot == s, group, 0) for s, group in enumerate(groups)) == 1


def neighbours(x, short):
    length = x.shape[0]
    place = lax.broadcasted_iota(jnp.int32, x.shape, 0)
    starts = (place == 0) | (short & (place % SHORT_LENGTH == 0))
    ends = (place == length - 1) | (short & (place % SHORT_LENGTH == SHORT_LENGTH - 1))
    earlier = jnp.where(starts, 0.0, pltpu.roll(x, 1, 0))
    later = jnp.where(ends, 0.0, pltpu.roll(x, length - 1, 0))
    return earlier, later


def both_tables(long, short, x, mask):
    whole = dot(long[...], x)
    parts = [
        dot(short[...], x[i * SHORT_LENGTH : (i + 1) * SHORT_LENGTH])
        for i in range(x.shape[0] // SHORT_LENGTH)
    ]
    return jnp.where(mask, jnp.concatenate(parts, axis=0), whole)


def fold_kernel(where, marks_own, marks_other, v0, r1, r2, r3, long, long_t, short, short_t, gain, taps, o0, o1, o2, o3, vals, spectrum, cond_spec, base, low_base, low_short, conv):
    z = where[0]
    length, half = vals.shape
    owned = length // 4
    part = half // 4
    block = (owned + SHORT_LENGTH // 4) // 4
    for k, piece in enumerate((v0, r1, r2, r3)):
        there = (z - k) & 3
        vals[rows_at(there, owned), :] = piece[pl.ds(0, owned), :]
        got = piece[pl.ds(owned, block), :].astype(F32)
        got = jnp.concatenate([got[:, g * part : (g + 1) * part] for g in range(4)], axis=0)
        low_base[rows_at(there, owned), :] = got[:owned]
        low_short[rows_at(there, SHORT_LENGTH // 4), :] = got[owned:]
    vals.flush()
    mask = short_lanes(marks_own, marks_other, (length, half))
    tall = jnp.concatenate([low_short[...]] * (length // SHORT_LENGTH), axis=0)
    base[...] = jnp.where(
        mask, jnp.concatenate([tall] * 4, axis=1), jnp.concatenate([low_base[...]] * 4, axis=1)
    ).astype(BF)
    base.flush()
    wide = vals[...].astype(F32)
    before, after = neighbours(wide, mask)
    cond = taps[0:1, :] * before + taps[1:2, :] * wide + taps[2:3, :] * after
    high = cond.astype(BF)
    low = (cond - high.astype(F32)).astype(BF)
    spec = both_tables(long, short, vals[...], mask)
    spectrum[...] = spec.astype(BF)
    spectrum.flush()
    cspec = both_tables(long, short, high, mask) + both_tables(long, short, low, mask)
    cond_spec[...] = cspec.astype(BF)
    cond_spec.flush()
    kern = base[...].astype(F32) + gain[...] * (jnp.sqrt(cspec * cspec + 1.0) - 1.0)
    filtered = (kern * spec).astype(BF)
    conv[...] = both_tables(long_t, short_t, filtered, mask).astype(BF)
    for k, out in enumerate((o0, o1, o2, o3)):
        out[...] = conv[rows_at((z + k) & 3, owned), :]


def out_rows_kernel(where, local, n1, n2, n3, c1, c2, c3, keep, send, whole):
    z, chip, core = where[0], where[1], where[2]
    rows, half = local.shape
    quarter = rows // 4
    wide = 3 * half
    whole[rows_at(z, rows), :] = local[...]
    for k, near in ((1, n1), (2, n2), (3, n3)):
        base = ((z - k) & 3) * 4
        whole[rows_at(base + chip, quarter), :] = near[:, wide:]
        for m, far in ((1, c1), (2, c2), (3, c3)):
            whole[rows_at(base + (chip ^ m), quarter), :] = far[k - 1, :, wide:]
    keep[...] = whole[rows_at(core, half), :]
    send[...] = whole[rows_at(1 - core, half), :]


def mix_kernel(where, outer, c0, r1, r2, r3, w_keep, w_came, own, other, conv, mixed, w_rows, packs):
    z, core = where[0], where[2]
    half = outer.shape[1]
    w_rows[:, :half] = jnp.where(core == 0, w_keep[...], w_came[...])
    w_rows[:, half:] = jnp.where(core == 0, w_came[...], w_keep[...])
    w_rows.flush()
    join_channels(z, (c0, r1, r2, r3), packs, conv)
    conv.flush()
    mixed[...] = (outer[...].astype(F32) * conv[...].astype(F32)).astype(BF)
    count = own.shape[0]
    other[...] = dot(mixed[pl.ds(count, count), :], w_rows[...]).astype(BF)
    own[...] = dot(mixed[pl.ds(0, count), :], w_rows[...])


def second_kernel(where, x, own, came, gain, normed, residual):
    owned = x.shape[0]
    for s in range(x.shape[1]):
        at = pl.ds(s * owned, owned)
        total = x[:, s, :] + own[at, :] + came[at, :].astype(F32)
        residual[at, :] = total
        hat, _ = norm_parts(total)
        normed[at, :] = (hat * gain[...]).astype(BF)


def feed_place_kernel(where, own, other, w_gu, w_dn):
    chip = where[1]
    rows = w_gu.shape[1] // 4
    chunk = own.shape[1] - rows
    for p, part in enumerate((own, other)):
        for i in range(4):
            w_gu[p, pl.ds(i * rows, rows), :] = part[i, pl.ds(0, rows), :]
        for i in range(3):
            at = i + (i >= chip).astype(jnp.int32)
            w_dn[p, pl.ds(i * chunk, chunk), :] = part[at, pl.ds(rows, chunk), :]


def feed_kernel(where, second, cot, w_gu, w_dn, out, layer, act, grads):
    half = w_dn.shape[1]
    width = second.shape[1]
    for p in range(2):
        gate_up = dot(second[...], w_gu[p])
        gate, upward = gate_up[:, :half], gate_up[:, half:]
        grad_act = dot_nt(cot[...], w_dn[p])
        square = gate * gate
        tanh = jnp.tanh(GELU_A * gate * (1.0 + GELU_B * square))
        cdf = 0.5 * (1.0 + tanh)
        unit = gate * cdf
        slope = cdf + 0.5 * gate * (1.0 - tanh * tanh) * (GELU_A * (1.0 + 3.0 * GELU_B * square))
        act[:, p * half : (p + 1) * half] = (unit * upward).astype(BF)
        grads[:, p * width : p * width + half] = (grad_act * upward * slope).astype(BF)
        grads[:, p * width + half : (p + 1) * width] = (grad_act * unit).astype(BF)
    total = dot_nt(grads[:, :width], w_gu[0]) + dot_nt(grads[:, width:], w_gu[1])
    out[...] = total.astype(out.dtype)
    total = dot(act[:, :half], w_dn[0]) + dot(act[:, half:], w_dn[1])
    layer[...] = total.astype(layer.dtype)


def feed_weight_kernel(where, a0, a1, a2, a3, g0, g1, g2, g3, s0, s1, s2, s3, c0, c1, c2, c3, send, keep):
    chip = where[1]
    width = s0.shape[1]
    half = width // 2
    nz, piece, _ = keep.shape
    chunk = half // 3
    rows = piece - chunk
    for p, out in ((1, send), (0, keep)):
        total = None
        for s, g in ((s0, g0), (s1, g1), (s2, g2), (s3, g3)):
            part = dot_tn(s[...], g[:, p * width : (p + 1) * width])
            total = part if total is None else total + part
        for i in range(nz):
            out[i, pl.ds(0, rows), :] = total[i * rows : (i + 1) * rows].astype(BF)
        down = None
        for a, c in ((a0, c0), (a1, c1), (a2, c2), (a3, c3)):
            part = dot_tn(a[:, p * half : (p + 1) * half], c[...])
            down = part if down is None else down + part
        out[chip, pl.ds(rows, chunk), :] = jnp.zeros((chunk, width), BF)
        for i in range(3):
            to = i + (i >= chip).astype(jnp.int32)
            out[to, pl.ds(rows, chunk), :] = down[i * chunk : (i + 1) * chunk].astype(BF)


def add_kernel(where, a, b, out):
    out[...] = (a[...].astype(F32) + b[...].astype(F32)).astype(BF)


def layer_out_kernel(where, residual, own, r1, r2, r3, out):
    owned = out.shape[0]
    for s in range(out.shape[1]):
        at = pl.ds(s * owned, owned)
        out[:, s, :] = residual[at, :] + added([x.at[at] for x in (own, r1, r2, r3)])


def second_back_kernel(where, residual, gain, cot, own, r1, r2, r3, low, grad_gain, grad_residual):
    owned = cot.shape[0]
    grad = own[...] + r1[...].astype(F32) + r2[...].astype(F32) + r3[...].astype(F32)
    hat, inv = norm_parts(residual[...])
    pulled, grad_gain[...] = norm_pull(hat, inv, gain[...], grad)
    for s in range(cot.shape[1]):
        at = pl.ds(s * owned, owned)
        total = cot[:, s, :] + pulled[s * owned : (s + 1) * owned]
        grad_residual[at, :] = total
        low[at, :] = total.astype(BF)


def write_pieces(whole, outs, chip):
    rows = whole.shape[0] // 4
    quarter = rows // 4
    for m, out in enumerate(outs):
        for i in range(4):
            out[pl.ds(i * quarter, quarter), :] = whole[rows_at(i * 4 + (chip ^ m), quarter), :]


def mix_back_kernel(where, ga, gb, w_rows, outer, conv, o0, o1, o2, o3, grad_outer, grad_conv, packs):
    z = where[0]
    count = ga.shape[0]
    half = outer.shape[1]
    for i, grad in enumerate((ga, gb)):
        at = pl.ds(i * count, count)
        grad_mixed = dot_nt(grad[...], w_rows[...])
        grad_outer[at, :] = (grad_mixed * conv[at, :].astype(F32)).astype(BF)
        grad_conv[at, :] = (grad_mixed * outer[at, :].astype(F32)).astype(BF)
    grad_outer.flush()
    split_channels(grad_conv, packs)
    for k, out in enumerate((o0, o1, o2, o3)):
        out[...] = packs[(z + k) & 3]


def early_kernel(where, na, nb, grad_outer, mixed, other_mixed, ga, gb, p0, p1, p2, p3, whole):
    chip, core = where[1], where[2]
    count, half = na.shape[0], mixed.shape[1]
    first = jnp.where(core == 0, ga[:, :half], ga[:, half:])
    second = jnp.where(core == 0, gb[:, :half], gb[:, half:])
    mine = dot_tn(mixed[pl.ds(0, count), :], first) + dot_tn(mixed[pl.ds(count, count), :], second)
    theirs = dot_tn(other_mixed[pl.ds(count, count), :], first)
    theirs = theirs + dot_tn(other_mixed[pl.ds(0, count), :], second)
    whole[rows_at(core, half), half:] = mine.astype(BF)
    whole[rows_at(1 - core, half), half:] = theirs.astype(BF)
    total = dot_tn(na[...], grad_outer[pl.ds(0, count), :])
    total = total + dot_tn(nb[...], grad_outer[pl.ds(count, count), :])
    whole[:, :half] = total.astype(BF)
    write_pieces(whole, (p0, p1, p2, p3), chip)


def fold_back_kernel(where, marks_own, marks_other, g0, r1, r2, r3, long, short, spectrum, cond_spec, base, gain, taps, vals, long_t, short_t, o0, o1, o2, o3, filt, grads):
    z = where[0]
    length, half = grads.shape
    owned = length // 4
    part = half // 4
    for k, piece in enumerate((g0, r1, r2, r3)):
        grads[rows_at((z - k) & 3, owned), :] = piece[...]
    mask = short_lanes(marks_own, marks_other, (length, half))
    gf = both_tables(long, short, grads[...], mask)
    cspec = cond_spec[...].astype(F32)
    root = jnp.sqrt(cspec * cspec + 1.0)
    above = root - 1.0
    grad_base = gf * spectrum[...].astype(F32)
    grad_spec = (gf * (base[...].astype(F32) + gain[...] * above)).astype(BF)
    grad_cspec = (grad_base * gain[...] * (cspec / root)).astype(BF)
    grad_cond = both_tables(long_t, short_t, grad_cspec, mask)
    direct = both_tables(long_t, short_t, grad_spec, mask)
    wide = vals[...].astype(F32)
    before, after = neighbours(wide, mask)
    grad_before, grad_after = neighbours(grad_cond, mask)
    grads[...] = (
        direct + taps[0:1, :] * grad_after + taps[1:2, :] * grad_cond + taps[2:3, :] * grad_before
    ).astype(BF)
    for k, out in enumerate((o0, o1, o2, o3)):
        out[...] = grads[rows_at((z + k) & 3, owned), :]

    def over_slots(x):
        return sum(x[:, s * part : (s + 1) * part] for s in range(4))

    shorts = jnp.where(mask, grad_base, 0.0)
    small = [
        jnp.sum(x, axis=0, keepdims=True)
        for x in (grad_base * above, grad_cond * before, grad_cond * wide, grad_cond * after)
    ]
    folded = sum(
        shorts[i * SHORT_LENGTH : (i + 1) * SHORT_LENGTH] for i in range(length // SHORT_LENGTH)
    )
    fill = filt.shape[0] * (filt.shape[1] // part) - length - SHORT_LENGTH - 4
    found = jnp.concatenate(
        [
            over_slots(grad_base - shorts),
            over_slots(folded),
            over_slots(jnp.concatenate(small, axis=0)),
            jnp.zeros((fill, part), F32),
        ],
        axis=0,
    )
    size = filt.shape[0]
    blocks = [found[g * size : (g + 1) * size] for g in range(filt.shape[1] // part)]
    filt[...] = jnp.concatenate(blocks, axis=1).astype(BF)


def late_kernel(where, marks_own, marks_other, g0, r1, r2, r3, left, right, na, nb, p0, p1, p2, p3, late, grads, packs, whole):
    z, chip = where[0], where[1]
    half = left.shape[1]
    owned = packs.shape[1]
    join_channels(z, (g0, r1, r2, r3), packs, grads)
    count = na.shape[0]
    place = lax.broadcasted_iota(jnp.int32, (owned, half), 0)
    for i, marks in enumerate((marks_own, marks_other)):
        for s in range(count // owned):
            at = pl.ds(i * count + s * owned, owned)
            valid = valid_rows(marks, s, z, owned)
            grad = jnp.where(place < valid, grads[at, :].astype(F32), 0.0)
            late[at, :half] = (grad * right[at, :].astype(F32)).astype(BF)
            late[at, half:] = (grad * left[at, :].astype(F32)).astype(BF)
    total = dot_tn(na[...], late[pl.ds(0, count), :]) + dot_tn(nb[...], late[pl.ds(count, count), :])
    whole[...] = total.astype(BF)
    write_pieces(whole, (p0, p1, p2, p3), chip)


def first_grad_kernel(where, grad_outer, late, w, own, other):
    half = grad_outer.shape[1]
    count = own.shape[0]
    for i, out in ((1, other), (0, own)):
        at = pl.ds(i * count, count)
        total = dot_nt(grad_outer[at, :], w[:, :half]) + dot_nt(late[at, :], w[:, half:])
        out[...] = total.astype(out.dtype)


def first_back_kernel(where, x, gain, grad_residual, own, came, grad_gain, grad_inputs):
    owned = x.shape[0]
    riding = None
    for s in range(x.shape[1]):
        at = pl.ds(s * owned, owned)
        hat, inv = norm_parts(x[:, s, :])
        pulled, part = norm_pull(hat, inv, gain[...], own[at, :] + came[at, :].astype(F32))
        grad_inputs[:, s, :] = grad_residual[at, :] + pulled
        riding = part if riding is None else riding + part
    grad_gain[...] = riding


def added(pieces):
    total = pieces[0][...].astype(F32)
    for piece in pieces[1:]:
        total = total + piece[...].astype(F32)
    return total


def late_share_kernel(where, p0, r1, r2, r3, e0, e1, e2, e3, one, two, o0, o1, o2, o3, late, early):
    z = where[0]
    late[...] = added((p0, r1, r2, r3)).astype(BF)
    early[...] = added((e0, e1, e2, e3)).astype(BF)
    quarter = p0.shape[0] // 4
    width = p0.shape[1]
    place = lax.broadcasted_iota(jnp.int32, (RIDE, width), 0)
    extra = jnp.where(place == 0, jnp.broadcast_to(one[...], (RIDE, width)), 0.0)
    extra = jnp.where(place == 1, jnp.broadcast_to(two[...], (RIDE, width)), extra).astype(BF)
    for k, out in enumerate((o0, o1, o2, o3)):
        at = rows_at((z + k) & 3, quarter)
        out[pl.ds(0, quarter), :] = late[at, :]
        out[pl.ds(quarter, quarter), :] = early[at, :]
        out[pl.ds(2 * quarter, RIDE), :] = extra


def late_sum_kernel(where, s0, r1, r2, r3, f0, f1, f2, f3, piece, filt):
    piece[...] = added((s0, r1, r2, r3)).astype(BF)
    filt[...] = added((f0, f1, f2, f3)).astype(BF)


def gather_kernel(where, s0, r1, r2, r3, f0, f1, f2, f3, out):
    z, chip = where[0], where[1]
    quarter = (s0.shape[0] - RIDE) // 2
    parts = (s0, r1, r2, r3)
    for m, piece in enumerate(parts):
        for i in range(2):
            out[rows_at(i * 4 + (chip ^ m), quarter), :] = piece[pl.ds(i * quarter, quarter), :]
    riding = added([piece[pl.ds(2 * quarter, RIDE), :] for piece in parts])
    top = 8 * quarter
    out[pl.ds(top, RIDE), :] = riding.astype(BF)
    step = f0.shape[0]
    for k, piece in enumerate((f0, f1, f2, f3)):
        at = top + RIDE + ((z - k) & 3) * step
        out[pl.ds(pl.multiple_of(at, 16), step), :] = piece[...]


def feed_order_kernel(where, shares, gate_up, down):
    z = where[0]
    rows = gate_up.shape[0]
    chunk = shares.shape[1] - rows
    per_z = 6 * chunk
    for side in range(2):
        for zz in range(4):
            for c in range(6):
                mm = c if c < 2 * zz else c + 2
                at = (side * 3 + zz - (zz > mm // 2)) * chunk
                to = side * 4 * per_z + zz * per_z + c * chunk
                gate_up[:, to : to + chunk] = shares[mm, :rows, at : at + chunk].astype(F32)
    for c in range(6):
        mm = c + 2 * (c >= 2 * z).astype(jnp.int32)
        down[pl.ds(c * chunk, chunk), :] = shares[mm, pl.ds(rows, chunk), :].astype(F32)


def last_kernel(where, own, other, w_in, w_out, long, short, gain, taps, norm_one, norm_two):
    core = where[2]
    rows = w_in.shape[0]
    width = w_out.shape[1]
    half = width // 2
    part = half // 4
    top = 2 * rows

    def write(out, to, a, b):
        a, b = a.astype(F32), b.astype(F32)
        out[:, to : to + half] = jnp.where(core == 0, a, b)
        out[:, to + half : to + width] = jnp.where(core == 0, b, a)

    for start, at, to, out in (
        (rows, 0, 0, w_in),
        (0, 0, width, w_in),
        (0, half, 2 * width, w_in),
        (rows, half, 0, w_out),
    ):
        place = (pl.ds(start, rows), slice(at, at + half))
        write(out, to, own[place], other[place])
    place = pl.ds(top, RIDE)
    riding = own[place, :].astype(F32) + other[place, :].astype(F32)
    norm_one[...] = riding[0]
    norm_two[...] = riding[1]
    step = (own.shape[0] - top - RIDE) // 4
    length, count = long.shape[0], short.shape[0]

    def filter_rows(ref):
        got = []
        for there in range(4):
            at = pl.ds(top + RIDE + there * step, step)
            blocks = [ref[at, g * part : (g + 1) * part].astype(F32) for g in range(width // part)]
            got.append(jnp.concatenate(blocks, axis=0))
        return jnp.concatenate(got, axis=1)

    a, b = filter_rows(own), filter_rows(other)
    write(long, 0, a[:length], b[:length])
    write(short, 0, a[length : length + count], b[length : length + count])
    rest = length + count
    a_row, b_row = a[rest], b[rest]
    gain[pl.ds(0, half)] = jnp.where(core == 0, a_row, b_row)
    gain[pl.ds(half, half)] = jnp.where(core == 0, b_row, a_row)
    write(taps, 0, a[rest + 1 : rest + 4], b[rest + 1 : rest + 4])


def body(
    inputs,
    cotangent,
    group,
    lens,
    norm1_gain,
    w_in,
    kernel_long,
    kernel_short,
    conv_weight,
    cond_gain,
    w_out,
    norm2_gain,
    w_gate_up,
    w_down,
):
    nz = lax.axis_size("freq")
    ndp = lax.axis_size("dp")
    z = lax.axis_index("freq")
    d = lax.axis_index("dp")
    core = d % 2
    chip = (d // 2) % 4
    owned, slots, width = inputs.shape
    half = width // 2
    length = owned * nz
    tokens = owned * slots
    rows = w_in.shape[0]
    quarter = rows // 4
    others = ndp // GROUP
    blocks = [[g * GROUP + i for i in range(GROUP)] for g in range(others)]
    same_core = [[g * GROUP + 2 * i + c for i in range(4)] for g in range(others) for c in range(2)]
    across = [[i + GROUP * g for g in range(others)] for i in range(GROUP)]

    def core_swap(x):
        return lax.ppermute(x, "dp", [(i, i ^ 1) for i in range(ndp)])

    def chip_swap(x, m):
        return lax.ppermute(x, "dp", [(i, i ^ (2 * m)) for i in range(ndp)])

    def z_rot(x, k):
        return lax.ppermute(x, "freq", [(i, (i + k) % nz) for i in range(nz)])

    def z_swap(pieces):
        return [pieces[0]] + [z_rot(pieces[k], k) for k in range(1, nz)]

    def own_far(pieces):
        got = z_swap(pieces)
        return [Far(got[0])] + got[1:]

    def near_by(piece):
        return [piece] + [chip_swap(piece, m) for m in (1, 2, 3)]

    def exchanged(parts):
        return [parts[0]] + [chip_swap(parts[m], m) for m in (1, 2, 3)]

    def over_groups(x):
        if others > 1:
            return lax.psum(x, "dp", axis_index_groups=across)
        return x

    where = jnp.stack([z, chip, core, z]).astype(jnp.int32)
    part = kernel_short.shape[0]
    hidden = w_down.shape[0] * nz
    per_z = w_down.shape[0]
    chunk = per_z // 6
    taken = rows + chunk
    quarter_of = lambda place: place[1]
    near = run(
        near_kernel,
        "near",
        [((quarter, 4 * half), BF)],
        where,
        [Far(w_in, quarter_of, quarter), Far(w_out, quarter_of, quarter)],
    )[0]
    in_local, out_local, long_half, short_half = run(
        local_kernel,
        "local",
        [((rows, 3 * half), BF), ((rows, half), BF), ((owned, half), BF), ((part, half), BF)],
        where,
        [w_in, w_out, kernel_long, kernel_short],
        after=(near,),
    )
    all_near = [z_rot(near, k) for k in range(1, nz)]

    gain_one = norm1_gain[None]
    gain_two = norm2_gain[None]
    cot_low = run(low_kernel, "cot_low", [((tokens, width), BF)], where, [Far(cotangent)], after=(near,))[0]
    cots = [cot_low] + [chip_swap(cot_low, m) for m in (1, 2, 3)]
    normed = run(
        first_norm_kernel,
        "first_norm",
        [((tokens, width), BF)],
        where,
        [Far(inputs), gain_one],
        after=(cot_low,),
    )[0]
    normed_other = core_swap(normed)
    in_stack = run(
        hand_on_kernel,
        "hand_on",
        [((3, quarter, 4 * half), BF)],
        where,
        all_near,
    )[0]
    mlp_piece = run(
        feed_pick_kernel,
        "feed_pick",
        [((taken, width), BF)],
        where,
        [w_gate_up, w_down],
        after=(near,),
    )[0]
    in_far = [chip_swap(in_stack, m) for m in (1, 2, 3)]
    mlp_got = lax.all_gather(mlp_piece, "freq", axis=0)

    marks = jnp.concatenate([group[:, None], lens], axis=1).astype(jnp.int32)
    marks_other = core_swap(marks)
    lane = half // nz

    def channels(x):
        own = jnp.where(core == 0, x[:, :half], x[:, half:])
        picked = sum(
            jnp.where(z == i, own[:, i * lane : (i + 1) * lane], 0.0) for i in range(nz)
        )
        return jnp.concatenate([picked] * 4, axis=1)

    gain_lanes = channels(cond_gain[None])
    taps = channels(conv_weight)
    long = jnp.asarray(cosine_table(length), BF)
    long_t = jnp.asarray(cosine_table(length).T, BF)
    short = jnp.asarray(cosine_table(SHORT_LENGTH), BF)
    short_t = jnp.asarray(cosine_table(SHORT_LENGTH).T, BF)

    many = 2 * tokens
    block = (owned + part) // 4
    filler = -block % 16 + block
    piece = ((owned, half), BF)
    *sends, w_in_half, outer, left, right = run(
        project_kernel,
        "project",
        [((owned + filler, half), BF, HBM)]
        + [((owned + filler, half), BF)] * 3
        + [((width, 3 * half), BF, HBM), ((many, half), BF, HBM)]
        + [((many, half), BF, HBM)] * 2,
        where,
        [marks, marks_other, normed, normed_other, in_local, *all_near, *in_far, long_half, short_half],
        [
            pltpu.VMEM((many, half), BF),
            pltpu.VMEM((nz, owned, half), BF),
            pltpu.VMEM((nz, filler, half), F32),
        ],
    )
    came = own_far(sends)
    full = (length, half)
    *sends, vals, spectrum, cond_spec, base = run(
        fold_kernel,
        "fold",
        [(*piece, HBM)] + [piece] * 3 + [(full, BF, HBM)] * 4,
        where,
        [marks, marks_other, *came, long, long_t, short, short_t, gain_lanes, taps],
        [
            pltpu.VMEM((length, lane), F32),
            pltpu.VMEM((part * nz, lane), F32),
            pltpu.VMEM(full, BF),
        ],
        after=cots[1:3],
    )
    came = own_far(sends)
    w_keep, w_send = run(
        out_rows_kernel,
        "out_rows",
        [((half, half), BF, HBM), ((half, half), BF)],
        where,
        [out_local, *all_near, *in_far],
        [pltpu.VMEM((width, half), BF)],
        after=(sends[0],),
    )
    w_gu, w_dn = run(
        feed_place_kernel,
        "feed_place",
        [((2, width, width), BF, VMEM), ((2, half, width), BF, VMEM)],
        where,
        [mlp_got, core_swap(mlp_got)],
    )
    part_own, part_other, conv, mixed, w_out_rows = run(
        mix_kernel,
        "mix",
        [((tokens, width), F32), ((tokens, width), BF), ((many, half), BF, HBM)]
        + [((many, half), BF), ((half, width), BF, HBM)],
        where,
        [Far(outer), *came, Far(w_keep), core_swap(w_send)],
        [pltpu.VMEM((nz, owned, half), BF)],
        after=(cots[3],),
    )
    normed_two, residual = run(
        second_kernel,
        "second_norm",
        [((tokens, width), BF), ((tokens, width), F32, HBM)],
        where,
        [Far(inputs), part_own, core_swap(part_other), gain_two],
    )

    arrived = near_by(normed_two)
    acts, grads_gu, sums, layers = [None] * 4, [None] * 4, [None] * 4, [None] * 4
    order = ()
    for m in range(4):
        grad, layer, act, grad_gu = run(
            feed_kernel,
            "feed",
            [
                ((tokens, width), BF if m else F32),
                ((tokens, width), BF if m else F32),
                ((tokens, width), BF, VMEM),
                ((tokens, 2 * width), BF, VMEM),
            ],
            where,
            [arrived[m], cots[m], Held(w_gu), Held(w_dn)],
            after=order,
        )
        order = (grad,)
        acts[m], grads_gu[m], sums[m], layers[m] = Held(act), Held(grad_gu), grad, layer
    backs = [chip_swap(sums[m], m) for m in (1, 2, 3)]

    mlp_send, mlp_keep = run(
        feed_weight_kernel,
        "feed_weights",
        [((nz, taken, width), BF), ((nz, taken, width), BF, VMEM)],
        where,
        [*acts, *grads_gu, *arrived, *cots],
    )
    mlp_grads = run(
        add_kernel,
        "add",
        [((nz, taken, width), BF)],
        where,
        [Held(mlp_keep), core_swap(mlp_send)],
    )[0]
    mlp_share = lax.psum_scatter(mlp_grads, "freq", scatter_dimension=0, tiled=False)
    grad_mix, grad_gain_two, grad_residual = run(
        second_back_kernel,
        "second_norm_back",
        [((tokens, width), BF), ((1, width), F32), ((tokens, width), F32, HBM)],
        where,
        [Far(residual), gain_two, Far(cotangent), sums[0], *backs],
        after=(mlp_grads,),
    )
    grad_mix_other = core_swap(grad_mix)
    *got, grad_outer = run(
        mix_back_kernel,
        "mix_back",
        [(*piece, HBM)] + [piece] * 3 + [((many, half), BF, HBM)],
        where,
        [grad_mix, grad_mix_other, Far(w_out_rows), Far(outer), Far(conv)],
        [pltpu.VMEM((many, half), BF), pltpu.VMEM((nz, owned, half), BF)],
    )
    came = own_far(got)
    early_all = exchanged(
        run(
            early_kernel,
            "early_weights",
            [((rows, width), BF)] * 4,
            where,
            [
                normed,
                normed_other,
                Far(grad_outer),
                mixed,
                core_swap(mixed),
                grad_mix,
                grad_mix_other,
            ],
            [pltpu.VMEM((width, width), BF)],
        )
    )

    layer_far = [chip_swap(layers[m], m) for m in (1, 2, 3)]

    size = -(-(length + SHORT_LENGTH + 4) // (16 * width // lane)) * 16
    *sends, filt = run(
        fold_back_kernel,
        "fold_back",
        [(*piece, HBM)] + [piece] * 3 + [((size, width), BF)],
        where,
        [
            marks,
            marks_other,
            *came,
            long,
            short,
            Far(spectrum),
            Far(cond_spec),
            Far(base),
            gain_lanes,
            taps,
            Far(vals),
            long_t,
            short_t,
        ],
        [pltpu.VMEM(full, BF)],
        after=[Far(x) for x in layer_far],
    )
    came = own_far(sends)
    *parts, late = run(
        late_kernel,
        "late_weights",
        [((rows, width), BF)] * 4 + [((many, width), BF)],
        where,
        [
            marks,
            marks_other,
            *came,
            Far(left),
            Far(right),
            normed,
            normed_other,
        ],
        [
            pltpu.VMEM((many, half), BF),
            pltpu.VMEM((nz, owned, half), BF),
            pltpu.VMEM((width, width), BF),
        ],
        after=[Far(x) for x in (*early_all[1:], mlp_share)],
    )
    own, other = run(
        first_grad_kernel,
        "first_grad",
        [((tokens, width), F32), ((tokens, width), BF)],
        where,
        [Far(grad_outer), late, Far(w_in_half)],
    )
    grad_gain_one, grad_inputs = run(
        first_back_kernel,
        "first_norm_back",
        [((1, width), F32), ((owned, slots, width), F32, HBM)],
        where,
        [Far(inputs), gain_one, Far(grad_residual), own, core_swap(other)],
    )
    mlp_sum = lax.all_gather(over_groups(mlp_share), "dp", axis=0, axis_index_groups=blocks)
    layer_out = run(
        layer_out_kernel,
        "layer_out",
        [((owned, slots, width), F32, HBM)],
        where,
        [Far(residual), Far(layers[0]), *[Far(x) for x in layer_far]],
    )[0]
    late_sends = run(
        late_share_kernel,
        "late_share",
        [((2 * quarter + RIDE, width), BF)] * 4,
        where,
        [
            *exchanged(parts),
            early_all[0],
            *[Far(x) for x in early_all[1:]],
            grad_gain_one,
            grad_gain_two,
        ],
        [pltpu.VMEM((rows, width), BF)] * 2,
        after=(Far(layer_out),),
    )
    late_piece, filt = run(
        late_sum_kernel,
        "late_sum",
        [((2 * quarter + RIDE, width), BF), ((size, width), BF)],
        where,
        [*z_swap(late_sends), *near_by(over_groups(filt))],
    )
    grad_w_gate_up, grad_w_down = run(
        feed_order_kernel,
        "feed_order",
        [((rows, 2 * hidden), F32, HBM), ((per_z, width), F32, HBM)],
        where,
        [Far(mlp_sum)],
        after=(late_piece,),
    )
    gathered = run(
        gather_kernel,
        "gather",
        [((2 * rows + RIDE + nz * size, width), BF)],
        where,
        [*near_by(over_groups(late_piece)), *z_swap([filt] * nz)],
        after=[Far(grad_w_down)],
    )[0]
    grad_w_in, grad_w_out, grad_long, grad_short, grad_cond, grad_taps, grad_one, grad_two = run(
        last_kernel,
        "last",
        [
            ((rows, 3 * width), F32),
            ((rows, width), F32),
            ((length, width), F32),
            ((SHORT_LENGTH, width), F32),
            ((width,), F32),
            ((3, width), F32),
            ((width,), F32),
            ((width,), F32),
        ],
        where,
        [gathered, core_swap(gathered)],
    )

    return (
        layer_out,
        grad_inputs,
        grad_one,
        grad_w_in,
        grad_long,
        grad_short,
        grad_taps,
        grad_cond,
        grad_w_out,
        grad_two,
        grad_w_gate_up,
        grad_w_down,
    )


def solution(mesh):
    return jax.shard_map(
        body,
        mesh=mesh,
        in_specs=(
            P("freq", "dp", None),
            P("freq", "dp", None),
            P("dp"),
            P("dp", None),
            P(),
            P("freq", None),
            P("freq", None),
            P("freq", None),
            P(),
            P(),
            P("freq", None),
            P(),
            P("freq", None),
            P("freq", None),
        ),
        out_specs=(
            P("freq", "dp", None),
            P("freq", "dp", None),
            P(),
            P("freq", None),
            P(),
            P(),
            P(),
            P(),
            P("freq", None),
            P(),
            P("freq", None),
            P("freq", None),
        ),
        check_vma=False,
    )
```
